256 devices in a mesh: frame: 32 (over y_lo, z, core), head: 8 (over x, y_hi).
Axes of the slice: x: 4, y: 4 (y_hi: 2, y_lo: 2; y = y_hi * 2 + y_lo), z: 8, core: 2. Of those that a mesh axis runs over, the one named last changes fastest.
Arguments:
- video: bfloat16 [3, 4096, 3072], P(None, 'frame', 'head'), may hold values from -6 to 6
- w_qkv: bfloat16 [3072, 3, 3072], P(None, None, 'head'), may hold values from -0.5 to 0.5
- w_out: bfloat16 [3072, 3072], P('head'), may hold values from -0.15625 to 0.15625
- text_kv: bfloat16 [2, 3, 256, 3072], P(None, None, None, 'head'), may hold values from -16 to 16
- text_lengths: int32 [3], replicated, may hold values from 1 to 256
- norm_gains: float32 [2, 128], replicated, may hold values from 1.3 to 5
- mod_table: float32 [32, 3, 3072], P(None, None, 'head'), may hold values from -4 to 4
- timestep_ids: int32 [32], replicated, may hold values from 0 to 31
- queue_shift: int32 [1], replicated, may hold values from 0 to 31
Outputs:
- video_out: bfloat16 [3, 4096, 3072], P(None, 'frame', 'head')
The draws below stay inside these ranges and needn't reach their ends.
All inputs are finite; a program needn't handle non-finite values.
Results may differ from the reference program's by a relative error of at most 0.015.
Values may be sent and summed in bfloat16 or wider, within the bound.
No kernel may reach another device: no remote copies, remote signals or barrier semaphores. Data moves between devices by JAX's collectives and lax.ppermute only.
A program may use at most 128 MiB of HBM per device.

```python
import jax
import jax.numpy as jnp
from jax import lax

D = 3072
HEADS = 24
HD = 128
TXT = 256
BRANCH = 3
FRAME_TOK = 128
LAT_W = 16
LEVELS = 32
FRAMES = 32
TOKENS = 4096


def draw_video(key, part):
    key = jax.random.fold_in(key, 11)
    key_one = jax.random.fold_in(key, 0)
    field = jax.random.normal(key_one, (BRANCH, TOKENS, D), jnp.float32)
    return jnp.clip(field, -6.0, 6.0).astype(jnp.bfloat16)


def draw_w_qkv(key, part):
    key = jax.random.fold_in(key, 12)
    key_one = jax.random.fold_in(key, 0)
    base = jax.random.normal(key_one, (D, 3, HEADS, HD), jnp.float32) * D ** (-0.5)
    return jnp.clip(base.reshape(D, 3, HEADS * HD), -0.5, 0.5).astype(jnp.bfloat16)


def draw_norm_gains(key, part):
    key = jax.random.fold_in(key, 13)
    bounds = (1.3, 1.9)
    return jax.random.uniform(key, (2, HD), jnp.float32, bounds[0], bounds[1])


def draw_text_kv(key, part):
    key = jax.random.fold_in(key, 14)
    base = jax.random.normal(key, (2, BRANCH, TXT, HEADS * HD), jnp.float32)
    factor = jnp.array([1.3, 4.0], jnp.float32)[:, None, None, None]
    return jnp.clip(base * factor, -16.0, 16.0).astype(jnp.bfloat16)


def plant(values, stream_key, least, largest):
    longest = values.shape.index(max(values.shape))
    spots = []
    for shift in (0, 1):
        where = [jax.random.randint(jax.random.fold_in(stream_key, axis), (), 0, length) for axis, length in enumerate(values.shape)]
        where[longest] = (where[longest] + shift) % values.shape[longest]
        spots.append(tuple(where))
    return values.at[spots[0]].set(least).at[spots[1]].set(largest)


def raised(result, rng, source, target, parts, factor):
    def block_of(axis_at):
        return (jnp.arange(result.shape[axis_at]) // (result.shape[axis_at] // parts)).reshape((-1,) + (1,) * (result.ndim - 1 - axis_at))

    near = jax.random.permutation(rng, parts)[block_of(target)]
    second = (block_of(target) + parts // 2) % parts
    return jnp.where((block_of(source) == near) | (block_of(source) == second), factor * result, result)


def block_levels(stream_key, dims, pieces, least, largest):
    def one(axis_at, parts):
        heights = jax.random.uniform(jax.random.fold_in(jax.random.fold_in(stream_key, 6), axis_at), (parts,), jnp.float32, least / len(pieces), largest / len(pieces))
        return jnp.repeat(jnp.exp(heights), dims[axis_at] // parts).reshape((-1,) + (1,) * (len(dims) - axis_at - 1))

    gain = one(*pieces[0])
    for cut in pieces[1:]:
        gain = gain * one(*cut)
    return gain


def normal_values(own_key, extent, scale, reach, shards=(), kind=jnp.bfloat16):
    values = jax.random.normal(own_key, extent, jnp.float32) * scale
    if len(shards) > 0:
        values = block_levels(own_key, extent, shards, -0.22, 0.18) * values
    return jnp.clip(values, min=-reach, max=reach).astype(kind)


def bell_draw_with(rng, extent, spread, limit, cuts, heavy, kind=jnp.bfloat16):
    values = spread * jax.random.normal(rng, extent, jnp.float32)
    if cuts:
        values = values * block_levels(rng, extent, cuts, -0.22, 0.18)
    return jnp.clip(raised(values, jax.random.fold_in(rng, 3), *heavy), -limit, limit).astype(kind)


def setup_inputs(seed: int = 0) -> dict:
    arg_keys = jax.random.split(jax.random.key(seed), 10)
    return {
        "video": draw_video(jax.random.fold_in(arg_keys[9], 71), 0),
        "w_qkv": draw_w_qkv(jax.random.fold_in(arg_keys[9], 71), 0),
        "w_out": bell_draw_with(arg_keys[2], (HEADS * HD, D), (HEADS * HD) ** -0.5, 0.15625, ((0, 8),), (0, 1, 8, 2.0)),
        "text_kv": draw_text_kv(jax.random.fold_in(arg_keys[9], 71), 0),
        "text_lengths": jax.random.randint(arg_keys[4], (BRANCH,), 1, TXT + 1).astype(jnp.int32),
        "norm_gains": draw_norm_gains(jax.random.fold_in(arg_keys[9], 71), 0),
        "mod_table": normal_values(arg_keys[6], (LEVELS, 3, D), 0.7, 4.0, ((2, 8),), jnp.float32),
        "timestep_ids": plant(jax.random.randint(arg_keys[7], (FRAMES,), 0, LEVELS), jax.random.fold_in(arg_keys[7], 1), 0, LEVELS - 1).astype(jnp.int32),
        "queue_shift": jax.random.randint(arg_keys[8], (1,), 0, FRAMES).astype(jnp.int32),
    }


rope_base = 256.0
norm_eps = 1e-06

def rope_angles(token_index):
    time_dims = HD // 8
    space_dims = (HD - time_dims) // 2
    in_frame = token_index % FRAME_TOK
    sections = [(token_index // FRAME_TOK, time_dims), (in_frame // LAT_W, space_dims), (in_frame % LAT_W, space_dims)]
    angle_parts = []
    for position, sec_width in sections:
        frequency = rope_base ** (-jnp.arange(0, sec_width, 2).astype(jnp.float32) / sec_width)
        angle_parts.append(position.astype(jnp.float32)[:, None] * frequency[None, :])
    angles = jnp.concatenate(angle_parts, axis=1)
    return (jnp.cos(angles), jnp.sin(angles))

def rotate(inputs, cosine, sine_table):
    paired = inputs.reshape(inputs.shape[:-1] + (inputs.shape[-1] // 2, 2))
    even_part = paired[..., 0]
    odd_part = paired[..., 1]
    cosine = cosine[:, None, :]
    sine_table = sine_table[:, None, :]
    rotated = jnp.stack([even_part * cosine - odd_part * sine_table, even_part * sine_table + odd_part * cosine], axis=-1)
    return rotated.reshape(inputs.shape)

def rms_norm(inputs, gain_row):
    return inputs * lax.rsqrt(lax.optimization_barrier(jnp.mean(inputs * inputs, axis=-1, keepdims=True)) + norm_eps) * gain_row

def reference(video, w_qkv, w_out, text_kv, text_lengths, norm_gains, mod_table, timestep_ids, queue_shift):
    frames = timestep_ids.shape[0]
    queue_slot = ((jnp.arange(frames) + queue_shift[0]) % frames).astype(jnp.int32)
    noise_level = timestep_ids[queue_slot].astype(jnp.int32)
    looked = mod_table[noise_level]
    per_token = jnp.repeat(looked, FRAME_TOK, axis=0)
    widened = video.astype(jnp.float32)
    row_mean = lax.optimization_barrier(jnp.mean(widened, axis=-1, keepdims=True))
    row_var = lax.optimization_barrier(jnp.mean(widened * widened, axis=-1, keepdims=True)) - row_mean * row_mean
    normed = (widened - row_mean) * lax.rsqrt(row_var + norm_eps)
    modded = (normed * (1.0 + per_token[:, 1]) + per_token[:, 0]).astype(jnp.bfloat16)
    branches, tokens, model_dim = video.shape
    projected = jnp.dot(modded.reshape(branches * tokens, model_dim), w_qkv.reshape(model_dim, -1), preferred_element_type=jnp.float32)
    projected = projected.reshape(branches, tokens, 3, HEADS, HD)
    cosine, sine_table = rope_angles(jnp.arange(tokens))
    query = rotate(rms_norm(projected[:, :, 0], norm_gains[0]), cosine, sine_table).astype(jnp.bfloat16)
    key_rot = rotate(rms_norm(projected[:, :, 1], norm_gains[1]), cosine, sine_table).astype(jnp.bfloat16)
    value = projected[:, :, 2].astype(jnp.bfloat16)
    text_keys = text_kv[0].reshape(branches, TXT, HEADS, HD)
    text_values = text_kv[1].reshape(branches, TXT, HEADS, HD)
    all_keys = jnp.concatenate([key_rot, text_keys], axis=1)
    all_values = jnp.concatenate([value, text_values], axis=1)
    key_valid = jnp.concatenate([jnp.ones((branches, tokens), dtype=bool), jnp.arange(TXT)[None, :] < text_lengths[:, None]], axis=1)
    query_heads = query.transpose(0, 2, 1, 3).reshape(branches * HEADS, tokens, HD)
    key_heads = all_keys.transpose(0, 2, 1, 3).reshape(branches * HEADS, tokens + TXT, HD)
    value_heads = all_values.transpose(0, 2, 1, 3).reshape(branches * HEADS, tokens + TXT, HD)
    valid_heads = jnp.repeat(key_valid, HEADS, axis=0)

    def one_pair(pair_items):
        query_one, keys_one, values_one, valid_one = pair_items
        scores = jnp.dot(query_one, keys_one.T, preferred_element_type=jnp.float32) * HD ** (-0.5)
        scores = jnp.where(valid_one[None, :], scores, -jnp.inf)
        row_top = lax.optimization_barrier(jnp.max(scores, axis=1, keepdims=True))
        weights = jnp.exp(scores - row_top)
        row_total = lax.optimization_barrier(jnp.sum(weights, axis=1, keepdims=True))
        mixed_out = jnp.dot(weights.astype(jnp.bfloat16), values_one, preferred_element_type=jnp.float32) / row_total
        return mixed_out.astype(jnp.bfloat16)
    attention = lax.map(one_pair, (query_heads, key_heads, value_heads, valid_heads))
    attention = attention.reshape(branches, HEADS, tokens, HD).transpose(0, 2, 1, 3).reshape(branches * tokens, HEADS * HD)
    proj = jnp.dot(attention, w_out, preferred_element_type=jnp.float32).reshape(branches, tokens, model_dim)
    return (widened + per_token[:, 2] * proj).astype(jnp.bfloat16)
```

```python
import jax
import jax.numpy as jnp
import numpy as np
from jax import lax
from jax.experimental import pallas as pl
from jax.experimental.pallas import tpu as pltpu
from jax.sharding import PartitionSpec as P

HD = 128
TOK = 128
LAT_W = 16
FRAMES = 32
HEAD_AXIS = 8
BRANCH = 3
HEADS_HERE = 3
PAIRS = BRANCH * HEADS_HERE
DSH = 384
TXT = 256
RING = 8
ROWS = BRANCH * TOK
MOD_ROWS = 16
SENT = ROWS + MOD_ROWS
LAST = PAIRS - 1
STAT_ROWS = 16
LAST_ROWS = TOK + STAT_ROWS
RETURN = TOK + LAST_ROWS
WIDE = 3 * DSH
rope_base = 256.0
norm_eps = 1e-06
LOG2E = float(np.log2(np.e))
EXP_SCALE = float(HD ** (-0.5) * np.log2(np.e))
MIB = 1024 * 1024


def whole(shape):
    return pl.BlockSpec(shape, lambda *_: (0,) * len(shape))


def limbs_of(value):
    limbs = []
    for _ in range(3):
        limb = value.astype(jnp.bfloat16).astype(jnp.float32)
        limbs.append(limb)
        value = value - limb
    return limbs


def rope_tables(frame):
    time_dims = HD // 8
    space_dims = (HD - time_dims) // 2
    freq = np.concatenate(
        [
            np.repeat(rope_base ** (-np.arange(0, z, 2, dtype=np.float64) / z), 2)
            for z in (time_dims, space_dims, space_dims)
        ]
    ).astype(np.float32)
    section = np.repeat(np.arange(3), (time_dims, space_dims, space_dims))
    token = jnp.arange(TOK, dtype=jnp.int32)[:, None]
    section = jnp.asarray(section)[None, :]
    position = jnp.where(
        section == 0, frame, jnp.where(section == 1, token // LAT_W, token % LAT_W)
    )
    angle = position.astype(jnp.float32) * jnp.asarray(freq)[None, :]
    sign = jnp.asarray(np.tile(np.array([-1.0, 1.0], np.float32), HD // 2))
    return jnp.cos(angle), jnp.sin(angle) * sign[None, :]


def prep_kernel(
    frame_ref, head_ref, shift_ref, ids_ref, lengths_ref, video_ref, table_ref,
    own_ref, gate_ref, place_ref, where_ref,
):
    head = head_ref[0]
    for s, step in enumerate((0, 0, 2, -2, 2, -2, 4, 4)):
        near = lax.rem(head + step + HEAD_AXIS, HEAD_AXIS)
        place_ref[s] = near if s in (0, 2, 3, 6) else near + 1 - 2 * lax.rem(near, 2)
    slab = lax.rem(lax.div(frame_ref[0], 2), RING)
    branch = lax.div(slab, HEADS_HERE)
    text_block = jnp.minimum(slab, 1)
    where_ref[0] = branch
    where_ref[1] = lax.rem(slab, HEADS_HERE)
    where_ref[2] = lengths_ref[branch]
    where_ref[3] = jnp.where(slab < 2, lengths_ref[BRANCH - 1] - 128 * text_block, 0)
    where_ref[4] = text_block
    level = ids_ref[lax.rem(frame_ref[0] + shift_ref[0], FRAMES)]
    looked = [table_ref[part, pl.ds(level, 1), :] for part in range(3)]
    gate_ref[...] = looked[2]
    limbs = limbs_of(looked[0]) + limbs_of(looked[1])
    limbs.append(jnp.zeros((MOD_ROWS - 6, DSH), jnp.float32))
    for b in range(BRANCH):
        own_ref[b * TOK : (b + 1) * TOK, :] = video_ref[b]
    own_ref[ROWS:SENT, :] = jnp.concatenate(limbs, axis=0).astype(jnp.bfloat16)


def prep(frame, head, queue_shift, timestep_ids, lengths, video, table):
    return pl.pallas_call(
        prep_kernel,
        out_shape=(
            jax.ShapeDtypeStruct((SENT, DSH), jnp.bfloat16),
            jax.ShapeDtypeStruct((1, DSH), jnp.float32),
            jax.ShapeDtypeStruct((HEAD_AXIS,), jnp.int32),
            jax.ShapeDtypeStruct((5,), jnp.int32),
        ),
        grid_spec=pltpu.PrefetchScalarGridSpec(
            num_scalar_prefetch=5,
            grid=(1,),
            in_specs=[whole((BRANCH, TOK, DSH)), whole((3, FRAMES, DSH))],
            out_specs=(
                whole((SENT, DSH)),
                whole((1, DSH)),
                pl.BlockSpec(memory_space=pltpu.SMEM),
                pl.BlockSpec(memory_space=pltpu.SMEM),
            ),
        ),
        compiler_params=pltpu.CompilerParams(vmem_limit_bytes=16 * MIB),
        name="prep",
    )(frame, head, queue_shift, timestep_ids, lengths, video, table)


def project_kernel(place_ref, *refs):
    blocks = refs[:HEAD_AXIS]
    (
        w_hbm, gain_ref, cos_ref, sin_ref, out_ref, last_ref, mod_ref, acc_ref, w_ref, sems,
    ) = refs[HEAD_AXIS:]
    copies = [
        pltpu.make_async_copy(w_hbm.at[n], w_ref.at[:, pl.ds(n * DSH, DSH)], sems.at[n])
        for n in range(3)
    ]
    for copy in copies:
        copy.start()
    step = 64

    def chunk(n, carry):
        here = pl.ds(pl.multiple_of(n * step, step), step)
        total = jnp.zeros((step, 128), jnp.float32)
        square = jnp.zeros((step, 128), jnp.float32)
        for block in blocks:
            for lane in range(0, DSH, 128):
                x = block[here, lane : lane + 128].astype(jnp.float32)
                total += x
                square += x * x
        mean = jnp.sum(total, axis=1, keepdims=True) / (HEAD_AXIS * DSH)
        var = jnp.sum(square, axis=1, keepdims=True) / (HEAD_AXIS * DSH) - mean * mean
        inv = lax.rsqrt(var + norm_eps)
        for s, block in enumerate(blocks):
            limbs = block[ROWS:SENT, :].astype(jnp.float32)
            shift = limbs[0:1] + limbs[1:2] + limbs[2:3]
            scale = limbs[3:4] + limbs[4:5] + limbs[5:6]
            x = block[here, :].astype(jnp.float32)
            y = (x - mean) * inv * (1.0 + scale) + shift
            start = pl.multiple_of(place_ref[s] * DSH, DSH)
            mod_ref[here, pl.ds(start, DSH)] = y.astype(jnp.bfloat16)
        return carry

    lax.fori_loop(0, ROWS // step, chunk, 0)

    def piece(part, p):
        b, hd = divmod(p, HEADS_HERE)
        lane = part * DSH + hd * HD
        return acc_ref[b * TOK : (b + 1) * TOK, lane : lane + HD]

    def turned(part, p):
        t = piece(part, p)
        t = t * lax.rsqrt(jnp.mean(t * t, axis=1, keepdims=True) + norm_eps)
        t = t * gain_ref[part : part + 1, :]
        even = lax.broadcasted_iota(jnp.int32, t.shape, 1) % 2 == 0
        other = jnp.where(even, pltpu.roll(t, HD - 1, 1), pltpu.roll(t, 1, 1))
        return (t * cos_ref[...] + other * sin_ref[...]).astype(jnp.bfloat16)

    for copy in copies:
        copy.wait()
    acc_ref[...] = jnp.dot(mod_ref[...], w_ref[...], preferred_element_type=jnp.float32)
    for part in range(3):
        for p in range(PAIRS):
            if part == 2:
                result = piece(part, p).astype(jnp.bfloat16)
            else:
                result = turned(part, p)
            if part == 0 and p == LAST:
                for n in range(RING):
                    out_ref[n, 3 * TOK : 4 * TOK, :] = result
            elif part == 0:
                out_ref[p, 2 * TOK : 3 * TOK, :] = result
            elif p == LAST:
                last_ref[(part - 1) * TOK : part * TOK, :] = result
            else:
                out_ref[p, (part - 1) * TOK : part * TOK, :] = result


def project(places, blocks, w, gains, cosine, sine):
    return pl.pallas_call(
        project_kernel,
        out_shape=(
            jax.ShapeDtypeStruct((RING, 4 * TOK, HD), jnp.bfloat16),
            jax.ShapeDtypeStruct((2 * TOK, HD), jnp.bfloat16),
        ),
        grid_spec=pltpu.PrefetchScalarGridSpec(
            num_scalar_prefetch=1,
            grid=(1,),
            in_specs=[whole((SENT, DSH)) for _ in blocks]
            + [
                pl.BlockSpec(memory_space=pltpu.HBM),
                whole((2, HD)),
                whole((TOK, HD)),
                whole((TOK, HD)),
            ],
            out_specs=(whole((RING, 4 * TOK, HD)), whole((2 * TOK, HD))),
            scratch_shapes=[
                pltpu.VMEM((ROWS, HEAD_AXIS * DSH), jnp.bfloat16),
                pltpu.VMEM((ROWS, WIDE), jnp.float32),
                pltpu.VMEM((HEAD_AXIS * DSH, WIDE), jnp.bfloat16),
                pltpu.SemaphoreType.DMA((3,)),
            ],
        ),
        compiler_params=pltpu.CompilerParams(vmem_limit_bytes=28 * MIB),
        cost_estimate=pl.CostEstimate(
            flops=2 * ROWS * HEAD_AXIS * DSH * 3 * DSH, bytes_accessed=12_000_000, transcendentals=0
        ),
        name="project",
    )(places, *blocks, w, gains, cosine, sine)


QUAD = 4
TILE = QUAD * TOK
SET = RING * TOK
DIMS = (((1,), (1,)), ((), ()))


def score_keys(q, keys, score_ref, column, top):
    scores = lax.dot_general(q, keys, DIMS, preferred_element_type=jnp.float32)
    score_ref[:, column : column + scores.shape[1]] = scores
    for lane in range(0, scores.shape[1], 128):
        top = jnp.maximum(top, scores[:, lane : lane + 128])
    return top


def score_text(q, keys, valid, score_ref, column, top):
    scores = lax.dot_general(q, keys, DIMS, preferred_element_type=jnp.float32)
    index = lax.broadcasted_iota(jnp.int32, scores.shape, 1)
    scores = jnp.where(index < valid, scores, -jnp.inf)
    score_ref[:, column : column + scores.shape[1]] = scores
    for lane in range(0, scores.shape[1], 128):
        top = jnp.maximum(top, scores[:, lane : lane + 128])
    return top


def mix(score_ref, value_ref, top, count):
    mixed = jnp.zeros((TILE, 2 * HD), jnp.float32)
    for first in range(0, count, SET):
        stop = min(first + SET, count)
        weights = jnp.exp2(score_ref[:, first:stop] * EXP_SCALE - top).astype(jnp.bfloat16)
        mixed += jnp.dot(weights, value_ref[first:stop, :], preferred_element_type=jnp.float32)
    return mixed


def lay_values(value_ref, pieces):
    lane = lax.broadcasted_iota(jnp.int32, (value_ref.shape[0], HD), 1)
    value_ref[:, HD:] = jnp.where(lane == 0, 1.0, 0.0).astype(jnp.bfloat16)
    row = 0
    for piece in pieces:
        value_ref[row : row + piece.shape[0], :HD] = piece
        row += piece.shape[0]


def set_keys(ref):
    return ref[:, 0:TOK, :].reshape(SET, HD)


def set_values(ref):
    return ref[:, TOK : 2 * TOK, :].reshape(SET, HD)


def first_step():
    return pl.program_id(0) == 0


def tile_rows():
    return pl.ds(pl.multiple_of(pl.program_id(0) * TILE, TILE), TILE)


IN_VMEM = pl.BlockSpec(memory_space=pltpu.VMEM)


def attend_near_kernel(
    where_ref, q_ref, own_ref, core_ref, text_ref, w_hbm,
    mixed_ref, top_ref, w_ref, score_ref, value_ref, sem,
):
    copy = pltpu.make_async_copy(w_hbm, w_ref, sem)

    @pl.when(first_step())
    def _():
        copy.start()
        lay_values(value_ref, [set_values(own_ref), set_values(core_ref), text_ref[1, 0]])

    q = q_ref[...].reshape(TILE, HD)
    top = jnp.full((TILE, 128), -jnp.inf, jnp.float32)
    for n, ref in enumerate((own_ref, core_ref)):
        top = score_keys(q, set_keys(ref), score_ref, n * SET, top)
    top = score_text(q, text_ref[0, 0], where_ref[2], score_ref, 2 * SET, top)
    top = jnp.max(top, axis=1, keepdims=True) * EXP_SCALE
    here = tile_rows()
    mixed_ref[here, :] = mix(score_ref, value_ref, top, 2 * SET + TXT)
    top_ref[here, :] = jnp.broadcast_to(top, (TILE, 128))

    @pl.when(pl.program_id(0) == SET // TILE - 1)
    def _():
        copy.wait()


def attend_near(where, received, own, core, text_kv, w_out):
    return pl.pallas_call(
        attend_near_kernel,
        out_shape=(
            pltpu.VMEM((SET, 2 * HD), jnp.float32),
            pltpu.VMEM((SET, 128), jnp.float32),
            pltpu.VMEM(w_out.shape, w_out.dtype),
        ),
        grid_spec=pltpu.PrefetchScalarGridSpec(
            num_scalar_prefetch=1,
            grid=(SET // TILE,),
            in_specs=[
                pl.BlockSpec((QUAD, TOK, HD), lambda i, w: (i, 2, 0)),
                whole((RING, 2 * TOK, HD)),
                whole((RING, 2 * TOK, HD)),
                pl.BlockSpec((2, 1, TXT, HD), lambda i, w: (0, w[0], 0, w[1])),
                pl.BlockSpec(memory_space=pltpu.HBM),
            ],
            out_specs=(IN_VMEM, IN_VMEM, IN_VMEM),
            scratch_shapes=[
                pltpu.VMEM((TILE, 2 * SET + TXT), jnp.float32),
                pltpu.VMEM((2 * SET + TXT, 2 * HD), jnp.bfloat16),
                pltpu.SemaphoreType.DMA(()),
            ],
        ),
        compiler_params=pltpu.CompilerParams(vmem_limit_bytes=18 * MIB),
        cost_estimate=pl.CostEstimate(
            flops=4 * SET * 2304 * HD, bytes_accessed=3_000_000, transcendentals=SET * 2304
        ),
        name="attend_near",
    )(where, received, own, core, text_kv, w_out)


LAST_KEYS = QUAD * TOK + 128


def lay_last_kernel(where_ref, *refs):
    last_refs = refs[:QUAD]
    text_ref, keys_ref, value_ref = refs[QUAD:]
    for n, ref in enumerate(last_refs):
        keys_ref[n * TOK : (n + 1) * TOK, :] = ref[0:TOK, :]
    keys_ref[QUAD * TOK :, :] = text_ref[0, 0]
    lay_values(value_ref, [ref[TOK : 2 * TOK, :] for ref in last_refs] + [text_ref[1, 0]])


def lay_last(where, lasts, text_kv):
    return pl.pallas_call(
        lay_last_kernel,
        out_shape=(
            jax.ShapeDtypeStruct((LAST_KEYS, HD), jnp.bfloat16),
            jax.ShapeDtypeStruct((LAST_KEYS, 2 * HD), jnp.bfloat16),
        ),
        grid_spec=pltpu.PrefetchScalarGridSpec(
            num_scalar_prefetch=1,
            grid=(1,),
            in_specs=[whole((2 * TOK, HD)) for _ in lasts]
            + [
                pl.BlockSpec(
                    (2, 1, 128, HD), lambda i, w: (0, BRANCH - 1, w[4], HEADS_HERE - 1)
                )
            ],
            out_specs=(whole((LAST_KEYS, HD)), whole((LAST_KEYS, 2 * HD))),
        ),
        compiler_params=pltpu.CompilerParams(vmem_limit_bytes=16 * MIB),
        cost_estimate=pl.CostEstimate(
            flops=10_000_000_000, bytes_accessed=10_000_000, transcendentals=0
        ),
        name="lay_last",
    )(where, *lasts, text_kv)


def attend_last_kernel(where_ref, q_ref, keys_ref, value_ref, out_ref, score_ref):
    video_keys = QUAD * TOK
    q = q_ref[...].reshape(TILE, HD)
    top = jnp.full((TILE, 128), -jnp.inf, jnp.float32)
    top = score_keys(q, keys_ref[0:video_keys, :], score_ref, 0, top)
    top = score_text(q, keys_ref[video_keys:, :], where_ref[3], score_ref, video_keys, top)
    top = jnp.max(top, axis=1, keepdims=True) * EXP_SCALE
    mixed = mix(score_ref, value_ref, top, LAST_KEYS)
    total = mixed[:, HD : HD + 1]
    result = mixed[:, :HD] / total
    out_ref[:, 0:TOK, :] = result.astype(jnp.bfloat16).reshape(QUAD, TOK, HD)
    level = jnp.broadcast_to(top + jnp.log(total) * LOG2E, (TILE, HD))
    for f in range(QUAD):
        row = jnp.transpose(level[f * TOK : (f + 1) * TOK])[0:1]
        stats = limbs_of(row) + [jnp.zeros((STAT_ROWS - 3, HD), jnp.float32)]
        out_ref[f, TOK:LAST_ROWS, :] = jnp.concatenate(stats, axis=0).astype(jnp.bfloat16)


def attend_last(where, received, keys, values):
    return pl.pallas_call(
        attend_last_kernel,
        out_shape=jax.ShapeDtypeStruct((RING, LAST_ROWS, HD), jnp.bfloat16),
        grid_spec=pltpu.PrefetchScalarGridSpec(
            num_scalar_prefetch=1,
            grid=(SET // TILE,),
            in_specs=[
                pl.BlockSpec((QUAD, TOK, HD), lambda i, w: (i, 3, 0)),
                whole((LAST_KEYS, HD)),
                whole((LAST_KEYS, 2 * HD)),
            ],
            out_specs=pl.BlockSpec((QUAD, LAST_ROWS, HD), lambda i, w: (i, 0, 0)),
            scratch_shapes=[pltpu.VMEM((TILE, LAST_KEYS), jnp.float32)],
        ),
        compiler_params=pltpu.CompilerParams(vmem_limit_bytes=16 * MIB),
        cost_estimate=pl.CostEstimate(
            flops=4 * SET * 640 * HD, bytes_accessed=1_000_000, transcendentals=SET * 640
        ),
        name="attend_last",
    )(where, received, keys, values)


def attend_far_kernel(
    q_ref, y_ref, diagonal_ref, last_ref, mixed_ref, top_ref, out_ref, score_ref, value_ref
):
    @pl.when(first_step())
    def _():
        lay_values(value_ref, [set_values(y_ref), set_values(diagonal_ref)])

    q = q_ref[...].reshape(TILE, HD)
    top = jnp.full((TILE, 128), -jnp.inf, jnp.float32)
    for n, ref in enumerate((y_ref, diagonal_ref)):
        top = score_keys(q, set_keys(ref), score_ref, n * SET, top)
    here = tile_rows()
    before = top_ref[here, 0:1]
    top = jnp.maximum(jnp.max(top, axis=1, keepdims=True) * EXP_SCALE, before)
    mixed = mix(score_ref, value_ref, top, 2 * SET) + mixed_ref[here, :] * jnp.exp2(before - top)
    result = mixed[:, :HD] / mixed[:, HD : HD + 1]
    out_ref[:, 0:TOK, :] = result.astype(jnp.bfloat16).reshape(QUAD, TOK, HD)
    out_ref[:, TOK:RETURN, :] = last_ref[...]


def in_vmem(x):
    return pltpu.with_memory_space_constraint(x, pltpu.VMEM)


def in_hbm(x):
    return pltpu.with_memory_space_constraint(x, pltpu.HBM)


def attend_far(received, over_y, diagonal, last, mixed, top):
    return pl.pallas_call(
        attend_far_kernel,
        out_shape=jax.ShapeDtypeStruct((RING, RETURN, HD), jnp.bfloat16),
        grid=(SET // TILE,),
        in_specs=[
            pl.BlockSpec((QUAD, TOK, HD), lambda i: (i, 2, 0)),
            whole((RING, 2 * TOK, HD)),
            whole((RING, 2 * TOK, HD)),
            pl.BlockSpec((QUAD, LAST_ROWS, HD), lambda i: (i, 0, 0)),
            IN_VMEM,
            IN_VMEM,
        ],
        out_specs=pl.BlockSpec((QUAD, RETURN, HD), lambda i: (i, 0, 0)),
        scratch_shapes=[
            pltpu.VMEM((TILE, 2 * SET), jnp.float32),
            pltpu.VMEM((2 * SET, 2 * HD), jnp.bfloat16),
        ],
        compiler_params=pltpu.CompilerParams(vmem_limit_bytes=18 * MIB),
        cost_estimate=pl.CostEstimate(
            flops=4 * SET * 2048 * HD, bytes_accessed=4_000_000, transcendentals=SET * 2048
        ),
        name="attend_far",
    )(received, over_y, diagonal, last, in_vmem(mixed), in_vmem(top))


def output_kernel(place_ref, back_ref, w_ref, *refs):
    out_refs, attn_ref = refs[:HEAD_AXIS], refs[HEAD_AXIS]
    for p in range(RING):
        b, hd = divmod(p, HEADS_HERE)
        attn_ref[b * TOK : (b + 1) * TOK, hd * HD : (hd + 1) * HD] = back_ref[p, 0:TOK, :]
    levels = []
    for p in range(RING):
        stats = back_ref[p, 2 * TOK : RETURN, :].astype(jnp.float32)
        row = stats[0:1] + stats[1:2] + stats[2:3]
        levels.append(jnp.transpose(jnp.broadcast_to(row, (TOK, HD))))
    top = levels[0]
    for level in levels[1:]:
        top = jnp.maximum(top, level)
    total = jnp.zeros((TOK, HD), jnp.float32)
    mixed = jnp.zeros((TOK, HD), jnp.float32)
    for p, level in enumerate(levels):
        weight = jnp.exp2(level - top)
        total += weight
        mixed += weight * back_ref[p, TOK : 2 * TOK, :].astype(jnp.float32)
    attn_ref[(BRANCH - 1) * TOK :, (HEADS_HERE - 1) * HD :] = (mixed / total).astype(jnp.bfloat16)
    for s in range(HEAD_AXIS):
        start = pl.multiple_of(place_ref[s] * DSH, DSH)
        out_refs[s][...] = jnp.dot(
            attn_ref[...], w_ref[:, pl.ds(start, DSH)], preferred_element_type=jnp.float32
        ).astype(jnp.bfloat16)


def output(places, back, w_out):
    return pl.pallas_call(
        output_kernel,
        out_shape=tuple(
            jax.ShapeDtypeStruct((ROWS, DSH), jnp.bfloat16) for _ in range(HEAD_AXIS)
        ),
        grid_spec=pltpu.PrefetchScalarGridSpec(
            num_scalar_prefetch=1,
            grid=(1,),
            in_specs=[
                whole((RING, RETURN, HD)),
                IN_VMEM,
            ],
            out_specs=tuple(whole((ROWS, DSH)) for _ in range(HEAD_AXIS)),
            scratch_shapes=[pltpu.VMEM((ROWS, DSH), jnp.bfloat16)],
        ),
        compiler_params=pltpu.CompilerParams(vmem_limit_bytes=24 * MIB),
        cost_estimate=pl.CostEstimate(
            flops=2 * ROWS * DSH * DSH * HEAD_AXIS, bytes_accessed=5_000_000, transcendentals=0
        ),
        name="output",
    )(places, back, in_vmem(w_out))


def head_move(x, step):
    return lax.ppermute(x, "head", [(i, (i + step) % HEAD_AXIS) for i in range(HEAD_AXIS)])


def head_partner(x):
    return lax.ppermute(x, "head", [(i, i ^ 1) for i in range(HEAD_AXIS)])


def frame_move(x, flip):
    return lax.ppermute(x, "frame", [(i, i ^ flip) for i in range(FRAMES)])


def gather_head(own):
    partner = head_partner(own)
    opposite = head_move(own, 4)
    ahead = head_move(own, -2)
    behind = head_move(own, 2)
    return [
        own,
        partner,
        ahead,
        behind,
        head_move(partner, -2),
        head_move(partner, 2),
        opposite,
        head_partner(opposite),
    ]


def add(*terms):
    total = terms[0].astype(jnp.float32)
    for term in terms[1:]:
        total += term.astype(jnp.float32)
    return total


def scatter_head(parts):
    for_opposite = head_partner(parts[7])
    for_partner = [head_move(parts[4], 2), head_move(parts[5], -2)]
    direct = [head_move(parts[2], 2), head_move(parts[3], -2)]
    over_y = head_partner(add(parts[1], *for_partner).astype(jnp.bfloat16))
    across = head_move(add(parts[6], for_opposite).astype(jnp.bfloat16), 4)
    return add(parts[0], *direct, over_y, across)


def body(
    video, w_qkv, w_out, text_kv, text_lengths, norm_gains, mod_table, timestep_ids, queue_shift
):
    text_kv = in_hbm(text_kv)
    frame = lax.axis_index("frame").astype(jnp.int32)
    head = lax.axis_index("head").astype(jnp.int32)
    own, gate, places, where = prep(
        frame.reshape(1),
        head.reshape(1),
        queue_shift,
        in_hbm(timestep_ids),
        in_hbm(text_lengths),
        in_hbm(video),
        in_hbm(mod_table.transpose(1, 0, 2)),
    )
    cosine, sine = rope_tables(frame)
    blocks = gather_head(own)
    weights = in_hbm(w_qkv.transpose(1, 0, 2))
    send, last = project(places, blocks, weights, in_hbm(norm_gains), cosine, sine)
    rings = [[(y * RING + z) * 2 + core for z in range(RING)] for y in range(2) for core in range(2)]

    def over_rings(x):
        return lax.all_to_all(x, "frame", 0, 0, axis_index_groups=rings, tiled=True)

    received = over_rings(send)
    flips = (1, FRAMES // 2, FRAMES // 2 + 1)
    lasts = [last] + [frame_move(last, flip) for flip in flips]
    last_keys, last_values = lay_last(where, lasts, text_kv)
    near = received[:, : 2 * TOK]
    over_y = frame_move(near, FRAMES // 2)
    over_core = frame_move(near, 1)
    ninth = attend_last(where, received, last_keys, last_values)
    mixed, top, w_held = attend_near(where, received, near, over_core, text_kv, in_hbm(w_out))
    over_y, _, _ = lax.optimization_barrier((over_y, mixed, ninth))
    diagonal = frame_move(over_y, 1)
    returned = attend_far(received, over_y, diagonal, ninth, mixed, top)
    partial = output(places, over_rings(returned), w_held)
    proj = scatter_head(partial).reshape(video.shape)
    return (video.astype(jnp.float32) + gate * proj).astype(jnp.bfloat16)


def solution(mesh):
    in_specs = (
        P(None, "frame", "head"),
        P(None, None, "head"),
        P("head", None),
        P(None, None, None, "head"),
        P(),
        P(),
        P(None, None, "head"),
        P(),
        P(),
    )
    out_specs = P(None, "frame", "head")
    return jax.shard_map(body, mesh=mesh, in_specs=in_specs, out_specs=out_specs, check_vma=False)
```

```python
import jax
import jax.numpy as jnp
import numpy as np
from jax import lax
from jax.experimental import pallas as pl
from jax.experimental.pallas import tpu as pltpu
from jax.sharding import PartitionSpec as P

HD = 128
TOK = 128
LAT_W = 16
FRAMES = 32
HEAD_AXIS = 8
BRANCH = 3
HEADS_HERE = 3
PAIRS = BRANCH * HEADS_HERE
DSH = 384
TXT = 256
RING = 8
ROWS = BRANCH * TOK
MOD_ROWS = 16
SENT = ROWS + MOD_ROWS
LAST = PAIRS - 1
STAT_ROWS = 16
LAST_ROWS = TOK + STAT_ROWS
RETURN = TOK + LAST_ROWS
WIDE = 3 * DSH
rope_base = 256.0
norm_eps = 1e-06
LOG2E = float(np.log2(np.e))
EXP_SCALE = float(HD ** (-0.5) * np.log2(np.e))
MIB = 1024 * 1024


def whole(shape):
    return pl.BlockSpec(shape, lambda *_: (0,) * len(shape))


def limbs_of(value):
    limbs = []
    for _ in range(3):
        limb = value.astype(jnp.bfloat16).astype(jnp.float32)
        limbs.append(limb)
        value = value - limb
    return limbs


def rope_tables(frame):
    time_dims = HD // 8
    space_dims = (HD - time_dims) // 2
    freq = np.concatenate(
        [
            np.repeat(rope_base ** (-np.arange(0, z, 2, dtype=np.float64) / z), 2)
            for z in (time_dims, space_dims, space_dims)
        ]
    ).astype(np.float32)
    section = np.repeat(np.arange(3), (time_dims, space_dims, space_dims))
    token = jnp.arange(TOK, dtype=jnp.int32)[:, None]
    section = jnp.asarray(section)[None, :]
    position = jnp.where(
        section == 0, frame, jnp.where(section == 1, token // LAT_W, token % LAT_W)
    )
    angle = position.astype(jnp.float32) * jnp.asarray(freq)[None, :]
    sign = jnp.asarray(np.tile(np.array([-1.0, 1.0], np.float32), HD // 2))
    return jnp.cos(angle), jnp.sin(angle) * sign[None, :]


def prep_kernel(
    frame_ref, head_ref, shift_ref, ids_ref, lengths_ref, video_ref, table_ref,
    own_ref, gate_ref, place_ref, where_ref,
):
    head = head_ref[0]
    for s, step in enumerate((0, 0, 2, -2, 2, -2, 4, 4)):
        near = lax.rem(head + step + HEAD_AXIS, HEAD_AXIS)
        place_ref[s] = near if s in (0, 2, 3, 6) else near + 1 - 2 * lax.rem(near, 2)
    slab = lax.rem(lax.div(frame_ref[0], 2), RING)
    branch = lax.div(slab, HEADS_HERE)
    text_block = jnp.minimum(slab, 1)
    where_ref[0] = branch
    where_ref[1] = lax.rem(slab, HEADS_HERE)
    where_ref[2] = lengths_ref[branch]
    where_ref[3] = jnp.where(slab < 2, lengths_ref[BRANCH - 1] - 128 * text_block, 0)
    where_ref[4] = text_block
    level = ids_ref[lax.rem(frame_ref[0] + shift_ref[0], FRAMES)]
    looked = [table_ref[part, pl.ds(level, 1), :] for part in range(3)]
    gate_ref[...] = looked[2]
    limbs = limbs_of(looked[0]) + limbs_of(looked[1])
    limbs.append(jnp.zeros((MOD_ROWS - 6, DSH), jnp.float32))
    for b in range(BRANCH):
        own_ref[b * TOK : (b + 1) * TOK, :] = video_ref[b]
    own_ref[ROWS:SENT, :] = jnp.concatenate(limbs, axis=0).astype(jnp.bfloat16)


def prep(frame, head, queue_shift, timestep_ids, lengths, video, table):
    return pl.pallas_call(
        prep_kernel,
        out_shape=(
            jax.ShapeDtypeStruct((SENT, DSH), jnp.bfloat16),
            jax.ShapeDtypeStruct((1, DSH), jnp.float32),
            jax.ShapeDtypeStruct((HEAD_AXIS,), jnp.int32),
            jax.ShapeDtypeStruct((5,), jnp.int32),
        ),
        grid_spec=pltpu.PrefetchScalarGridSpec(
            num_scalar_prefetch=5,
            grid=(1,),
            in_specs=[whole((BRANCH, TOK, DSH)), whole((3, FRAMES, DSH))],
            out_specs=(
                whole((SENT, DSH)),
                whole((1, DSH)),
                pl.BlockSpec(memory_space=pltpu.SMEM),
                pl.BlockSpec(memory_space=pltpu.SMEM),
            ),
        ),
        compiler_params=pltpu.CompilerParams(vmem_limit_bytes=16 * MIB),
        name="prep",
    )(frame, head, queue_shift, timestep_ids, lengths, video, table)


def project_kernel(place_ref, *refs):
    blocks = refs[:HEAD_AXIS]
    (
        w_hbm, gain_ref, cos_ref, sin_ref, kv_ref, q_ref, last_ref, mod_ref, acc_ref, w_ref, sems,
    ) = refs[HEAD_AXIS:]
    copies = [
        pltpu.make_async_copy(w_hbm.at[n], w_ref.at[:, pl.ds(n * DSH, DSH)], sems.at[n])
        for n in range(3)
    ]
    for copy in copies:
        copy.start()
    step = 64

    def chunk(n, carry):
        here = pl.ds(pl.multiple_of(n * step, step), step)
        total = jnp.zeros((step, 128), jnp.float32)
        square = jnp.zeros((step, 128), jnp.float32)
        for block in blocks:
            for lane in range(0, DSH, 128):
                x = block[here, lane : lane + 128].astype(jnp.float32)
                total += x
                square += x * x
        mean = jnp.sum(total, axis=1, keepdims=True) / (HEAD_AXIS * DSH)
        var = jnp.sum(square, axis=1, keepdims=True) / (HEAD_AXIS * DSH) - mean * mean
        inv = lax.rsqrt(var + norm_eps)
        for s, block in enumerate(blocks):
            limbs = block[ROWS:SENT, :].astype(jnp.float32)
            shift = limbs[0:1] + limbs[1:2] + limbs[2:3]
            scale = limbs[3:4] + limbs[4:5] + limbs[5:6]
            x = block[here, :].astype(jnp.float32)
            y = (x - mean) * inv * (1.0 + scale) + shift
            start = pl.multiple_of(place_ref[s] * DSH, DSH)
            mod_ref[here, pl.ds(start, DSH)] = y.astype(jnp.bfloat16)
        return carry

    lax.fori_loop(0, ROWS // step, chunk, 0)

    def piece(part, p):
        b, hd = divmod(p, HEADS_HERE)
        lane = part * DSH + hd * HD
        return acc_ref[b * TOK : (b + 1) * TOK, lane : lane + HD]

    def turned(part, p):
        t = piece(part, p)
        t = t * lax.rsqrt(jnp.mean(t * t, axis=1, keepdims=True) + norm_eps)
        t = t * gain_ref[part : part + 1, :]
        even = lax.broadcasted_iota(jnp.int32, t.shape, 1) % 2 == 0
        other = jnp.where(even, pltpu.roll(t, HD - 1, 1), pltpu.roll(t, 1, 1))
        return (t * cos_ref[...] + other * sin_ref[...]).astype(jnp.bfloat16)

    for copy in copies:
        copy.wait()
    acc_ref[...] = jnp.dot(mod_ref[...], w_ref[...], preferred_element_type=jnp.float32)
    for part in range(3):
        for p in range(PAIRS):
            if part == 2:
                result = piece(part, p).astype(jnp.bfloat16)
            else:
                result = turned(part, p)
            if part == 0 and p == LAST:
                for n in range(RING):
                    q_ref[n, TOK : 2 * TOK, :] = result
            elif part == 0:
                q_ref[p, 0:TOK, :] = result
            elif p == LAST:
                last_ref[(part - 1) * TOK : part * TOK, :] = result
            else:
                kv_ref[p, (part - 1) * TOK : part * TOK, :] = result


def project(places, blocks, w, gains, cosine, sine):
    return pl.pallas_call(
        project_kernel,
        out_shape=(
            jax.ShapeDtypeStruct((RING, 2 * TOK, HD), jnp.bfloat16),
            jax.ShapeDtypeStruct((RING, 2 * TOK, HD), jnp.bfloat16),
            jax.ShapeDtypeStruct((2 * TOK, HD), jnp.bfloat16),
        ),
        grid_spec=pltpu.PrefetchScalarGridSpec(
            num_scalar_prefetch=1,
            grid=(1,),
            in_specs=[whole((SENT, DSH)) for _ in blocks]
            + [
                pl.BlockSpec(memory_space=pltpu.HBM),
                whole((2, HD)),
                whole((TOK, HD)),
                whole((TOK, HD)),
            ],
            out_specs=(
                whole((RING, 2 * TOK, HD)),
                whole((RING, 2 * TOK, HD)),
                whole((2 * TOK, HD)),
            ),
            scratch_shapes=[
                pltpu.VMEM((ROWS, HEAD_AXIS * DSH), jnp.bfloat16),
                pltpu.VMEM((ROWS, WIDE), jnp.float32),
                pltpu.VMEM((HEAD_AXIS * DSH, WIDE), jnp.bfloat16),
                pltpu.SemaphoreType.DMA((3,)),
            ],
        ),
        compiler_params=pltpu.CompilerParams(vmem_limit_bytes=28 * MIB),
        cost_estimate=pl.CostEstimate(
            flops=2 * ROWS * HEAD_AXIS * DSH * 3 * DSH, bytes_accessed=12_000_000, transcendentals=0
        ),
        name="project",
    )(places, *blocks, w, gains, cosine, sine)


QUAD = 4
TILE = QUAD * TOK
SET = RING * TOK
KEYS = QUAD * SET + TXT
CHUNK = 1024
DIMS = (((1,), (1,)), ((), ()))


def attend_rows(flag_ref, q, keys_ref, value_ref, valid, score_ref, top_ref, mixed_ref):
    count = keys_ref.shape[0]
    text = TXT if count == KEYS else TXT // 2

    def scores_of(first, stop):
        scores = lax.dot_general(
            q, keys_ref[first:stop, :], DIMS, preferred_element_type=jnp.float32
        )
        if first == count - text:
            index = lax.broadcasted_iota(jnp.int32, scores.shape, 1)
            scores = jnp.where(index < valid, scores, -jnp.inf)
        return scores

    cuts = list(range(0, count - text, CHUNK)) + [count - text, count]
    pieces = list(zip(cuts[:-1], cuts[1:]))

    @pl.when(flag_ref[0] == 1)
    def _():
        mixed = jnp.zeros((TILE, 2 * HD), jnp.float32)
        for first, stop in pieces:
            weights = jnp.exp2(scores_of(first, stop) * EXP_SCALE).astype(jnp.bfloat16)
            mixed += jnp.dot(weights, value_ref[first:stop, :], preferred_element_type=jnp.float32)
        mixed_ref[...] = mixed
        top_ref[...] = jnp.zeros((TILE, 128), jnp.float32)

    @pl.when(flag_ref[0] != 1)
    def _():
        top = jnp.full((TILE, 128), -jnp.inf, jnp.float32)
        for first, stop in pieces:
            scores = scores_of(first, stop)
            score_ref[:, first:stop] = scores
            for lane in range(0, stop - first, 128):
                top = jnp.maximum(top, scores[:, lane : lane + 128])
        top = jnp.max(top, axis=1, keepdims=True) * EXP_SCALE
        top_ref[...] = jnp.broadcast_to(top, (TILE, 128))
        mixed_ref[...] = jnp.zeros((TILE, 2 * HD), jnp.float32)
        width = 128

        def step(n, carry):
            here = pl.ds(pl.multiple_of(n * width, width), width)
            weights = jnp.exp2(score_ref[:, here] * EXP_SCALE - top).astype(jnp.bfloat16)
            mixed_ref[...] += jnp.dot(
                weights, value_ref[here, :], preferred_element_type=jnp.float32
            )
            return carry

        lax.fori_loop(0, count // width, step, 0)


def lay_values(value_ref, pieces):
    lane = lax.broadcasted_iota(jnp.int32, (value_ref.shape[0], HD), 1)
    value_ref[:, HD:] = jnp.where(lane == 0, 1.0, 0.0).astype(jnp.bfloat16)
    row = 0
    for piece in pieces:
        value_ref[row : row + piece.shape[0], :HD] = piece
        row += piece.shape[0]


IN_VMEM = pl.BlockSpec(memory_space=pltpu.VMEM)


def in_vmem(x):
    return pltpu.with_memory_space_constraint(x, pltpu.VMEM)


def in_hbm(x):
    return pltpu.with_memory_space_constraint(x, pltpu.HBM)


def lay_kernel(where_ref, *refs):
    set_refs = refs[:QUAD]
    text_ref, last_text_ref, gain_ref, w_hbm, keys_ref, value_ref, w_ref, flag_ref, sem = refs[QUAD:]
    copy = pltpu.make_async_copy(w_hbm, w_ref, sem)
    copy.start()
    for n, ref in enumerate(set_refs):
        keys_ref[n * SET : (n + 1) * SET, :] = ref[:, 0:TOK, :].reshape(SET, HD)
    keys_ref[QUAD * SET :, :] = text_ref[0, 0]
    lay_values(
        value_ref,
        [ref[:, TOK : 2 * TOK, :].reshape(SET, HD) for ref in set_refs] + [text_ref[1, 0]],
    )
    slack = 1.03 * HD
    gains = gain_ref[...] * gain_ref[...]
    query_norm = slack * jnp.max(gains[0:1])
    key_norm = slack * jnp.max(gains[1:2])
    for ref in (text_ref, last_text_ref):
        text = ref[0, 0].astype(jnp.float32)
        key_norm = jnp.maximum(key_norm, jnp.max(jnp.sum(text * text, axis=1)))
    bound = EXP_SCALE * EXP_SCALE * query_norm * key_norm
    flag_ref[0] = jnp.where(bound < MOST_LOG2 * MOST_LOG2, 1, 0)
    copy.wait()


MOST_LOG2 = 90.0


def lay(where, sets, text_kv, gains, w_out):
    return pl.pallas_call(
        lay_kernel,
        out_shape=(
            pltpu.VMEM((KEYS, HD), jnp.bfloat16),
            pltpu.VMEM((KEYS, 2 * HD), jnp.bfloat16),
            pltpu.VMEM(w_out.shape, w_out.dtype),
            jax.ShapeDtypeStruct((1,), jnp.int32),
        ),
        grid_spec=pltpu.PrefetchScalarGridSpec(
            num_scalar_prefetch=1,
            grid=(1,),
            in_specs=[whole((RING, 2 * TOK, HD)) for _ in sets]
            + [
                pl.BlockSpec((2, 1, TXT, HD), lambda i, w: (0, w[0], 0, w[1])),
                pl.BlockSpec(
                    (1, 1, TXT, HD), lambda i, w: (0, BRANCH - 1, 0, HEADS_HERE - 1)
                ),
                whole((2, HD)),
                pl.BlockSpec(memory_space=pltpu.HBM),
            ],
            out_specs=(IN_VMEM, IN_VMEM, IN_VMEM, pl.BlockSpec(memory_space=pltpu.SMEM)),
            scratch_shapes=[pltpu.SemaphoreType.DMA(())],
        ),
        compiler_params=pltpu.CompilerParams(vmem_limit_bytes=16 * MIB),
        cost_estimate=pl.CostEstimate(
            flops=5_000_000_000, bytes_accessed=10_000_000, transcendentals=0
        ),
        name="lay",
    )(where, *sets, text_kv, text_kv, gains, in_hbm(w_out))


LAST_KEYS = QUAD * TOK + TXT // 2


def lay_last_kernel(where_ref, *refs):
    last_refs = refs[:QUAD]
    text_ref, keys_ref, value_ref = refs[QUAD:]
    for n, ref in enumerate(last_refs):
        keys_ref[n * TOK : (n + 1) * TOK, :] = ref[0:TOK, :]
    keys_ref[QUAD * TOK :, :] = text_ref[0, 0]
    lay_values(value_ref, [ref[TOK : 2 * TOK, :] for ref in last_refs] + [text_ref[1, 0]])


def lay_last(where, lasts, text_kv):
    return pl.pallas_call(
        lay_last_kernel,
        out_shape=(
            pltpu.VMEM((LAST_KEYS, HD), jnp.bfloat16),
            pltpu.VMEM((LAST_KEYS, 2 * HD), jnp.bfloat16),
        ),
        grid_spec=pltpu.PrefetchScalarGridSpec(
            num_scalar_prefetch=1,
            grid=(1,),
            in_specs=[whole((2 * TOK, HD)) for _ in lasts]
            + [
                pl.BlockSpec(
                    (2, 1, TXT // 2, HD), lambda i, w: (0, BRANCH - 1, w[4], HEADS_HERE - 1)
                )
            ],
            out_specs=(IN_VMEM, IN_VMEM),
        ),
        compiler_params=pltpu.CompilerParams(vmem_limit_bytes=16 * MIB),
        cost_estimate=pl.CostEstimate(
            flops=10_000_000_000, bytes_accessed=10_000_000, transcendentals=0
        ),
        name="lay_last",
    )(where, *lasts, text_kv)


def attend_kernel(
    where_ref, flag_ref, q_ref, keys_ref, value_ref, last_keys_ref, last_value_ref,
    out_ref, score_ref, top_ref, mixed_ref,
):
    q = q_ref[:, 0:TOK, :].reshape(TILE, HD)
    attend_rows(
        flag_ref, q, keys_ref, value_ref, where_ref[2], score_ref, top_ref, mixed_ref
    )
    result = mixed_ref[:, :HD] / mixed_ref[:, HD : HD + 1]
    out_ref[:, 0:TOK, :] = result.astype(jnp.bfloat16).reshape(QUAD, TOK, HD)
    q = q_ref[:, TOK : 2 * TOK, :].reshape(TILE, HD)
    attend_rows(
        flag_ref, q, last_keys_ref, last_value_ref, where_ref[3], score_ref, top_ref, mixed_ref
    )
    total = mixed_ref[:, HD : HD + 1]
    result = mixed_ref[:, :HD] / total
    out_ref[:, TOK : 2 * TOK, :] = result.astype(jnp.bfloat16).reshape(QUAD, TOK, HD)
    level = top_ref[...] + jnp.log(total) * LOG2E
    for f in range(QUAD):
        row = jnp.transpose(level[f * TOK : (f + 1) * TOK])[0:1]
        stats = limbs_of(row) + [jnp.zeros((STAT_ROWS - 3, HD), jnp.float32)]
        out_ref[f, 2 * TOK : RETURN, :] = jnp.concatenate(stats, axis=0).astype(jnp.bfloat16)


def attend(where, flag, queries, keys, values, last_keys, last_values):
    return pl.pallas_call(
        attend_kernel,
        out_shape=jax.ShapeDtypeStruct((RING, RETURN, HD), jnp.bfloat16),
        grid_spec=pltpu.PrefetchScalarGridSpec(
            num_scalar_prefetch=2,
            grid=(SET // TILE,),
            in_specs=[pl.BlockSpec((QUAD, 2 * TOK, HD), lambda i, w, f: (i, 0, 0))]
            + [IN_VMEM] * 4,
            out_specs=pl.BlockSpec((QUAD, RETURN, HD), lambda i, w, f: (i, 0, 0)),
            scratch_shapes=[
                pltpu.VMEM((TILE, KEYS), jnp.float32),
                pltpu.VMEM((TILE, 128), jnp.float32),
                pltpu.VMEM((TILE, 2 * HD), jnp.float32),
            ],
        ),
        compiler_params=pltpu.CompilerParams(vmem_limit_bytes=24 * MIB),
        cost_estimate=pl.CostEstimate(
            flops=4 * SET * 4992 * HD, bytes_accessed=4_000_000, transcendentals=SET * 4992
        ),
        name="attend",
    )(where, flag, queries, *(in_vmem(x) for x in (keys, values, last_keys, last_values)))


def output_kernel(place_ref, back_ref, w_ref, *refs):
    out_refs, attn_ref = refs[:HEAD_AXIS], refs[HEAD_AXIS]
    for p in range(RING):
        b, hd = divmod(p, HEADS_HERE)
        attn_ref[b * TOK : (b + 1) * TOK, hd * HD : (hd + 1) * HD] = back_ref[p, 0:TOK, :]
    levels = []
    for p in range(RING):
        stats = back_ref[p, 2 * TOK : RETURN, :].astype(jnp.float32)
        row = stats[0:1] + stats[1:2] + stats[2:3]
        levels.append(jnp.transpose(jnp.broadcast_to(row, (TOK, HD))))
    top = levels[0]
    for level in levels[1:]:
        top = jnp.maximum(top, level)
    total = jnp.zeros((TOK, HD), jnp.float32)
    mixed = jnp.zeros((TOK, HD), jnp.float32)
    for p, level in enumerate(levels):
        weight = jnp.exp2(level - top)
        total += weight
        mixed += weight * back_ref[p, TOK : 2 * TOK, :].astype(jnp.float32)
    attn_ref[(BRANCH - 1) * TOK :, (HEADS_HERE - 1) * HD :] = (mixed / total).astype(jnp.bfloat16)
    for s in range(HEAD_AXIS):
        start = pl.multiple_of(place_ref[s] * DSH, DSH)
        out_refs[s][...] = jnp.dot(
            attn_ref[...], w_ref[:, pl.ds(start, DSH)], preferred_element_type=jnp.float32
        ).astype(jnp.bfloat16)


def output(places, back, w_out):
    return pl.pallas_call(
        output_kernel,
        out_shape=tuple(
            jax.ShapeDtypeStruct((ROWS, DSH), jnp.bfloat16) for _ in range(HEAD_AXIS)
        ),
        grid_spec=pltpu.PrefetchScalarGridSpec(
            num_scalar_prefetch=1,
            grid=(1,),
            in_specs=[
                whole((RING, RETURN, HD)),
                IN_VMEM,
            ],
            out_specs=tuple(whole((ROWS, DSH)) for _ in range(HEAD_AXIS)),
            scratch_shapes=[pltpu.VMEM((ROWS, DSH), jnp.bfloat16)],
        ),
        compiler_params=pltpu.CompilerParams(vmem_limit_bytes=24 * MIB),
        cost_estimate=pl.CostEstimate(
            flops=2 * ROWS * DSH * DSH * HEAD_AXIS, bytes_accessed=5_000_000, transcendentals=0
        ),
        name="output",
    )(places, back, in_vmem(w_out))


def head_move(x, step):
    return lax.ppermute(x, "head", [(i, (i + step) % HEAD_AXIS) for i in range(HEAD_AXIS)])


def head_partner(x):
    return lax.ppermute(x, "head", [(i, i ^ 1) for i in range(HEAD_AXIS)])


def frame_move(x, flip):
    return lax.ppermute(x, "frame", [(i, i ^ flip) for i in range(FRAMES)])


def gather_head(own):
    partner = head_partner(own)
    opposite = head_move(own, 4)
    ahead = head_move(own, -2)
    behind = head_move(own, 2)
    return [
        own,
        partner,
        ahead,
        behind,
        head_move(partner, -2),
        head_move(partner, 2),
        opposite,
        head_partner(opposite),
    ]


def add(*terms):
    total = terms[0].astype(jnp.float32)
    for term in terms[1:]:
        total += term.astype(jnp.float32)
    return total


def scatter_head(parts):
    for_opposite = head_partner(parts[7])
    for_partner = [head_move(parts[4], 2), head_move(parts[5], -2)]
    direct = [head_move(parts[2], 2), head_move(parts[3], -2)]
    over_y = head_partner(add(parts[1], *for_partner).astype(jnp.bfloat16))
    across = head_move(add(parts[6], for_opposite).astype(jnp.bfloat16), 4)
    return add(parts[0], *direct, over_y, across)


def body(
    video, w_qkv, w_out, text_kv, text_lengths, norm_gains, mod_table, timestep_ids, queue_shift
):
    text_kv = in_hbm(text_kv)
    frame = lax.axis_index("frame").astype(jnp.int32)
    head = lax.axis_index("head").astype(jnp.int32)
    own, gate, places, where = prep(
        frame.reshape(1),
        head.reshape(1),
        queue_shift,
        in_hbm(timestep_ids),
        in_hbm(text_lengths),
        in_hbm(video),
        in_hbm(mod_table.transpose(1, 0, 2)),
    )
    cosine, sine = rope_tables(frame)
    blocks = gather_head(own)
    weights = in_hbm(w_qkv.transpose(1, 0, 2))
    gains = in_hbm(norm_gains)
    send_keys, send_queries, last = project(places, blocks, weights, gains, cosine, sine)
    rings = [[(y * RING + z) * 2 + core for z in range(RING)] for y in range(2) for core in range(2)]

    def over_rings(x):
        return lax.all_to_all(x, "frame", 0, 0, axis_index_groups=rings, tiled=True)

    near = over_rings(send_keys)
    lasts = [last] + [frame_move(last, flip) for flip in (1, FRAMES // 2, FRAMES // 2 + 1)]
    last_keys, last_values = lay_last(where, lasts, text_kv)
    send_queries, near = lax.optimization_barrier((send_queries, near))
    over_y = frame_move(near, FRAMES // 2)
    sets = [near, over_y, frame_move(near, 1), frame_move(over_y, 1)]
    queries = over_rings(send_queries)
    keys, values, w_held, flag = lay(where, sets, text_kv, gains, w_out)
    returned = attend(where, flag, queries, keys, values, last_keys, last_values)
    partial = output(places, over_rings(returned), w_held)
    proj = scatter_head(partial).reshape(video.shape)
    return (video.astype(jnp.float32) + gate * proj).astype(jnp.bfloat16)


def solution(mesh):
    in_specs = (
        P(None, "frame", "head"),
        P(None, None, "head"),
        P("head", None),
        P(None, None, None, "head"),
        P(),
        P(),
        P(None, None, "head"),
        P(),
        P(),
    )
    out_specs = P(None, "frame", "head")
    return jax.shard_map(body, mesh=mesh, in_specs=in_specs, out_specs=out_specs, check_vma=False)
```

```python
import jax
import jax.numpy as jnp
import numpy as np
from jax import lax
from jax.experimental import pallas as pl
from jax.experimental.pallas import tpu as pltpu
from jax.sharding import PartitionSpec as P

HD = 128
TOK = 128
LAT_W = 16
FRAMES = 32
HEAD_AXIS = 8
BRANCH = 3
HEADS_HERE = 3
PAIRS = BRANCH * HEADS_HERE
DSH = 384
TXT = 256
RING = 8
ROWS = BRANCH * TOK
MOD_ROWS = 16
SENT = ROWS + MOD_ROWS
LAST = PAIRS - 1
STAT_ROWS = 16
LAST_ROWS = TOK + STAT_ROWS
RETURN = TOK + LAST_ROWS
WIDE = 3 * DSH
rope_base = 256.0
norm_eps = 1e-06
LOG2E = float(np.log2(np.e))
EXP_SCALE = float(HD ** (-0.5) * np.log2(np.e))
MIB = 1024 * 1024


def whole(shape):
    return pl.BlockSpec(shape, lambda *_: (0,) * len(shape))


def limbs_of(value):
    limbs = []
    for _ in range(3):
        limb = value.astype(jnp.bfloat16).astype(jnp.float32)
        limbs.append(limb)
        value = value - limb
    return limbs


def rope_tables(frame):
    time_dims = HD // 8
    space_dims = (HD - time_dims) // 2
    freq = np.concatenate(
        [
            np.repeat(rope_base ** (-np.arange(0, z, 2, dtype=np.float64) / z), 2)
            for z in (time_dims, space_dims, space_dims)
        ]
    ).astype(np.float32)
    section = np.repeat(np.arange(3), (time_dims, space_dims, space_dims))
    token = jnp.arange(TOK, dtype=jnp.int32)[:, None]
    section = jnp.asarray(section)[None, :]
    position = jnp.where(
        section == 0, frame, jnp.where(section == 1, token // LAT_W, token % LAT_W)
    )
    angle = position.astype(jnp.float32) * jnp.asarray(freq)[None, :]
    sign = jnp.asarray(np.tile(np.array([-1.0, 1.0], np.float32), HD // 2))
    return jnp.cos(angle), jnp.sin(angle) * sign[None, :]


def prep_kernel(
    frame_ref, head_ref, shift_ref, ids_ref, lengths_ref, video_ref, table_ref,
    own_ref, gate_ref, place_ref, where_ref,
):
    head = head_ref[0]
    for s, step in enumerate((0, 0, 2, -2, 2, -2, 4, 4)):
        near = lax.rem(head + step + HEAD_AXIS, HEAD_AXIS)
        place_ref[s] = near if s in (0, 2, 3, 6) else near + 1 - 2 * lax.rem(near, 2)
    slab = lax.rem(lax.div(frame_ref[0], 2), RING)
    branch = lax.div(slab, HEADS_HERE)
    text_block = jnp.minimum(slab, 1)
    where_ref[0] = branch
    where_ref[1] = lax.rem(slab, HEADS_HERE)
    where_ref[2] = lengths_ref[branch]
    where_ref[3] = jnp.where(slab < 2, lengths_ref[BRANCH - 1] - 128 * text_block, 0)
    where_ref[4] = text_block
    level = ids_ref[lax.rem(frame_ref[0] + shift_ref[0], FRAMES)]
    looked = [table_ref[part, pl.ds(level, 1), :] for part in range(3)]
    gate_ref[...] = looked[2]
    limbs = limbs_of(looked[0]) + limbs_of(looked[1])
    limbs.append(jnp.zeros((MOD_ROWS - 6, DSH), jnp.float32))
    for b in range(BRANCH):
        own_ref[b * TOK : (b + 1) * TOK, :] = video_ref[b]
    own_ref[ROWS:SENT, :] = jnp.concatenate(limbs, axis=0).astype(jnp.bfloat16)


def prep(frame, head, queue_shift, timestep_ids, lengths, video, table):
    return pl.pallas_call(
        prep_kernel,
        out_shape=(
            jax.ShapeDtypeStruct((SENT, DSH), jnp.bfloat16),
            jax.ShapeDtypeStruct((1, DSH), jnp.float32),
            jax.ShapeDtypeStruct((HEAD_AXIS,), jnp.int32),
            jax.ShapeDtypeStruct((5,), jnp.int32),
        ),
        grid_spec=pltpu.PrefetchScalarGridSpec(
            num_scalar_prefetch=5,
            grid=(1,),
            in_specs=[whole((BRANCH, TOK, DSH)), whole((3, FRAMES, DSH))],
            out_specs=(
                whole((SENT, DSH)),
                whole((1, DSH)),
                pl.BlockSpec(memory_space=pltpu.SMEM),
                pl.BlockSpec(memory_space=pltpu.SMEM),
            ),
        ),
        compiler_params=pltpu.CompilerParams(vmem_limit_bytes=16 * MIB),
        name="prep",
    )(frame, head, queue_shift, timestep_ids, lengths, video, table)


def project_kernel(place_ref, *refs):
    blocks = refs[:HEAD_AXIS]
    (
        w_hbm, gain_ref, cos_ref, sin_ref, kv_ref, q_ref, last_ref, mod_ref, acc_ref, w_ref, sems,
    ) = refs[HEAD_AXIS:]
    copies = [
        pltpu.make_async_copy(w_hbm.at[n], w_ref.at[:, pl.ds(n * DSH, DSH)], sems.at[n])
        for n in range(3)
    ]
    for copy in copies:
        copy.start()
    step = 64

    def chunk(n, carry):
        here = pl.ds(pl.multiple_of(n * step, step), step)
        total = jnp.zeros((step, 128), jnp.float32)
        square = jnp.zeros((step, 128), jnp.float32)
        for block in blocks:
            for lane in range(0, DSH, 128):
                x = block[here, lane : lane + 128].astype(jnp.float32)
                total += x
                square += x * x
        mean = jnp.sum(total, axis=1, keepdims=True) / (HEAD_AXIS * DSH)
        var = jnp.sum(square, axis=1, keepdims=True) / (HEAD_AXIS * DSH) - mean * mean
        inv = lax.rsqrt(var + norm_eps)
        for s, block in enumerate(blocks):
            limbs = block[ROWS:SENT, :].astype(jnp.float32)
            shift = limbs[0:1] + limbs[1:2] + limbs[2:3]
            scale = limbs[3:4] + limbs[4:5] + limbs[5:6]
            x = block[here, :].astype(jnp.float32)
            y = (x - mean) * inv * (1.0 + scale) + shift
            start = pl.multiple_of(place_ref[s] * DSH, DSH)
            mod_ref[here, pl.ds(start, DSH)] = y.astype(jnp.bfloat16)
        return carry

    lax.fori_loop(0, ROWS // step, chunk, 0)

    def piece(part, p):
        b, hd = divmod(p, HEADS_HERE)
        lane = part * DSH + hd * HD
        return acc_ref[b * TOK : (b + 1) * TOK, lane : lane + HD]

    def turned(part, p):
        t = piece(part, p)
        t = t * lax.rsqrt(jnp.mean(t * t, axis=1, keepdims=True) + norm_eps)
        t = t * gain_ref[part : part + 1, :]
        even = lax.broadcasted_iota(jnp.int32, t.shape, 1) % 2 == 0
        other = jnp.where(even, pltpu.roll(t, HD - 1, 1), pltpu.roll(t, 1, 1))
        return t * cos_ref[...] + other * sin_ref[...]

    for copy in copies:
        copy.wait()
    acc_ref[...] = jnp.dot(mod_ref[...], w_ref[...], preferred_element_type=jnp.float32)
    for part in range(3):
        for p in range(PAIRS):
            if part == 2:
                result = piece(part, p)
            else:
                result = turned(part, p)
            if part == 1:
                result = jnp.transpose(result)
            result = result.astype(jnp.bfloat16)
            if part == 0 and p == LAST:
                for n in range(RING):
                    q_ref[n, TOK : 2 * TOK, :] = result
            elif part == 0:
                q_ref[p, 0:TOK, :] = result
            elif p == LAST:
                last_ref[(part - 1) * TOK : part * TOK, :] = result
            else:
                kv_ref[p, (part - 1) * TOK : part * TOK, :] = result


def project(places, blocks, w, gains, cosine, sine):
    return pl.pallas_call(
        project_kernel,
        out_shape=(
            jax.ShapeDtypeStruct((RING, 2 * TOK, HD), jnp.bfloat16),
            jax.ShapeDtypeStruct((RING, 2 * TOK, HD), jnp.bfloat16),
            jax.ShapeDtypeStruct((2 * TOK, HD), jnp.bfloat16),
        ),
        grid_spec=pltpu.PrefetchScalarGridSpec(
            num_scalar_prefetch=1,
            grid=(1,),
            in_specs=[whole((SENT, DSH)) for _ in blocks]
            + [
                pl.BlockSpec(memory_space=pltpu.HBM),
                whole((2, HD)),
                whole((TOK, HD)),
                whole((TOK, HD)),
            ],
            out_specs=(
                whole((RING, 2 * TOK, HD)),
                whole((RING, 2 * TOK, HD)),
                whole((2 * TOK, HD)),
            ),
            scratch_shapes=[
                pltpu.VMEM((ROWS, HEAD_AXIS * DSH), jnp.bfloat16),
                pltpu.VMEM((ROWS, WIDE), jnp.float32),
                pltpu.VMEM((HEAD_AXIS * DSH, WIDE), jnp.bfloat16),
                pltpu.SemaphoreType.DMA((3,)),
            ],
        ),
        compiler_params=pltpu.CompilerParams(vmem_limit_bytes=22 * MIB),
        cost_estimate=pl.CostEstimate(
            flops=2 * ROWS * HEAD_AXIS * DSH * 3 * DSH, bytes_accessed=12_000_000, transcendentals=0
        ),
        name="project",
    )(places, *blocks, w, gains, cosine, sine)


QUAD = 4
TILE = QUAD * TOK
SET = RING * TOK
KEYS = QUAD * SET + TXT
CHUNK = 1024


def attend_rows(flag_ref, q, keys_ref, value_ref, valid, score_ref, top_ref, mixed_ref):
    count = keys_ref.shape[1]
    text = TXT if count == KEYS else TXT // 2

    def scores_of(first, stop):
        scores = jnp.dot(q, keys_ref[:, first:stop], preferred_element_type=jnp.float32)
        if first == count - text:
            index = lax.broadcasted_iota(jnp.int32, scores.shape, 1)
            scores = jnp.where(index < valid, scores, -jnp.inf)
        return scores

    cuts = list(range(0, count - text, CHUNK)) + [count - text, count]
    pieces = list(zip(cuts[:-1], cuts[1:]))

    @pl.when(flag_ref[0] == 1)
    def _():
        mixed = jnp.zeros((TILE, 2 * HD), jnp.float32)
        for first, stop in pieces:
            weights = jnp.exp2(scores_of(first, stop) * EXP_SCALE).astype(jnp.bfloat16)
            mixed += jnp.dot(weights, value_ref[first:stop, :], preferred_element_type=jnp.float32)
        mixed_ref[...] = mixed
        top_ref[...] = jnp.zeros((TILE, 128), jnp.float32)

    @pl.when(flag_ref[0] != 1)
    def _():
        top = jnp.full((TILE, 128), -jnp.inf, jnp.float32)
        for first, stop in pieces:
            scores = scores_of(first, stop)
            score_ref[:, first:stop] = scores
            for lane in range(0, stop - first, 128):
                top = jnp.maximum(top, scores[:, lane : lane + 128])
        top = jnp.max(top, axis=1, keepdims=True) * EXP_SCALE
        top_ref[...] = jnp.broadcast_to(top, (TILE, 128))
        mixed_ref[...] = jnp.zeros((TILE, 2 * HD), jnp.float32)
        width = 128

        def step(n, carry):
            here = pl.ds(pl.multiple_of(n * width, width), width)
            weights = jnp.exp2(score_ref[:, here] * EXP_SCALE - top).astype(jnp.bfloat16)
            mixed_ref[...] += jnp.dot(
                weights, value_ref[here, :], preferred_element_type=jnp.float32
            )
            return carry

        lax.fori_loop(0, count // width, step, 0)


def lay_values(value_ref, pieces):
    lane = lax.broadcasted_iota(jnp.int32, (value_ref.shape[0], HD), 1)
    value_ref[:, HD:] = jnp.where(lane == 0, 1.0, 0.0).astype(jnp.bfloat16)
    row = 0
    for piece in pieces:
        value_ref[row : row + piece.shape[0], :HD] = piece
        row += piece.shape[0]


IN_VMEM = pl.BlockSpec(memory_space=pltpu.VMEM)


def in_vmem(x):
    return pltpu.with_memory_space_constraint(x, pltpu.VMEM)


def in_hbm(x):
    return pltpu.with_memory_space_constraint(x, pltpu.HBM)


def turned_text(text_ref):
    return jnp.transpose(text_ref[0, 0].astype(jnp.float32)).astype(jnp.bfloat16)


def lay_kernel(where_ref, *refs):
    set_refs = refs[:QUAD]
    text_ref, last_text_ref, gain_ref, w_hbm, keys_ref, value_ref, w_ref, flag_ref, sem = refs[QUAD:]
    copy = pltpu.make_async_copy(w_hbm, w_ref, sem)
    copy.start()
    for n, ref in enumerate(set_refs):
        for f in range(RING):
            keys_ref[:, n * SET + f * TOK : n * SET + (f + 1) * TOK] = ref[f, 0:TOK, :]
    keys_ref[:, QUAD * SET :] = turned_text(text_ref)
    lay_values(
        value_ref,
        [ref[:, TOK : 2 * TOK, :].reshape(SET, HD) for ref in set_refs] + [text_ref[1, 0]],
    )
    slack = 1.03 * HD
    gains = gain_ref[...] * gain_ref[...]
    query_norm = slack * jnp.max(gains[0:1])
    key_norm = slack * jnp.max(gains[1:2])
    for ref in (text_ref, last_text_ref):
        text = ref[0, 0].astype(jnp.float32)
        key_norm = jnp.maximum(key_norm, jnp.max(jnp.sum(text * text, axis=1)))
    bound = EXP_SCALE * EXP_SCALE * query_norm * key_norm
    flag_ref[0] = jnp.where(bound < MOST_LOG2 * MOST_LOG2, 1, 0)
    copy.wait()


MOST_LOG2 = 90.0


def lay(where, sets, text_kv, gains, w_out):
    return pl.pallas_call(
        lay_kernel,
        out_shape=(
            pltpu.VMEM((HD, KEYS), jnp.bfloat16),
            pltpu.VMEM((KEYS, 2 * HD), jnp.bfloat16),
            pltpu.VMEM(w_out.shape, w_out.dtype),
            jax.ShapeDtypeStruct((1,), jnp.int32),
        ),
        grid_spec=pltpu.PrefetchScalarGridSpec(
            num_scalar_prefetch=1,
            grid=(1,),
            in_specs=[whole((RING, 2 * TOK, HD)) for _ in sets]
            + [
                pl.BlockSpec((2, 1, TXT, HD), lambda i, w: (0, w[0], 0, w[1])),
                pl.BlockSpec(
                    (1, 1, TXT, HD), lambda i, w: (0, BRANCH - 1, 0, HEADS_HERE - 1)
                ),
                whole((2, HD)),
                pl.BlockSpec(memory_space=pltpu.HBM),
            ],
            out_specs=(IN_VMEM, IN_VMEM, IN_VMEM, pl.BlockSpec(memory_space=pltpu.SMEM)),
            scratch_shapes=[pltpu.SemaphoreType.DMA(())],
        ),
        compiler_params=pltpu.CompilerParams(vmem_limit_bytes=8 * MIB),
        cost_estimate=pl.CostEstimate(
            flops=5_000_000_000, bytes_accessed=10_000_000, transcendentals=0
        ),
        name="lay",
    )(where, *sets, text_kv, text_kv, gains, in_hbm(w_out))


LAST_KEYS = QUAD * TOK + TXT // 2


def lay_last_kernel(where_ref, *refs):
    last_refs = refs[:QUAD]
    text_ref, keys_ref, value_ref = refs[QUAD:]
    for n, ref in enumerate(last_refs):
        keys_ref[:, n * TOK : (n + 1) * TOK] = ref[0:TOK, :]
    keys_ref[:, QUAD * TOK :] = turned_text(text_ref)
    lay_values(value_ref, [ref[TOK : 2 * TOK, :] for ref in last_refs] + [text_ref[1, 0]])


def lay_last(where, lasts, text_kv):
    return pl.pallas_call(
        lay_last_kernel,
        out_shape=(
            pltpu.VMEM((HD, LAST_KEYS), jnp.bfloat16),
            pltpu.VMEM((LAST_KEYS, 2 * HD), jnp.bfloat16),
        ),
        grid_spec=pltpu.PrefetchScalarGridSpec(
            num_scalar_prefetch=1,
            grid=(1,),
            in_specs=[whole((2 * TOK, HD)) for _ in lasts]
            + [
                pl.BlockSpec(
                    (2, 1, TXT // 2, HD), lambda i, w: (0, BRANCH - 1, w[4], HEADS_HERE - 1)
                )
            ],
            out_specs=(IN_VMEM, IN_VMEM),
        ),
        compiler_params=pltpu.CompilerParams(vmem_limit_bytes=4 * MIB),
        cost_estimate=pl.CostEstimate(
            flops=10_000_000_000, bytes_accessed=10_000_000, transcendentals=0
        ),
        name="lay_last",
    )(where, *lasts, text_kv)


def attend_kernel(
    where_ref, flag_ref, q_ref, keys_ref, value_ref, last_keys_ref, last_value_ref,
    out_ref, score_ref, top_ref, mixed_ref,
):
    q = q_ref[:, 0:TOK, :].reshape(TILE, HD)
    attend_rows(
        flag_ref, q, keys_ref, value_ref, where_ref[2], score_ref, top_ref, mixed_ref
    )
    result = mixed_ref[:, :HD] / mixed_ref[:, HD : HD + 1]
    out_ref[:, 0:TOK, :] = result.astype(jnp.bfloat16).reshape(QUAD, TOK, HD)
    q = q_ref[:, TOK : 2 * TOK, :].reshape(TILE, HD)
    attend_rows(
        flag_ref, q, last_keys_ref, last_value_ref, where_ref[3], score_ref, top_ref, mixed_ref
    )
    total = mixed_ref[:, HD : HD + 1]
    result = mixed_ref[:, :HD] / total
    out_ref[:, TOK : 2 * TOK, :] = result.astype(jnp.bfloat16).reshape(QUAD, TOK, HD)
    level = top_ref[...] + jnp.log(total) * LOG2E
    for f in range(QUAD):
        row = jnp.transpose(level[f * TOK : (f + 1) * TOK])[0:1]
        stats = limbs_of(row) + [jnp.zeros((STAT_ROWS - 3, HD), jnp.float32)]
        out_ref[f, 2 * TOK : RETURN, :] = jnp.concatenate(stats, axis=0).astype(jnp.bfloat16)


def attend(where, flag, queries, keys, values, last_keys, last_values):
    return pl.pallas_call(
        attend_kernel,
        out_shape=jax.ShapeDtypeStruct((RING, RETURN, HD), jnp.bfloat16),
        grid_spec=pltpu.PrefetchScalarGridSpec(
            num_scalar_prefetch=2,
            grid=(SET // TILE,),
            in_specs=[pl.BlockSpec((QUAD, 2 * TOK, HD), lambda i, w, f: (i, 0, 0))]
            + [IN_VMEM] * 4,
            out_specs=pl.BlockSpec((QUAD, RETURN, HD), lambda i, w, f: (i, 0, 0)),
            scratch_shapes=[
                pltpu.VMEM((TILE, KEYS), jnp.float32),
                pltpu.VMEM((TILE, 128), jnp.float32),
                pltpu.VMEM((TILE, 2 * HD), jnp.float32),
            ],
        ),
        compiler_params=pltpu.CompilerParams(vmem_limit_bytes=18 * MIB),
        cost_estimate=pl.CostEstimate(
            flops=4 * SET * 4992 * HD, bytes_accessed=4_000_000, transcendentals=SET * 4992
        ),
        name="attend",
    )(where, flag, queries, *(in_vmem(x) for x in (keys, values, last_keys, last_values)))


def output_kernel(place_ref, back_ref, w_ref, *refs):
    out_refs, attn_ref = refs[:HEAD_AXIS], refs[HEAD_AXIS]
    for p in range(RING):
        b, hd = divmod(p, HEADS_HERE)
        attn_ref[b * TOK : (b + 1) * TOK, hd * HD : (hd + 1) * HD] = back_ref[p, 0:TOK, :]
    levels = []
    for p in range(RING):
        stats = back_ref[p, 2 * TOK : RETURN, :].astype(jnp.float32)
        row = stats[0:1] + stats[1:2] + stats[2:3]
        levels.append(jnp.transpose(jnp.broadcast_to(row, (TOK, HD))))
    top = levels[0]
    for level in levels[1:]:
        top = jnp.maximum(top, level)
    total = jnp.zeros((TOK, HD), jnp.float32)
    mixed = jnp.zeros((TOK, HD), jnp.float32)
    for p, level in enumerate(levels):
        weight = jnp.exp2(level - top)
        total += weight
        mixed += weight * back_ref[p, TOK : 2 * TOK, :].astype(jnp.float32)
    attn_ref[(BRANCH - 1) * TOK :, (HEADS_HERE - 1) * HD :] = (mixed / total).astype(jnp.bfloat16)
    for s in range(HEAD_AXIS):
        start = pl.multiple_of(place_ref[s] * DSH, DSH)
        out_refs[s][...] = jnp.dot(
            attn_ref[...], w_ref[:, pl.ds(start, DSH)], preferred_element_type=jnp.float32
        ).astype(jnp.bfloat16)


def output(places, back, w_out):
    return pl.pallas_call(
        output_kernel,
        out_shape=tuple(
            jax.ShapeDtypeStruct((ROWS, DSH), jnp.bfloat16) for _ in range(HEAD_AXIS)
        ),
        grid_spec=pltpu.PrefetchScalarGridSpec(
            num_scalar_prefetch=1,
            grid=(1,),
            in_specs=[
                whole((RING, RETURN, HD)),
                IN_VMEM,
            ],
            out_specs=tuple(whole((ROWS, DSH)) for _ in range(HEAD_AXIS)),
            scratch_shapes=[pltpu.VMEM((ROWS, DSH), jnp.bfloat16)],
        ),
        compiler_params=pltpu.CompilerParams(vmem_limit_bytes=24 * MIB),
        cost_estimate=pl.CostEstimate(
            flops=2 * ROWS * DSH * DSH * HEAD_AXIS, bytes_accessed=5_000_000, transcendentals=0
        ),
        name="output",
    )(places, back, in_vmem(w_out))


def head_move(x, step):
    return lax.ppermute(x, "head", [(i, (i + step) % HEAD_AXIS) for i in range(HEAD_AXIS)])


def head_partner(x):
    return lax.ppermute(x, "head", [(i, i ^ 1) for i in range(HEAD_AXIS)])


def frame_move(x, flip):
    return lax.ppermute(x, "frame", [(i, i ^ flip) for i in range(FRAMES)])


def gather_head(own):
    partner = head_partner(own)
    opposite = head_move(own, 4)
    ahead = head_move(own, -2)
    behind = head_move(own, 2)
    return [
        own,
        partner,
        ahead,
        behind,
        head_move(partner, -2),
        head_move(partner, 2),
        opposite,
        head_partner(opposite),
    ]


def add(*terms):
    total = terms[0].astype(jnp.float32)
    for term in terms[1:]:
        total += term.astype(jnp.float32)
    return total


def scatter_head(parts):
    for_opposite = head_partner(parts[7])
    for_partner = [head_move(parts[4], 2), head_move(parts[5], -2)]
    direct = [head_move(parts[2], 2), head_move(parts[3], -2)]
    over_y = head_partner(add(parts[1], *for_partner).astype(jnp.bfloat16))
    across = head_move(add(parts[6], for_opposite).astype(jnp.bfloat16), 4)
    return add(parts[0], *direct, over_y, across)


def body(
    video, w_qkv, w_out, text_kv, text_lengths, norm_gains, mod_table, timestep_ids, queue_shift
):
    text_kv = in_hbm(text_kv)
    frame = lax.axis_index("frame").astype(jnp.int32)
    head = lax.axis_index("head").astype(jnp.int32)
    own, gate, places, where = prep(
        frame.reshape(1),
        head.reshape(1),
        queue_shift,
        in_hbm(timestep_ids),
        in_hbm(text_lengths),
        in_hbm(video),
        in_hbm(mod_table.transpose(1, 0, 2)),
    )
    cosine, sine = rope_tables(frame)
    blocks = gather_head(own)
    weights = in_hbm(w_qkv.transpose(1, 0, 2))
    gains = in_hbm(norm_gains)
    send_keys, send_queries, last = project(places, blocks, weights, gains, cosine, sine)
    rings = [[(y * RING + z) * 2 + core for z in range(RING)] for y in range(2) for core in range(2)]

    def over_rings(x):
        return lax.all_to_all(x, "frame", 0, 0, axis_index_groups=rings, tiled=True)

    near = over_rings(send_keys)
    lasts = [last] + [frame_move(last, flip) for flip in (1, FRAMES // 2, FRAMES // 2 + 1)]
    send_queries, near, *lasts = lax.optimization_barrier((send_queries, near, *lasts))
    last_keys, last_values = lay_last(where, lasts, text_kv)
    over_y = frame_move(near, FRAMES // 2)
    sets = [near, over_y, frame_move(near, 1), frame_move(over_y, 1)]
    queries = over_rings(send_queries)
    keys, values, w_held, flag = lay(where, sets, text_kv, gains, w_out)
    returned = attend(where, flag, queries, keys, values, last_keys, last_values)
    partial = output(places, over_rings(returned), w_held)
    proj = scatter_head(partial).reshape(video.shape)
    return (video.astype(jnp.float32) + gate * proj).astype(jnp.bfloat16)


def solution(mesh):
    in_specs = (
        P(None, "frame", "head"),
        P(None, None, "head"),
        P("head", None),
        P(None, None, None, "head"),
        P(),
        P(),
        P(None, None, "head"),
        P(),
        P(),
    )
    out_specs = P(None, "frame", "head")
    return jax.shard_map(body, mesh=mesh, in_specs=in_specs, out_specs=out_specs, check_vma=False)
```

```python
import jax
import jax.numpy as jnp
import numpy as np
from jax import lax
from jax.experimental import pallas as pl
from jax.experimental.pallas import tpu as pltpu
from jax.sharding import PartitionSpec as P

HD = 128
TOK = 128
LAT_W = 16
FRAMES = 32
HEAD_AXIS = 8
BRANCH = 3
HEADS_HERE = 3
PAIRS = BRANCH * HEADS_HERE
DSH = 384
TXT = 256
RING = 8
ROWS = BRANCH * TOK
MOD_ROWS = 16
SENT = ROWS + MOD_ROWS
LAST = PAIRS - 1
STAT_ROWS = 16
LAST_ROWS = TOK + STAT_ROWS
RETURN = TOK + LAST_ROWS
WIDE = 3 * DSH
rope_base = 256.0
norm_eps = 1e-06
LOG2E = float(np.log2(np.e))
EXP_SCALE = float(HD ** (-0.5) * np.log2(np.e))
MIB = 1024 * 1024


def whole(shape):
    return pl.BlockSpec(shape, lambda *_: (0,) * len(shape))


IN_VMEM = pl.BlockSpec(memory_space=pltpu.VMEM)


def in_vmem(x):
    return pltpu.with_memory_space_constraint(x, pltpu.VMEM)


def in_hbm(x):
    return pltpu.with_memory_space_constraint(x, pltpu.HBM)


def limbs_of(value):
    limbs = []
    for _ in range(3):
        limb = value.astype(jnp.bfloat16).astype(jnp.float32)
        limbs.append(limb)
        value = value - limb
    return limbs


def rope_tables(frame):
    time_dims = HD // 8
    space_dims = (HD - time_dims) // 2
    freq = np.concatenate(
        [
            np.repeat(rope_base ** (-np.arange(0, z, 2, dtype=np.float64) / z), 2)
            for z in (time_dims, space_dims, space_dims)
        ]
    ).astype(np.float32)
    section = np.repeat(np.arange(3), (time_dims, space_dims, space_dims))
    token = jnp.arange(TOK, dtype=jnp.int32)[:, None]
    section = jnp.asarray(section)[None, :]
    position = jnp.where(
        section == 0, frame, jnp.where(section == 1, token // LAT_W, token % LAT_W)
    )
    angle = position.astype(jnp.float32) * jnp.asarray(freq)[None, :]
    sign = jnp.asarray(np.tile(np.array([-1.0, 1.0], np.float32), HD // 2))
    return jnp.cos(angle), jnp.sin(angle) * sign[None, :]


def prep_kernel(
    frame_ref, head_ref, shift_ref, ids_ref, lengths_ref, video_ref, table_ref, gain_ref,
    own_ref, gate_ref, gain_out_ref, place_ref, where_ref,
):
    head = head_ref[0]
    for s, step in enumerate((0, 0, 2, -2, 2, -2, 4, 4)):
        near = lax.rem(head + step + HEAD_AXIS, HEAD_AXIS)
        place_ref[s] = near if s in (0, 2, 3, 6) else near + 1 - 2 * lax.rem(near, 2)
    slab = lax.rem(lax.div(frame_ref[0], 2), RING)
    branch = lax.div(slab, HEADS_HERE)
    text_block = jnp.minimum(slab, 1)
    where_ref[0] = branch
    where_ref[1] = lax.rem(slab, HEADS_HERE)
    where_ref[2] = lengths_ref[branch]
    where_ref[3] = jnp.where(slab < 2, lengths_ref[BRANCH - 1] - 128 * text_block, 0)
    where_ref[4] = text_block
    level = ids_ref[lax.rem(frame_ref[0] + shift_ref[0], FRAMES)]
    looked = [table_ref[part, pl.ds(level, 1), :] for part in range(3)]
    gate_ref[...] = looked[2]
    gain_out_ref[...] = gain_ref[...]
    limbs = limbs_of(looked[0]) + limbs_of(looked[1])
    limbs.append(jnp.zeros((MOD_ROWS - 6, DSH), jnp.float32))
    for b in range(BRANCH):
        own_ref[b * TOK : (b + 1) * TOK, :] = video_ref[b]
    own_ref[ROWS:SENT, :] = jnp.concatenate(limbs, axis=0).astype(jnp.bfloat16)


def prep(frame, head, queue_shift, timestep_ids, lengths, video, table, gains):
    return pl.pallas_call(
        prep_kernel,
        out_shape=(
            pltpu.VMEM((SENT, DSH), jnp.bfloat16),
            jax.ShapeDtypeStruct((1, DSH), jnp.float32),
            pltpu.VMEM((2, HD), jnp.float32),
            jax.ShapeDtypeStruct((HEAD_AXIS,), jnp.int32),
            jax.ShapeDtypeStruct((5,), jnp.int32),
        ),
        grid_spec=pltpu.PrefetchScalarGridSpec(
            num_scalar_prefetch=5,
            grid=(1,),
            in_specs=[whole((BRANCH, TOK, DSH)), whole((3, FRAMES, DSH)), whole((2, HD))],
            out_specs=(
                IN_VMEM,
                whole((1, DSH)),
                IN_VMEM,
                pl.BlockSpec(memory_space=pltpu.SMEM),
                pl.BlockSpec(memory_space=pltpu.SMEM),
            ),
        ),
        compiler_params=pltpu.CompilerParams(vmem_limit_bytes=16 * MIB),
        name="prep",
    )(frame, head, queue_shift, timestep_ids, lengths, video, table, gains)


def project_kernel(place_ref, *refs):
    blocks = refs[:HEAD_AXIS]
    (
        w_hbm, gain_ref, cos_ref, sin_ref, out_ref, last_ref, mod_ref, acc_ref, w_ref, sems,
    ) = refs[HEAD_AXIS:]
    copies = [
        pltpu.make_async_copy(w_hbm.at[n], w_ref.at[:, pl.ds(n * DSH, DSH)], sems.at[n])
        for n in range(3)
    ]
    for copy in copies:
        copy.start()
    step = 64

    def chunk(n, carry):
        here = pl.ds(pl.multiple_of(n * step, step), step)
        total = jnp.zeros((step, 128), jnp.float32)
        square = jnp.zeros((step, 128), jnp.float32)
        for block in blocks:
            for lane in range(0, DSH, 128):
                x = block[here, lane : lane + 128].astype(jnp.float32)
                total += x
                square += x * x
        mean = jnp.sum(total, axis=1, keepdims=True) / (HEAD_AXIS * DSH)
        var = jnp.sum(square, axis=1, keepdims=True) / (HEAD_AXIS * DSH) - mean * mean
        inv = lax.rsqrt(var + norm_eps)
        for s, block in enumerate(blocks):
            limbs = block[ROWS:SENT, :].astype(jnp.float32)
            shift = limbs[0:1] + limbs[1:2] + limbs[2:3]
            scale = limbs[3:4] + limbs[4:5] + limbs[5:6]
            x = block[here, :].astype(jnp.float32)
            y = (x - mean) * inv * (1.0 + scale) + shift
            start = pl.multiple_of(place_ref[s] * DSH, DSH)
            mod_ref[here, pl.ds(start, DSH)] = y.astype(jnp.bfloat16)
        return carry

    lax.fori_loop(0, ROWS // step, chunk, 0)

    def piece(part, p):
        b, hd = divmod(p, HEADS_HERE)
        lane = part * DSH + hd * HD
        return acc_ref[b * TOK : (b + 1) * TOK, lane : lane + HD]

    def turned(part, p):
        t = piece(part, p)
        t = t * lax.rsqrt(jnp.mean(t * t, axis=1, keepdims=True) + norm_eps)
        t = t * gain_ref[part : part + 1, :]
        even = lax.broadcasted_iota(jnp.int32, t.shape, 1) % 2 == 0
        other = jnp.where(even, pltpu.roll(t, HD - 1, 1), pltpu.roll(t, 1, 1))
        return (t * cos_ref[...] + other * sin_ref[...]).astype(jnp.bfloat16)

    for copy in copies:
        copy.wait()
    acc_ref[...] = jnp.dot(mod_ref[...], w_ref[...], preferred_element_type=jnp.float32)
    for part in range(3):
        for p in range(PAIRS):
            if part == 2:
                result = piece(part, p).astype(jnp.bfloat16)
            else:
                result = turned(part, p)
            if part == 0 and p == LAST:
                for n in range(RING):
                    out_ref[n, 3 * TOK : 4 * TOK, :] = result
            elif part == 0:
                out_ref[p, 2 * TOK : 3 * TOK, :] = result
            elif p == LAST:
                last_ref[(part - 1) * TOK : part * TOK, :] = result
            else:
                out_ref[p, (part - 1) * TOK : part * TOK, :] = result


def project(places, blocks, w, gains, cosine, sine):
    return pl.pallas_call(
        project_kernel,
        out_shape=(
            pltpu.VMEM((RING, 4 * TOK, HD), jnp.bfloat16),
            pltpu.VMEM((2 * TOK, HD), jnp.bfloat16),
        ),
        grid_spec=pltpu.PrefetchScalarGridSpec(
            num_scalar_prefetch=1,
            grid=(1,),
            in_specs=[IN_VMEM] * HEAD_AXIS
            + [pl.BlockSpec(memory_space=pltpu.HBM), IN_VMEM, IN_VMEM, IN_VMEM],
            out_specs=(IN_VMEM, IN_VMEM),
            scratch_shapes=[
                pltpu.VMEM((ROWS, HEAD_AXIS * DSH), jnp.bfloat16),
                pltpu.VMEM((ROWS, WIDE), jnp.float32),
                pltpu.VMEM((HEAD_AXIS * DSH, WIDE), jnp.bfloat16),
                pltpu.SemaphoreType.DMA((3,)),
            ],
        ),
        compiler_params=pltpu.CompilerParams(vmem_limit_bytes=28 * MIB),
        cost_estimate=pl.CostEstimate(
            flops=2 * ROWS * HEAD_AXIS * DSH * 3 * DSH, bytes_accessed=12_000_000, transcendentals=0
        ),
        name="project",
    )(places, *map(in_vmem, blocks), w, *map(in_vmem, (gains, cosine, sine)))


QUAD = 4
TILE = QUAD * TOK
SET = RING * TOK
DIMS = (((1,), (1,)), ((), ()))


def score_keys(q, keys, score_ref, column, top):
    scores = lax.dot_general(q, keys, DIMS, preferred_element_type=jnp.float32)
    score_ref[:, column : column + scores.shape[1]] = scores
    for lane in range(0, scores.shape[1], 128):
        top = jnp.maximum(top, scores[:, lane : lane + 128])
    return top


def score_text(q, keys, valid, score_ref, column, top):
    scores = lax.dot_general(q, keys, DIMS, preferred_element_type=jnp.float32)
    index = lax.broadcasted_iota(jnp.int32, scores.shape, 1)
    scores = jnp.where(index < valid, scores, -jnp.inf)
    score_ref[:, column : column + scores.shape[1]] = scores
    for lane in range(0, scores.shape[1], 128):
        top = jnp.maximum(top, scores[:, lane : lane + 128])
    return top


def mix(score_ref, value_ref, top, count):
    mixed = jnp.zeros((TILE, 2 * HD), jnp.float32)
    for first in range(0, count, SET):
        stop = min(first + SET, count)
        weights = jnp.exp2(score_ref[:, first:stop] * EXP_SCALE - top).astype(jnp.bfloat16)
        mixed += jnp.dot(weights, value_ref[first:stop, :], preferred_element_type=jnp.float32)
    return mixed


def lay_values(value_ref, pieces):
    lane = lax.broadcasted_iota(jnp.int32, (value_ref.shape[0], HD), 1)
    value_ref[:, HD:] = jnp.where(lane == 0, 1.0, 0.0).astype(jnp.bfloat16)
    row = 0
    for piece in pieces:
        value_ref[row : row + piece.shape[0], :HD] = piece
        row += piece.shape[0]


def set_keys(ref):
    return ref[:, 0:TOK, :].reshape(SET, HD)


def set_values(ref):
    return ref[:, TOK : 2 * TOK, :].reshape(SET, HD)


def first_step():
    return pl.program_id(0) == 0


def tile_rows():
    return pl.ds(pl.multiple_of(pl.program_id(0) * TILE, TILE), TILE)


def attend_near_kernel(
    where_ref, q_ref, own_ref, core_ref, text_ref, w_hbm,
    mixed_ref, top_ref, q_out_ref, w_ref, score_ref, value_ref, sem,
):
    copy = pltpu.make_async_copy(w_hbm, w_ref, sem)

    @pl.when(first_step())
    def _():
        copy.start()
        lay_values(value_ref, [set_values(own_ref), set_values(core_ref), text_ref[1, 0]])

    q = q_ref[...].reshape(TILE, HD)
    top = jnp.full((TILE, 128), -jnp.inf, jnp.float32)
    for n, ref in enumerate((own_ref, core_ref)):
        top = score_keys(q, set_keys(ref), score_ref, n * SET, top)
    top = score_text(q, text_ref[0, 0], where_ref[2], score_ref, 2 * SET, top)
    top = jnp.max(top, axis=1, keepdims=True) * EXP_SCALE
    here = tile_rows()
    mixed_ref[here, :] = mix(score_ref, value_ref, top, 2 * SET + TXT)
    top_ref[here, :] = jnp.broadcast_to(top, (TILE, 128))
    q_out_ref[here, :] = q

    @pl.when(pl.program_id(0) == SET // TILE - 1)
    def _():
        copy.wait()


def attend_near(where, received, own, core, text_kv, w_out):
    return pl.pallas_call(
        attend_near_kernel,
        out_shape=(
            pltpu.VMEM((SET, 2 * HD), jnp.float32),
            pltpu.VMEM((SET, 128), jnp.float32),
            pltpu.VMEM((SET, HD), jnp.bfloat16),
            pltpu.VMEM(w_out.shape, w_out.dtype),
        ),
        grid_spec=pltpu.PrefetchScalarGridSpec(
            num_scalar_prefetch=1,
            grid=(SET // TILE,),
            in_specs=[
                pl.BlockSpec((QUAD, TOK, HD), lambda i, w: (i, 2, 0)),
                whole((RING, 2 * TOK, HD)),
                whole((RING, 2 * TOK, HD)),
                pl.BlockSpec((2, 1, TXT, HD), lambda i, w: (0, w[0], 0, w[1])),
                pl.BlockSpec(memory_space=pltpu.HBM),
            ],
            out_specs=(IN_VMEM,) * 4,
            scratch_shapes=[
                pltpu.VMEM((TILE, 2 * SET + TXT), jnp.float32),
                pltpu.VMEM((2 * SET + TXT, 2 * HD), jnp.bfloat16),
                pltpu.SemaphoreType.DMA(()),
            ],
        ),
        compiler_params=pltpu.CompilerParams(vmem_limit_bytes=18 * MIB),
        cost_estimate=pl.CostEstimate(
            flops=4 * SET * 2304 * HD, bytes_accessed=3_000_000, transcendentals=SET * 2304
        ),
        name="attend_near",
    )(where, received, own, core, text_kv, w_out)


LAST_KEYS = QUAD * TOK + 128


def lay_last_kernel(where_ref, *refs):
    last_refs = refs[:QUAD]
    text_ref, keys_ref, value_ref = refs[QUAD:]
    for n, ref in enumerate(last_refs):
        keys_ref[n * TOK : (n + 1) * TOK, :] = ref[0:TOK, :]
    keys_ref[QUAD * TOK :, :] = text_ref[0, 0]
    lay_values(value_ref, [ref[TOK : 2 * TOK, :] for ref in last_refs] + [text_ref[1, 0]])


def lay_last(where, lasts, text_kv):
    return pl.pallas_call(
        lay_last_kernel,
        out_shape=(
            jax.ShapeDtypeStruct((LAST_KEYS, HD), jnp.bfloat16),
            jax.ShapeDtypeStruct((LAST_KEYS, 2 * HD), jnp.bfloat16),
        ),
        grid_spec=pltpu.PrefetchScalarGridSpec(
            num_scalar_prefetch=1,
            grid=(1,),
            in_specs=[whole((2 * TOK, HD)) for _ in lasts]
            + [
                pl.BlockSpec(
                    (2, 1, 128, HD), lambda i, w: (0, BRANCH - 1, w[4], HEADS_HERE - 1)
                )
            ],
            out_specs=(whole((LAST_KEYS, HD)), whole((LAST_KEYS, 2 * HD))),
        ),
        compiler_params=pltpu.CompilerParams(vmem_limit_bytes=16 * MIB),
        cost_estimate=pl.CostEstimate(
            flops=10_000_000_000, bytes_accessed=10_000_000, transcendentals=0
        ),
        name="lay_last",
    )(where, *lasts, text_kv)


def attend_last_kernel(where_ref, q_ref, keys_ref, value_ref, out_ref, score_ref):
    video_keys = QUAD * TOK
    q = q_ref[...].reshape(TILE, HD)
    top = jnp.full((TILE, 128), -jnp.inf, jnp.float32)
    top = score_keys(q, keys_ref[0:video_keys, :], score_ref, 0, top)
    top = score_text(q, keys_ref[video_keys:, :], where_ref[3], score_ref, video_keys, top)
    top = jnp.max(top, axis=1, keepdims=True) * EXP_SCALE
    mixed = mix(score_ref, value_ref, top, LAST_KEYS)
    total = mixed[:, HD : HD + 1]
    result = mixed[:, :HD] / total
    first = pl.program_id(0) * QUAD
    out_ref[pl.ds(first, QUAD), 0:TOK, :] = result.astype(jnp.bfloat16).reshape(QUAD, TOK, HD)
    level = jnp.broadcast_to(top + jnp.log(total) * LOG2E, (TILE, HD))
    for f in range(QUAD):
        row = jnp.transpose(level[f * TOK : (f + 1) * TOK])[0:1]
        stats = limbs_of(row) + [jnp.zeros((STAT_ROWS - 3, HD), jnp.float32)]
        out_ref[first + f, TOK:LAST_ROWS, :] = jnp.concatenate(stats, axis=0).astype(jnp.bfloat16)


def attend_last(where, received, keys, values):
    return pl.pallas_call(
        attend_last_kernel,
        out_shape=pltpu.VMEM((RING, LAST_ROWS, HD), jnp.bfloat16),
        grid_spec=pltpu.PrefetchScalarGridSpec(
            num_scalar_prefetch=1,
            grid=(SET // TILE,),
            in_specs=[
                pl.BlockSpec((QUAD, TOK, HD), lambda i, w: (i, 3, 0)),
                whole((LAST_KEYS, HD)),
                whole((LAST_KEYS, 2 * HD)),
            ],
            out_specs=IN_VMEM,
            scratch_shapes=[pltpu.VMEM((TILE, LAST_KEYS), jnp.float32)],
        ),
        compiler_params=pltpu.CompilerParams(vmem_limit_bytes=16 * MIB),
        cost_estimate=pl.CostEstimate(
            flops=4 * SET * 640 * HD, bytes_accessed=1_000_000, transcendentals=SET * 640
        ),
        name="attend_last",
    )(where, received, keys, values)


def attend_far_kernel(
    q_ref, y_ref, diagonal_ref, last_ref, mixed_ref, top_ref, out_ref, score_ref, value_ref
):
    @pl.when(first_step())
    def _():
        lay_values(value_ref, [set_values(y_ref), set_values(diagonal_ref)])

    here = tile_rows()
    q = q_ref[here, :]
    top = jnp.full((TILE, 128), -jnp.inf, jnp.float32)
    for n, ref in enumerate((y_ref, diagonal_ref)):
        top = score_keys(q, set_keys(ref), score_ref, n * SET, top)
    before = top_ref[here, 0:1]
    top = jnp.maximum(jnp.max(top, axis=1, keepdims=True) * EXP_SCALE, before)
    mixed = mix(score_ref, value_ref, top, 2 * SET) + mixed_ref[here, :] * jnp.exp2(before - top)
    result = mixed[:, :HD] / mixed[:, HD : HD + 1]
    frames = pl.ds(pl.program_id(0) * QUAD, QUAD)
    out_ref[frames, 0:TOK, :] = result.astype(jnp.bfloat16).reshape(QUAD, TOK, HD)
    out_ref[frames, TOK:RETURN, :] = last_ref[frames]


def attend_far(queries, over_y, diagonal, last, mixed, top):
    return pl.pallas_call(
        attend_far_kernel,
        out_shape=pltpu.VMEM((RING, RETURN, HD), jnp.bfloat16),
        grid=(SET // TILE,),
        in_specs=[IN_VMEM] * 6,
        out_specs=IN_VMEM,
        scratch_shapes=[
            pltpu.VMEM((TILE, 2 * SET), jnp.float32),
            pltpu.VMEM((2 * SET, 2 * HD), jnp.bfloat16),
        ],
        compiler_params=pltpu.CompilerParams(vmem_limit_bytes=18 * MIB),
        cost_estimate=pl.CostEstimate(
            flops=4 * SET * 2048 * HD, bytes_accessed=4_000_000, transcendentals=SET * 2048
        ),
        name="attend_far",
    )(*map(in_vmem, (queries, over_y, diagonal, last, mixed, top)))


def output_kernel(place_ref, back_ref, w_ref, *refs):
    out_refs, attn_ref = refs[:HEAD_AXIS], refs[HEAD_AXIS]
    for p in range(RING):
        b, hd = divmod(p, HEADS_HERE)
        attn_ref[b * TOK : (b + 1) * TOK, hd * HD : (hd + 1) * HD] = back_ref[p, 0:TOK, :]
    levels = []
    for p in range(RING):
        stats = back_ref[p, 2 * TOK : RETURN, :].astype(jnp.float32)
        row = stats[0:1] + stats[1:2] + stats[2:3]
        levels.append(jnp.transpose(jnp.broadcast_to(row, (TOK, HD))))
    top = levels[0]
    for level in levels[1:]:
        top = jnp.maximum(top, level)
    total = jnp.zeros((TOK, HD), jnp.float32)
    mixed = jnp.zeros((TOK, HD), jnp.float32)
    for p, level in enumerate(levels):
        weight = jnp.exp2(level - top)
        total += weight
        mixed += weight * back_ref[p, TOK : 2 * TOK, :].astype(jnp.float32)
    attn_ref[(BRANCH - 1) * TOK :, (HEADS_HERE - 1) * HD :] = (mixed / total).astype(jnp.bfloat16)
    for s in range(HEAD_AXIS):
        start = pl.multiple_of(place_ref[s] * DSH, DSH)
        out_refs[s][...] = jnp.dot(
            attn_ref[...], w_ref[:, pl.ds(start, DSH)], preferred_element_type=jnp.float32
        ).astype(jnp.bfloat16)


def output(places, back, w_out):
    return pl.pallas_call(
        output_kernel,
        out_shape=tuple(
            pltpu.VMEM((ROWS, DSH), jnp.bfloat16) for _ in range(HEAD_AXIS)
        ),
        grid_spec=pltpu.PrefetchScalarGridSpec(
            num_scalar_prefetch=1,
            grid=(1,),
            in_specs=[
                IN_VMEM,
                IN_VMEM,
            ],
            out_specs=(IN_VMEM,) * HEAD_AXIS,
            scratch_shapes=[pltpu.VMEM((ROWS, DSH), jnp.bfloat16)],
        ),
        compiler_params=pltpu.CompilerParams(vmem_limit_bytes=24 * MIB),
        cost_estimate=pl.CostEstimate(
            flops=2 * ROWS * DSH * DSH * HEAD_AXIS, bytes_accessed=5_000_000, transcendentals=0
        ),
        name="output",
    )(places, in_vmem(back), in_vmem(w_out))


def head_move(x, step):
    return lax.ppermute(x, "head", [(i, (i + step) % HEAD_AXIS) for i in range(HEAD_AXIS)])


def head_partner(x):
    return lax.ppermute(x, "head", [(i, i ^ 1) for i in range(HEAD_AXIS)])


def frame_move(x, flip):
    return lax.ppermute(x, "frame", [(i, i ^ flip) for i in range(FRAMES)])


def gather_head(own):
    partner = head_partner(own)
    opposite = head_move(own, 4)
    ahead = head_move(own, -2)
    behind = head_move(own, 2)
    return [
        own,
        partner,
        ahead,
        behind,
        head_move(partner, -2),
        head_move(partner, 2),
        opposite,
        head_partner(opposite),
    ]


def add(*terms):
    total = terms[0].astype(jnp.float32)
    for term in terms[1:]:
        total += term.astype(jnp.float32)
    return total


def scatter_head(parts):
    for_opposite = head_partner(parts[7])
    for_partner = [head_move(parts[4], 2), head_move(parts[5], -2)]
    direct = [head_move(parts[2], 2), head_move(parts[3], -2)]
    over_y = head_partner(add(parts[1], *for_partner).astype(jnp.bfloat16))
    across = head_move(add(parts[6], for_opposite).astype(jnp.bfloat16), 4)
    return add(parts[0], *direct, over_y, across)


def body(
    video, w_qkv, w_out, text_kv, text_lengths, norm_gains, mod_table, timestep_ids, queue_shift
):
    text_kv = in_hbm(text_kv)
    frame = lax.axis_index("frame").astype(jnp.int32)
    head = lax.axis_index("head").astype(jnp.int32)
    own, gate, gains, places, where = prep(
        frame.reshape(1),
        head.reshape(1),
        queue_shift,
        in_hbm(timestep_ids),
        in_hbm(text_lengths),
        in_hbm(video),
        in_hbm(mod_table.transpose(1, 0, 2)),
        in_hbm(norm_gains),
    )
    cosine, sine = rope_tables(frame)
    blocks = gather_head(own)
    weights = in_hbm(w_qkv.transpose(1, 0, 2))
    send, last = project(places, blocks, weights, gains, cosine, sine)
    rings = [[(y * RING + z) * 2 + core for z in range(RING)] for y in range(2) for core in range(2)]

    def over_rings(x):
        return lax.all_to_all(x, "frame", 0, 0, axis_index_groups=rings, tiled=True)

    received = over_rings(send)
    flips = (1, FRAMES // 2, FRAMES // 2 + 1)
    lasts = [last] + [frame_move(last, flip) for flip in flips]
    last_keys, last_values = lay_last(where, lasts, text_kv)
    near = received[:, : 2 * TOK]
    over_y = frame_move(near, FRAMES // 2)
    over_core = frame_move(near, 1)
    ninth = attend_last(where, received, last_keys, last_values)
    mixed, top, queries, w_held = attend_near(where, received, near, over_core, text_kv, in_hbm(w_out))
    over_y, _, _ = lax.optimization_barrier((over_y, mixed, ninth))
    diagonal = frame_move(over_y, 1)
    returned = attend_far(queries, over_y, diagonal, ninth, mixed, top)
    partial = output(places, over_rings(returned), w_held)
    proj = scatter_head(partial).reshape(video.shape)
    return (video.astype(jnp.float32) + gate * proj).astype(jnp.bfloat16)


def solution(mesh):
    in_specs = (
        P(None, "frame", "head"),
        P(None, None, "head"),
        P("head", None),
        P(None, None, None, "head"),
        P(),
        P(),
        P(None, None, "head"),
        P(),
        P(),
    )
    out_specs = P(None, "frame", "head")
    return jax.shard_map(body, mesh=mesh, in_specs=in_specs, out_specs=out_specs, check_vma=False)
```

```python
import functools

import jax
import jax.numpy as jnp
import numpy as np
from jax import lax
from jax.experimental import pallas as pl
from jax.experimental.pallas import tpu as pltpu
from jax.sharding import PartitionSpec as P

HD = 128
TOK = 128
LAT_W = 16
FRAMES = 32
HEAD_AXIS = 8
BRANCH = 3
HEADS_HERE = 3
PAIRS = BRANCH * HEADS_HERE
DSH = 384
TXT = 256
RING = 8
ROWS = BRANCH * TOK
MOD_ROWS = 16
SENT = ROWS + MOD_ROWS
LAST = PAIRS - 1
STAT_ROWS = 16
LAST_ROWS = TOK + STAT_ROWS
RETURN = TOK + LAST_ROWS
WIDE = 3 * DSH
rope_base = 256.0
norm_eps = 1e-06
LOG2E = float(np.log2(np.e))
EXP_SCALE = float(HD ** (-0.5) * np.log2(np.e))
MIB = 1024 * 1024


def whole(shape):
    return pl.BlockSpec(shape, lambda *_: (0,) * len(shape))


IN_VMEM = pl.BlockSpec(memory_space=pltpu.VMEM)


def in_vmem(x):
    return pltpu.with_memory_space_constraint(x, pltpu.VMEM)


def in_hbm(x):
    return pltpu.with_memory_space_constraint(x, pltpu.HBM)


def limbs_of(value):
    limbs = []
    for _ in range(3):
        limb = value.astype(jnp.bfloat16).astype(jnp.float32)
        limbs.append(limb)
        value = value - limb
    return limbs


def rope_tables(frame):
    time_dims = HD // 8
    space_dims = (HD - time_dims) // 2
    freq = np.concatenate(
        [
            np.repeat(rope_base ** (-np.arange(0, z, 2, dtype=np.float64) / z), 2)
            for z in (time_dims, space_dims, space_dims)
        ]
    ).astype(np.float32)
    section = np.repeat(np.arange(3), (time_dims, space_dims, space_dims))
    token = jnp.arange(TOK, dtype=jnp.int32)[:, None]
    section = jnp.asarray(section)[None, :]
    position = jnp.where(
        section == 0, frame, jnp.where(section == 1, token // LAT_W, token % LAT_W)
    )
    angle = position.astype(jnp.float32) * jnp.asarray(freq)[None, :]
    sign = jnp.asarray(np.tile(np.array([-1.0, 1.0], np.float32), HD // 2))
    return jnp.cos(angle), jnp.sin(angle) * sign[None, :]


def prep_kernel(
    frame_ref, head_ref, shift_ref, ids_ref, lengths_ref, video_ref, table_ref, gain_ref,
    own_ref, gate_ref, gain_out_ref, place_ref, where_ref,
):
    head = head_ref[0]
    for s, step in enumerate((0, 0, 2, -2, 2, -2, 4, 4)):
        near = lax.rem(head + step + HEAD_AXIS, HEAD_AXIS)
        place_ref[s] = near if s in (0, 2, 3, 6) else near + 1 - 2 * lax.rem(near, 2)
    slab = lax.rem(lax.div(frame_ref[0], 2), RING)
    branch = lax.div(slab, HEADS_HERE)
    text_block = jnp.minimum(slab, 1)
    where_ref[0] = branch
    where_ref[1] = lax.rem(slab, HEADS_HERE)
    where_ref[2] = lengths_ref[branch]
    where_ref[3] = jnp.where(slab < 2, lengths_ref[BRANCH - 1] - 128 * text_block, 0)
    where_ref[4] = text_block
    level = ids_ref[lax.rem(frame_ref[0] + shift_ref[0], FRAMES)]
    looked = [table_ref[part, pl.ds(level, 1), :] for part in range(3)]
    gate_ref[...] = looked[2]
    gain_out_ref[...] = gain_ref[...]
    limbs = limbs_of(looked[0]) + limbs_of(looked[1])
    limbs.append(jnp.zeros((MOD_ROWS - 6, DSH), jnp.float32))
    for b in range(BRANCH):
        own_ref[b * TOK : (b + 1) * TOK, :] = video_ref[b]
    own_ref[ROWS:SENT, :] = jnp.concatenate(limbs, axis=0).astype(jnp.bfloat16)


def prep(frame, head, queue_shift, timestep_ids, lengths, video, table, gains):
    return pl.pallas_call(
        prep_kernel,
        out_shape=(
            pltpu.VMEM((SENT, DSH), jnp.bfloat16),
            jax.ShapeDtypeStruct((1, DSH), jnp.float32),
            pltpu.VMEM((2, HD), jnp.float32),
            jax.ShapeDtypeStruct((HEAD_AXIS,), jnp.int32),
            jax.ShapeDtypeStruct((5,), jnp.int32),
        ),
        grid_spec=pltpu.PrefetchScalarGridSpec(
            num_scalar_prefetch=5,
            grid=(1,),
            in_specs=[whole((BRANCH, TOK, DSH)), whole((3, FRAMES, DSH)), whole((2, HD))],
            out_specs=(
                IN_VMEM,
                whole((1, DSH)),
                IN_VMEM,
                pl.BlockSpec(memory_space=pltpu.SMEM),
                pl.BlockSpec(memory_space=pltpu.SMEM),
            ),
        ),
        compiler_params=pltpu.CompilerParams(vmem_limit_bytes=16 * MIB),
        name="prep",
    )(frame, head, queue_shift, timestep_ids, lengths, video, table, gains)


def project_kernel(place_ref, *refs):
    blocks = refs[:HEAD_AXIS]
    (
        w_hbm, gain_ref, cos_ref, sin_ref, out_ref, last_ref, mod_ref, acc_ref, w_ref, sems,
    ) = refs[HEAD_AXIS:]
    copies = [
        pltpu.make_async_copy(w_hbm.at[n], w_ref.at[:, pl.ds(n * DSH, DSH)], sems.at[n])
        for n in range(3)
    ]
    for copy in copies:
        copy.start()
    step = 64

    def chunk(n, carry):
        here = pl.ds(pl.multiple_of(n * step, step), step)
        total = jnp.zeros((step, 128), jnp.float32)
        square = jnp.zeros((step, 128), jnp.float32)
        for block in blocks:
            for lane in range(0, DSH, 128):
                x = block[here, lane : lane + 128].astype(jnp.float32)
                total += x
                square += x * x
        mean = jnp.sum(total, axis=1, keepdims=True) / (HEAD_AXIS * DSH)
        var = jnp.sum(square, axis=1, keepdims=True) / (HEAD_AXIS * DSH) - mean * mean
        inv = lax.rsqrt(var + norm_eps)
        for s, block in enumerate(blocks):
            limbs = block[ROWS:SENT, :].astype(jnp.float32)
            shift = limbs[0:1] + limbs[1:2] + limbs[2:3]
            scale = limbs[3:4] + limbs[4:5] + limbs[5:6]
            x = block[here, :].astype(jnp.float32)
            y = (x - mean) * inv * (1.0 + scale) + shift
            start = pl.multiple_of(place_ref[s] * DSH, DSH)
            mod_ref[here, pl.ds(start, DSH)] = y.astype(jnp.bfloat16)
        return carry

    lax.fori_loop(0, ROWS // step, chunk, 0)

    def piece(part, p):
        b, hd = divmod(p, HEADS_HERE)
        lane = part * DSH + hd * HD
        return acc_ref[b * TOK : (b + 1) * TOK, lane : lane + HD]

    def turned(part, p):
        t = piece(part, p)
        t = t * lax.rsqrt(jnp.mean(t * t, axis=1, keepdims=True) + norm_eps)
        t = t * gain_ref[part : part + 1, :]
        even = lax.broadcasted_iota(jnp.int32, t.shape, 1) % 2 == 0
        other = jnp.where(even, pltpu.roll(t, HD - 1, 1), pltpu.roll(t, 1, 1))
        return (t * cos_ref[...] + other * sin_ref[...]).astype(jnp.bfloat16)

    for copy in copies:
        copy.wait()
    acc_ref[...] = jnp.dot(mod_ref[...], w_ref[...], preferred_element_type=jnp.float32)
    for part in range(3):
        for p in range(PAIRS):
            if part == 2:
                result = piece(part, p).astype(jnp.bfloat16)
            else:
                result = turned(part, p)
            if part == 0 and p == LAST:
                for n in range(RING):
                    out_ref[n, 3 * TOK : 4 * TOK, :] = result
            elif part == 0:
                out_ref[p, 2 * TOK : 3 * TOK, :] = result
            elif p == LAST:
                last_ref[(part - 1) * TOK : part * TOK, :] = result
            else:
                out_ref[p, (part - 1) * TOK : part * TOK, :] = result


def project(places, blocks, w, gains, cosine, sine):
    return pl.pallas_call(
        project_kernel,
        out_shape=(
            pltpu.VMEM((RING, 4 * TOK, HD), jnp.bfloat16),
            pltpu.VMEM((2 * TOK, HD), jnp.bfloat16),
        ),
        grid_spec=pltpu.PrefetchScalarGridSpec(
            num_scalar_prefetch=1,
            grid=(1,),
            in_specs=[IN_VMEM] * HEAD_AXIS
            + [pl.BlockSpec(memory_space=pltpu.HBM), IN_VMEM, IN_VMEM, IN_VMEM],
            out_specs=(IN_VMEM, IN_VMEM),
            scratch_shapes=[
                pltpu.VMEM((ROWS, HEAD_AXIS * DSH), jnp.bfloat16),
                pltpu.VMEM((ROWS, WIDE), jnp.float32),
                pltpu.VMEM((HEAD_AXIS * DSH, WIDE), jnp.bfloat16),
                pltpu.SemaphoreType.DMA((3,)),
            ],
        ),
        compiler_params=pltpu.CompilerParams(vmem_limit_bytes=28 * MIB),
        cost_estimate=pl.CostEstimate(
            flops=2 * ROWS * HEAD_AXIS * DSH * 3 * DSH, bytes_accessed=12_000_000, transcendentals=0
        ),
        name="project",
    )(places, *map(in_vmem, blocks), w, *map(in_vmem, (gains, cosine, sine)))


QUAD = 4
TILE = QUAD * TOK
SET = RING * TOK
DIMS = (((1,), (1,)), ((), ()))


def score_keys(q, keys, score_ref, column, top):
    scores = lax.dot_general(q, keys, DIMS, preferred_element_type=jnp.float32)
    score_ref[:, column : column + scores.shape[1]] = scores
    for lane in range(0, scores.shape[1], 128):
        top = jnp.maximum(top, scores[:, lane : lane + 128])
    return top


def score_text(q, keys, valid, score_ref, column, top):
    scores = lax.dot_general(q, keys, DIMS, preferred_element_type=jnp.float32)
    index = lax.broadcasted_iota(jnp.int32, scores.shape, 1)
    scores = jnp.where(index < valid, scores, -jnp.inf)
    score_ref[:, column : column + scores.shape[1]] = scores
    for lane in range(0, scores.shape[1], 128):
        top = jnp.maximum(top, scores[:, lane : lane + 128])
    return top


def mix(score_ref, value_ref, top, count):
    mixed = jnp.zeros((TILE, 2 * HD), jnp.float32)
    for first in range(0, count, SET):
        stop = min(first + SET, count)
        weights = jnp.exp2(score_ref[:, first:stop] * EXP_SCALE - top).astype(jnp.bfloat16)
        mixed += jnp.dot(weights, value_ref[first:stop, :], preferred_element_type=jnp.float32)
    return mixed


def lay_values(value_ref, pieces):
    lane = lax.broadcasted_iota(jnp.int32, (value_ref.shape[0], HD), 1)
    value_ref[:, HD:] = jnp.where(lane == 0, 1.0, 0.0).astype(jnp.bfloat16)
    row = 0
    for piece in pieces:
        value_ref[row : row + piece.shape[0], :HD] = piece
        row += piece.shape[0]


def set_keys(ref):
    return ref[:, 0:TOK, :].reshape(SET, HD)


def set_values(ref):
    return ref[:, TOK : 2 * TOK, :].reshape(SET, HD)


def first_step():
    return pl.program_id(0) == 0


def tile_rows():
    return pl.ds(pl.multiple_of(pl.program_id(0) * TILE, TILE), TILE)


def gather_rows(q, pieces, score_ref, before):
    top = jnp.full((TILE, 128), -jnp.inf, jnp.float32)
    column = 0
    for keys, _, valid in pieces:
        if valid is None:
            top = score_keys(q, keys, score_ref, column, top)
        else:
            top = score_text(q, keys, valid, score_ref, column, top)
        column += keys.shape[0]
    top = jnp.max(top, axis=1, keepdims=True) * EXP_SCALE
    if before is not None:
        top = jnp.maximum(top, before)
    total = jnp.zeros((TILE, 128), jnp.float32)
    mixed = jnp.zeros((TILE, HD), jnp.float32)
    column = 0
    for _, values, _ in pieces:
        stop = column + values.shape[0]
        weights = jnp.exp2(score_ref[:, column:stop] * EXP_SCALE - top)
        for lane in range(0, stop - column, 128):
            total += weights[:, lane : lane + 128]
        mixed += jnp.dot(weights.astype(jnp.bfloat16), values, preferred_element_type=jnp.float32)
        column = stop
    return top, total, mixed


def set_piece(ref):
    return set_keys(ref), set_values(ref), None


def attend_near_kernel(
    where_ref, q_ref, own_ref, core_ref, text_ref, w_hbm,
    mixed_ref, total_ref, top_ref, q_out_ref, w_ref, score_ref, sem,
):
    copy = pltpu.make_async_copy(w_hbm, w_ref, sem)

    @pl.when(first_step())
    def _():
        copy.start()

    q = q_ref[...].reshape(TILE, HD)
    text = (text_ref[0, 0], text_ref[1, 0], where_ref[2])
    top, total, mixed = gather_rows(
        q, [set_piece(own_ref), set_piece(core_ref), text], score_ref, None
    )
    here = tile_rows()
    mixed_ref[here, :] = mixed
    total_ref[here, :] = total
    top_ref[here, :] = jnp.broadcast_to(top, (TILE, 128))
    q_out_ref[here, :] = q

    @pl.when(pl.program_id(0) == SET // TILE - 1)
    def _():
        copy.wait()


STATE = (pltpu.VMEM((SET, HD), jnp.float32),) * 3


def attend_near(where, received, own, core, text_kv, w_out):
    return pl.pallas_call(
        attend_near_kernel,
        out_shape=STATE + (pltpu.VMEM((SET, HD), jnp.bfloat16), pltpu.VMEM(w_out.shape, w_out.dtype)),
        grid_spec=pltpu.PrefetchScalarGridSpec(
            num_scalar_prefetch=1,
            grid=(SET // TILE,),
            in_specs=[
                pl.BlockSpec((QUAD, TOK, HD), lambda i, w: (i, 2, 0)),
                whole((RING, 2 * TOK, HD)),
                whole((RING, 2 * TOK, HD)),
                pl.BlockSpec((2, 1, TXT, HD), lambda i, w: (0, w[0], 0, w[1])),
                pl.BlockSpec(memory_space=pltpu.HBM),
            ],
            out_specs=(IN_VMEM,) * 5,
            scratch_shapes=[
                pltpu.VMEM((TILE, 2 * SET + TXT), jnp.float32),
                pltpu.SemaphoreType.DMA(()),
            ],
        ),
        compiler_params=pltpu.CompilerParams(vmem_limit_bytes=18 * MIB),
        cost_estimate=pl.CostEstimate(
            flops=4 * SET * 2304 * HD, bytes_accessed=3_000_000, transcendentals=SET * 2304
        ),
        name="attend_near",
    )(where, received, own, core, text_kv, w_out)


LAST_KEYS = QUAD * TOK + 128


def lay_last_kernel(where_ref, *refs):
    last_refs = refs[:QUAD]
    text_ref, keys_ref, value_ref = refs[QUAD:]
    for n, ref in enumerate(last_refs):
        keys_ref[n * TOK : (n + 1) * TOK, :] = ref[0:TOK, :]
    keys_ref[QUAD * TOK :, :] = text_ref[0, 0]
    lay_values(value_ref, [ref[TOK : 2 * TOK, :] for ref in last_refs] + [text_ref[1, 0]])


def lay_last(where, lasts, text_kv):
    return pl.pallas_call(
        lay_last_kernel,
        out_shape=(
            jax.ShapeDtypeStruct((LAST_KEYS, HD), jnp.bfloat16),
            jax.ShapeDtypeStruct((LAST_KEYS, 2 * HD), jnp.bfloat16),
        ),
        grid_spec=pltpu.PrefetchScalarGridSpec(
            num_scalar_prefetch=1,
            grid=(1,),
            in_specs=[whole((2 * TOK, HD)) for _ in lasts]
            + [
                pl.BlockSpec(
                    (2, 1, 128, HD), lambda i, w: (0, BRANCH - 1, w[4], HEADS_HERE - 1)
                )
            ],
            out_specs=(whole((LAST_KEYS, HD)), whole((LAST_KEYS, 2 * HD))),
        ),
        compiler_params=pltpu.CompilerParams(vmem_limit_bytes=16 * MIB),
        cost_estimate=pl.CostEstimate(
            flops=10_000_000_000, bytes_accessed=10_000_000, transcendentals=0
        ),
        name="lay_last",
    )(where, *lasts, text_kv)


def attend_last_kernel(where_ref, q_ref, keys_ref, value_ref, out_ref, score_ref):
    video_keys = QUAD * TOK
    q = q_ref[...].reshape(TILE, HD)
    top = jnp.full((TILE, 128), -jnp.inf, jnp.float32)
    top = score_keys(q, keys_ref[0:video_keys, :], score_ref, 0, top)
    top = score_text(q, keys_ref[video_keys:, :], where_ref[3], score_ref, video_keys, top)
    top = jnp.max(top, axis=1, keepdims=True) * EXP_SCALE
    mixed = mix(score_ref, value_ref, top, LAST_KEYS)
    total = mixed[:, HD : HD + 1]
    result = mixed[:, :HD] / total
    first = pl.program_id(0) * QUAD
    out_ref[pl.ds(first, QUAD), 0:TOK, :] = result.astype(jnp.bfloat16).reshape(QUAD, TOK, HD)
    level = jnp.broadcast_to(top + jnp.log(total) * LOG2E, (TILE, HD))
    for f in range(QUAD):
        row = jnp.transpose(level[f * TOK : (f + 1) * TOK])[0:1]
        stats = limbs_of(row) + [jnp.zeros((STAT_ROWS - 3, HD), jnp.float32)]
        out_ref[first + f, TOK:LAST_ROWS, :] = jnp.concatenate(stats, axis=0).astype(jnp.bfloat16)


def attend_last(where, received, keys, values):
    return pl.pallas_call(
        attend_last_kernel,
        out_shape=pltpu.VMEM((RING, LAST_ROWS, HD), jnp.bfloat16),
        grid_spec=pltpu.PrefetchScalarGridSpec(
            num_scalar_prefetch=1,
            grid=(SET // TILE,),
            in_specs=[
                pl.BlockSpec((QUAD, TOK, HD), lambda i, w: (i, 3, 0)),
                whole((LAST_KEYS, HD)),
                whole((LAST_KEYS, 2 * HD)),
            ],
            out_specs=IN_VMEM,
            scratch_shapes=[pltpu.VMEM((TILE, LAST_KEYS), jnp.float32)],
        ),
        compiler_params=pltpu.CompilerParams(vmem_limit_bytes=16 * MIB),
        cost_estimate=pl.CostEstimate(
            flops=4 * SET * 640 * HD, bytes_accessed=1_000_000, transcendentals=SET * 640
        ),
        name="attend_last",
    )(where, received, keys, values)


def attend_far_kernel(finish, q_ref, set_ref, *refs):
    mixed_in, total_in, top_in, *refs = refs
    here = tile_rows()
    before = top_in[here, 0:1]
    score_ref = refs[-1]
    top, total, mixed = gather_rows(q_ref[here, :], [set_piece(set_ref)], score_ref, before)
    decay = jnp.exp2(before - top)
    total += total_in[here, :] * decay
    mixed += mixed_in[here, :] * decay
    if finish:
        last_ref, out_ref = refs[:2]
        result = (mixed / jnp.sum(total, axis=1, keepdims=True)).astype(jnp.bfloat16)
        frames = pl.ds(pl.program_id(0) * QUAD, QUAD)
        out_ref[frames, 0:TOK, :] = result.reshape(QUAD, TOK, HD)
        out_ref[frames, TOK:RETURN, :] = last_ref[frames]
    else:
        mixed_ref, total_ref, top_ref = refs[:3]
        mixed_ref[here, :] = mixed
        total_ref[here, :] = total
        top_ref[here, :] = jnp.broadcast_to(top, (TILE, 128))


def attend_far(queries, keys, state, last=None):
    finish = last is not None
    operands = [queries, keys, *state] + ([last] if finish else [])
    return pl.pallas_call(
        functools.partial(attend_far_kernel, finish),
        out_shape=pltpu.VMEM((RING, RETURN, HD), jnp.bfloat16) if finish else STATE,
        grid=(SET // TILE,),
        in_specs=[IN_VMEM] * len(operands),
        out_specs=IN_VMEM if finish else (IN_VMEM,) * 3,
        scratch_shapes=[pltpu.VMEM((TILE, SET), jnp.float32)],
        compiler_params=pltpu.CompilerParams(vmem_limit_bytes=16 * MIB),
        cost_estimate=pl.CostEstimate(
            flops=4 * SET * SET * HD, bytes_accessed=3_000_000, transcendentals=SET * SET
        ),
        name="attend_far",
    )(*map(in_vmem, operands))


def output_kernel(place_ref, back_ref, w_ref, *refs):
    out_refs, attn_ref = refs[:-1], refs[-1]
    for p in range(RING):
        b, hd = divmod(p, HEADS_HERE)
        attn_ref[b * TOK : (b + 1) * TOK, hd * HD : (hd + 1) * HD] = back_ref[p, 0:TOK, :]
    levels = []
    for p in range(RING):
        stats = back_ref[p, 2 * TOK : RETURN, :].astype(jnp.float32)
        row = stats[0:1] + stats[1:2] + stats[2:3]
        levels.append(jnp.transpose(jnp.broadcast_to(row, (TOK, HD))))
    top = levels[0]
    for level in levels[1:]:
        top = jnp.maximum(top, level)
    total = jnp.zeros((TOK, HD), jnp.float32)
    mixed = jnp.zeros((TOK, HD), jnp.float32)
    for p, level in enumerate(levels):
        weight = jnp.exp2(level - top)
        total += weight
        mixed += weight * back_ref[p, TOK : 2 * TOK, :].astype(jnp.float32)
    attn_ref[(BRANCH - 1) * TOK :, (HEADS_HERE - 1) * HD :] = (mixed / total).astype(jnp.bfloat16)
    targets = [(0, 0), (1, 0), (2, 0), (3, 0), (2, 1), (3, 1), (4, 0), (5, 0)]
    for s, (n, half) in enumerate(targets):
        start = pl.multiple_of(place_ref[s] * DSH, DSH)
        out_refs[n][half * ROWS : (half + 1) * ROWS, :] = jnp.dot(
            attn_ref[...], w_ref[:, pl.ds(start, DSH)], preferred_element_type=jnp.float32
        ).astype(jnp.bfloat16)


PART_ROWS = (ROWS, ROWS, 2 * ROWS, 2 * ROWS, ROWS, ROWS)


def output(places, back, w_out):
    return pl.pallas_call(
        output_kernel,
        out_shape=tuple(
            pltpu.VMEM((rows, DSH), jnp.bfloat16) for rows in PART_ROWS
        ),
        grid_spec=pltpu.PrefetchScalarGridSpec(
            num_scalar_prefetch=1,
            grid=(1,),
            in_specs=[
                IN_VMEM,
                IN_VMEM,
            ],
            out_specs=(IN_VMEM,) * len(PART_ROWS),
            scratch_shapes=[pltpu.VMEM((ROWS, DSH), jnp.bfloat16)],
        ),
        compiler_params=pltpu.CompilerParams(vmem_limit_bytes=24 * MIB),
        cost_estimate=pl.CostEstimate(
            flops=2 * ROWS * DSH * DSH * HEAD_AXIS, bytes_accessed=5_000_000, transcendentals=0
        ),
        name="output",
    )(places, in_vmem(back), in_vmem(w_out))


def head_move(x, step):
    return lax.ppermute(x, "head", [(i, (i + step) % HEAD_AXIS) for i in range(HEAD_AXIS)])


def head_partner(x):
    return lax.ppermute(x, "head", [(i, i ^ 1) for i in range(HEAD_AXIS)])


def frame_move(x, flip):
    return lax.ppermute(x, "frame", [(i, i ^ flip) for i in range(FRAMES)])


def gather_head(own):
    partner = head_partner(own)
    opposite = head_move(own, 4)
    ahead = head_move(own, -2)
    behind = head_move(own, 2)
    return [
        own,
        partner,
        ahead,
        behind,
        head_move(partner, -2),
        head_move(partner, 2),
        opposite,
        head_partner(opposite),
    ]


def add(*terms):
    total = terms[0].astype(jnp.float32)
    for term in terms[1:]:
        total += term.astype(jnp.float32)
    return total


def scatter_head(parts):
    own, partner, ahead, behind, opposite, over = parts
    for_opposite = head_partner(over)
    near = [head_move(ahead, 2), head_move(behind, -2)]
    across = head_move(add(opposite, for_opposite).astype(jnp.bfloat16), 4)
    for_partner = [x[ROWS:] for x in near]
    over_y = head_partner(add(partner, *for_partner).astype(jnp.bfloat16))
    return add(own, *(x[:ROWS] for x in near), over_y, across)


def body(
    video, w_qkv, w_out, text_kv, text_lengths, norm_gains, mod_table, timestep_ids, queue_shift
):
    text_kv = in_hbm(text_kv)
    frame = lax.axis_index("frame").astype(jnp.int32)
    head = lax.axis_index("head").astype(jnp.int32)
    own, gate, gains, places, where = prep(
        frame.reshape(1),
        head.reshape(1),
        queue_shift,
        in_hbm(timestep_ids),
        in_hbm(text_lengths),
        in_hbm(video),
        in_hbm(mod_table.transpose(1, 0, 2)),
        in_hbm(norm_gains),
    )
    cosine, sine = rope_tables(frame)
    blocks = gather_head(own)
    weights = in_hbm(w_qkv.transpose(1, 0, 2))
    send, last = project(places, blocks, weights, gains, cosine, sine)
    rings = [[(y * RING + z) * 2 + core for z in range(RING)] for y in range(2) for core in range(2)]

    def over_rings(x):
        return lax.all_to_all(x, "frame", 0, 0, axis_index_groups=rings, tiled=True)

    received = over_rings(send)
    flips = (1, FRAMES // 2, FRAMES // 2 + 1)
    lasts = [last] + [frame_move(last, flip) for flip in flips]
    last_keys, last_values = lay_last(where, lasts, text_kv)
    near = received[:, : 2 * TOK]
    over_y = frame_move(near, FRAMES // 2)
    near_later, last_keys = lax.optimization_barrier((near, last_keys))
    over_core = frame_move(near_later, 1)
    ninth = attend_last(where, received, last_keys, last_values)
    *state, queries, w_held = attend_near(where, received, near, over_core, text_kv, in_hbm(w_out))
    over_y, _, _ = lax.optimization_barrier((over_y, state[0], ninth))
    diagonal = frame_move(over_y, 1)
    state = attend_far(queries, over_y, state)
    returned = attend_far(queries, diagonal, state, ninth)
    partial = output(places, over_rings(returned), w_held)
    proj = scatter_head(partial).reshape(video.shape)
    return (video.astype(jnp.float32) + gate * proj).astype(jnp.bfloat16)


def solution(mesh):
    in_specs = (
        P(None, "frame", "head"),
        P(None, None, "head"),
        P("head", None),
        P(None, None, None, "head"),
        P(),
        P(),
        P(None, None, "head"),
        P(),
        P(),
    )
    out_specs = P(None, "frame", "head")
    return jax.shard_map(body, mesh=mesh, in_specs=in_specs, out_specs=out_specs, check_vma=False)
```

```python
import functools

import jax
import jax.numpy as jnp
import numpy as np
from jax import lax
from jax.experimental import pallas as pl
from jax.experimental.pallas import tpu as pltpu
from jax.sharding import PartitionSpec as P

HD = 128
TOK = 128
LAT_W = 16
FRAMES = 32
HEAD_AXIS = 8
BRANCH = 3
HEADS_HERE = 3
PAIRS = BRANCH * HEADS_HERE
DSH = 384
TXT = 256
RING = 8
ROWS = BRANCH * TOK
MOD_ROWS = 16
SENT = ROWS + MOD_ROWS
LAST = PAIRS - 1
STAT_ROWS = 16
LAST_ROWS = TOK + STAT_ROWS
RETURN = TOK + LAST_ROWS
WIDE = 3 * DSH
rope_base = 256.0
norm_eps = 1e-06
LOG2E = float(np.log2(np.e))
EXP_SCALE = float(HD ** (-0.5) * np.log2(np.e))
MIB = 1024 * 1024


def whole(shape):
    return pl.BlockSpec(shape, lambda *_: (0,) * len(shape))


IN_VMEM = pl.BlockSpec(memory_space=pltpu.VMEM)


def in_vmem(x):
    return pltpu.with_memory_space_constraint(x, pltpu.VMEM)


def in_hbm(x):
    return pltpu.with_memory_space_constraint(x, pltpu.HBM)


def limbs_of(value):
    limbs = []
    for _ in range(3):
        limb = value.astype(jnp.bfloat16).astype(jnp.float32)
        limbs.append(limb)
        value = value - limb
    return limbs


def rope_tables(frame):
    time_dims = HD // 8
    space_dims = (HD - time_dims) // 2
    freq = np.concatenate(
        [
            np.repeat(rope_base ** (-np.arange(0, z, 2, dtype=np.float64) / z), 2)
            for z in (time_dims, space_dims, space_dims)
        ]
    ).astype(np.float32)
    section = np.repeat(np.arange(3), (time_dims, space_dims, space_dims))
    token = jnp.arange(TOK, dtype=jnp.int32)[:, None]
    section = jnp.asarray(section)[None, :]
    position = jnp.where(
        section == 0, frame, jnp.where(section == 1, token // LAT_W, token % LAT_W)
    )
    angle = position.astype(jnp.float32) * jnp.asarray(freq)[None, :]
    sign = jnp.asarray(np.tile(np.array([-1.0, 1.0], np.float32), HD // 2))
    return jnp.cos(angle), jnp.sin(angle) * sign[None, :]


def prep_kernel(
    frame_ref, head_ref, shift_ref, ids_ref, lengths_ref, video_ref, table_ref, gain_ref,
    own_ref, gate_ref, gain_out_ref, place_ref, where_ref,
):
    head = head_ref[0]
    for s, step in enumerate((0, 0, 2, -2, 2, -2, 4, 4)):
        near = lax.rem(head + step + HEAD_AXIS, HEAD_AXIS)
        place_ref[s] = near if s in (0, 2, 3, 6) else near + 1 - 2 * lax.rem(near, 2)
    slab = lax.rem(lax.div(frame_ref[0], 2), RING)
    branch = lax.div(slab, HEADS_HERE)
    text_block = jnp.minimum(slab, 1)
    where_ref[0] = branch
    where_ref[1] = lax.rem(slab, HEADS_HERE)
    where_ref[2] = lengths_ref[branch]
    where_ref[3] = jnp.where(slab < 2, lengths_ref[BRANCH - 1] - 128 * text_block, 0)
    where_ref[4] = text_block
    level = ids_ref[lax.rem(frame_ref[0] + shift_ref[0], FRAMES)]
    looked = [table_ref[part, pl.ds(level, 1), :] for part in range(3)]
    gate_ref[...] = looked[2]
    gain_out_ref[...] = gain_ref[...]
    limbs = limbs_of(looked[0]) + limbs_of(looked[1])
    limbs.append(jnp.zeros((MOD_ROWS - 6, DSH), jnp.float32))
    for b in range(BRANCH):
        own_ref[b * TOK : (b + 1) * TOK, :] = video_ref[b]
    own_ref[ROWS:SENT, :] = jnp.concatenate(limbs, axis=0).astype(jnp.bfloat16)


def prep(frame, head, queue_shift, timestep_ids, lengths, video, table, gains):
    return pl.pallas_call(
        prep_kernel,
        out_shape=(
            pltpu.VMEM((SENT, DSH), jnp.bfloat16),
            jax.ShapeDtypeStruct((1, DSH), jnp.float32),
            pltpu.VMEM((2, HD), jnp.float32),
            jax.ShapeDtypeStruct((HEAD_AXIS,), jnp.int32),
            jax.ShapeDtypeStruct((5,), jnp.int32),
        ),
        grid_spec=pltpu.PrefetchScalarGridSpec(
            num_scalar_prefetch=5,
            grid=(1,),
            in_specs=[whole((BRANCH, TOK, DSH)), whole((3, FRAMES, DSH)), whole((2, HD))],
            out_specs=(
                IN_VMEM,
                whole((1, DSH)),
                IN_VMEM,
                pl.BlockSpec(memory_space=pltpu.SMEM),
                pl.BlockSpec(memory_space=pltpu.SMEM),
            ),
        ),
        compiler_params=pltpu.CompilerParams(vmem_limit_bytes=16 * MIB),
        name="prep",
    )(frame, head, queue_shift, timestep_ids, lengths, video, table, gains)


def project_kernel(place_ref, *refs):
    blocks = refs[:HEAD_AXIS]
    (
        w_hbm, gain_ref, cos_ref, sin_ref, out_ref, last_ref, mod_ref, acc_ref, w_ref, sems,
    ) = refs[HEAD_AXIS:]
    copies = [
        pltpu.make_async_copy(w_hbm.at[n], w_ref.at[:, pl.ds(n * DSH, DSH)], sems.at[n])
        for n in range(3)
    ]
    for copy in copies:
        copy.start()
    step = 64

    def chunk(n, carry):
        here = pl.ds(pl.multiple_of(n * step, step), step)
        total = jnp.zeros((step, 128), jnp.float32)
        square = jnp.zeros((step, 128), jnp.float32)
        for block in blocks:
            for lane in range(0, DSH, 128):
                x = block[here, lane : lane + 128].astype(jnp.float32)
                total += x
                square += x * x
        mean = jnp.sum(total, axis=1, keepdims=True) / (HEAD_AXIS * DSH)
        var = jnp.sum(square, axis=1, keepdims=True) / (HEAD_AXIS * DSH) - mean * mean
        inv = lax.rsqrt(var + norm_eps)
        for s, block in enumerate(blocks):
            limbs = block[ROWS:SENT, :].astype(jnp.float32)
            shift = limbs[0:1] + limbs[1:2] + limbs[2:3]
            scale = limbs[3:4] + limbs[4:5] + limbs[5:6]
            x = block[here, :].astype(jnp.float32)
            y = (x - mean) * inv * (1.0 + scale) + shift
            start = pl.multiple_of(place_ref[s] * DSH, DSH)
            mod_ref[here, pl.ds(start, DSH)] = y.astype(jnp.bfloat16)
        return carry

    lax.fori_loop(0, ROWS // step, chunk, 0)

    def piece(part, p):
        b, hd = divmod(p, HEADS_HERE)
        lane = part * DSH + hd * HD
        return acc_ref[b * TOK : (b + 1) * TOK, lane : lane + HD]

    def turned(part, p):
        t = piece(part, p)
        t = t * lax.rsqrt(jnp.mean(t * t, axis=1, keepdims=True) + norm_eps)
        t = t * gain_ref[part : part + 1, :]
        even = lax.broadcasted_iota(jnp.int32, t.shape, 1) % 2 == 0
        other = jnp.where(even, pltpu.roll(t, HD - 1, 1), pltpu.roll(t, 1, 1))
        return (t * cos_ref[...] + other * sin_ref[...]).astype(jnp.bfloat16)

    for copy in copies:
        copy.wait()
    acc_ref[...] = jnp.dot(mod_ref[...], w_ref[...], preferred_element_type=jnp.float32)
    for part in range(3):
        for p in range(PAIRS):
            if part == 2:
                result = piece(part, p).astype(jnp.bfloat16)
            else:
                result = turned(part, p)
            if part == 0 and p == LAST:
                for n in range(RING):
                    out_ref[n, 3 * TOK : 4 * TOK, :] = result
            elif part == 0:
                out_ref[p, 2 * TOK : 3 * TOK, :] = result
            elif p == LAST:
                last_ref[(part - 1) * TOK : part * TOK, :] = result
            else:
                out_ref[p, (part - 1) * TOK : part * TOK, :] = result


def project(places, blocks, w, gains, cosine, sine):
    return pl.pallas_call(
        project_kernel,
        out_shape=(
            pltpu.VMEM((RING, 4 * TOK, HD), jnp.bfloat16),
            pltpu.VMEM((2 * TOK, HD), jnp.bfloat16),
        ),
        grid_spec=pltpu.PrefetchScalarGridSpec(
            num_scalar_prefetch=1,
            grid=(1,),
            in_specs=[IN_VMEM] * HEAD_AXIS
            + [pl.BlockSpec(memory_space=pltpu.HBM), IN_VMEM, IN_VMEM, IN_VMEM],
            out_specs=(IN_VMEM, IN_VMEM),
            scratch_shapes=[
                pltpu.VMEM((ROWS, HEAD_AXIS * DSH), jnp.bfloat16),
                pltpu.VMEM((ROWS, WIDE), jnp.float32),
                pltpu.VMEM((HEAD_AXIS * DSH, WIDE), jnp.bfloat16),
                pltpu.SemaphoreType.DMA((3,)),
            ],
        ),
        compiler_params=pltpu.CompilerParams(vmem_limit_bytes=28 * MIB),
        cost_estimate=pl.CostEstimate(
            flops=2 * ROWS * HEAD_AXIS * DSH * 3 * DSH, bytes_accessed=12_000_000, transcendentals=0
        ),
        name="project",
    )(places, *map(in_vmem, blocks), w, *map(in_vmem, (gains, cosine, sine)))


QUAD = 4
TILE = QUAD * TOK
SET = RING * TOK
DIMS = (((1,), (1,)), ((), ()))


def score_keys(q, keys, score_ref, column, top):
    scores = lax.dot_general(q, keys, DIMS, preferred_element_type=jnp.float32)
    score_ref[:, column : column + scores.shape[1]] = scores
    for lane in range(0, scores.shape[1], 128):
        top = jnp.maximum(top, scores[:, lane : lane + 128])
    return top


def score_text(q, keys, valid, score_ref, column, top):
    scores = lax.dot_general(q, keys, DIMS, preferred_element_type=jnp.float32)
    index = lax.broadcasted_iota(jnp.int32, scores.shape, 1)
    scores = jnp.where(index < valid, scores, -jnp.inf)
    score_ref[:, column : column + scores.shape[1]] = scores
    for lane in range(0, scores.shape[1], 128):
        top = jnp.maximum(top, scores[:, lane : lane + 128])
    return top


def mix(score_ref, value_ref, top, count):
    mixed = jnp.zeros((TILE, 2 * HD), jnp.float32)
    for first in range(0, count, SET):
        stop = min(first + SET, count)
        weights = jnp.exp2(score_ref[:, first:stop] * EXP_SCALE - top).astype(jnp.bfloat16)
        mixed += jnp.dot(weights, value_ref[first:stop, :], preferred_element_type=jnp.float32)
    return mixed


def lay_values(value_ref, pieces):
    lane = lax.broadcasted_iota(jnp.int32, (value_ref.shape[0], HD), 1)
    value_ref[:, HD:] = jnp.where(lane == 0, 1.0, 0.0).astype(jnp.bfloat16)
    row = 0
    for piece in pieces:
        value_ref[row : row + piece.shape[0], :HD] = piece
        row += piece.shape[0]


def set_keys(ref):
    return ref[:, 0:TOK, :].reshape(SET, HD)


def set_values(ref):
    return ref[:, TOK : 2 * TOK, :].reshape(SET, HD)


def first_step():
    return pl.program_id(0) == 0


def tile_rows():
    return pl.ds(pl.multiple_of(pl.program_id(0) * TILE, TILE), TILE)


def gather_rows(q, pieces, score_ref, before):
    top = jnp.full((TILE, 128), -jnp.inf, jnp.float32)
    column = 0
    for keys, _, valid in pieces:
        if valid is None:
            top = score_keys(q, keys, score_ref, column, top)
        else:
            top = score_text(q, keys, valid, score_ref, column, top)
        column += keys.shape[0]
    top = jnp.max(top, axis=1, keepdims=True) * EXP_SCALE
    if before is not None:
        top = jnp.maximum(top, before)
    total = jnp.zeros((TILE, 128), jnp.float32)
    mixed = jnp.zeros((TILE, HD), jnp.float32)
    column = 0
    for _, values, _ in pieces:
        stop = column + values.shape[0]
        weights = jnp.exp2(score_ref[:, column:stop] * EXP_SCALE - top)
        for lane in range(0, stop - column, 128):
            total += weights[:, lane : lane + 128]
        mixed += jnp.dot(weights.astype(jnp.bfloat16), values, preferred_element_type=jnp.float32)
        column = stop
    return top, total, mixed


def set_piece(ref):
    return set_keys(ref), set_values(ref), None


def attend_near_kernel(
    where_ref, q_ref, own_ref, core_ref, text_ref, w_hbm,
    mixed_ref, total_ref, top_ref, q_out_ref, w_ref, score_ref, sem,
):
    copy = pltpu.make_async_copy(w_hbm, w_ref, sem)

    @pl.when(first_step())
    def _():
        copy.start()

    q = q_ref[...].reshape(TILE, HD)
    text = (text_ref[0, 0], text_ref[1, 0], where_ref[2])
    top, total, mixed = gather_rows(
        q, [set_piece(own_ref), set_piece(core_ref), text], score_ref, None
    )
    here = tile_rows()
    mixed_ref[here, :] = mixed
    total_ref[here, :] = total
    top_ref[here, :] = jnp.broadcast_to(top, (TILE, 128))
    q_out_ref[here, :] = q

    @pl.when(pl.program_id(0) == SET // TILE - 1)
    def _():
        copy.wait()


STATE = (pltpu.VMEM((SET, HD), jnp.float32),) * 3


def attend_near(where, received, own, core, text_kv, w_out):
    return pl.pallas_call(
        attend_near_kernel,
        out_shape=STATE + (pltpu.VMEM((SET, HD), jnp.bfloat16), pltpu.VMEM(w_out.shape, w_out.dtype)),
        grid_spec=pltpu.PrefetchScalarGridSpec(
            num_scalar_prefetch=1,
            grid=(SET // TILE,),
            in_specs=[
                pl.BlockSpec((QUAD, TOK, HD), lambda i, w: (i, 2, 0)),
                whole((RING, 2 * TOK, HD)),
                whole((RING, 2 * TOK, HD)),
                pl.BlockSpec((2, 1, TXT, HD), lambda i, w: (0, w[0], 0, w[1])),
                pl.BlockSpec(memory_space=pltpu.HBM),
            ],
            out_specs=(IN_VMEM,) * 5,
            scratch_shapes=[
                pltpu.VMEM((TILE, 2 * SET + TXT), jnp.float32),
                pltpu.SemaphoreType.DMA(()),
            ],
        ),
        compiler_params=pltpu.CompilerParams(vmem_limit_bytes=18 * MIB),
        cost_estimate=pl.CostEstimate(
            flops=4 * SET * 2304 * HD, bytes_accessed=3_000_000, transcendentals=SET * 2304
        ),
        name="attend_near",
    )(where, received, own, core, text_kv, w_out)


LAST_KEYS = QUAD * TOK + 128


def lay_last_kernel(where_ref, *refs):
    last_refs = refs[:QUAD]
    text_ref, keys_ref, value_ref = refs[QUAD:]
    for n, ref in enumerate(last_refs):
        keys_ref[n * TOK : (n + 1) * TOK, :] = ref[0:TOK, :]
    keys_ref[QUAD * TOK :, :] = text_ref[0, 0]
    lay_values(value_ref, [ref[TOK : 2 * TOK, :] for ref in last_refs] + [text_ref[1, 0]])


def lay_last(where, lasts, text_kv):
    return pl.pallas_call(
        lay_last_kernel,
        out_shape=(
            jax.ShapeDtypeStruct((LAST_KEYS, HD), jnp.bfloat16),
            jax.ShapeDtypeStruct((LAST_KEYS, 2 * HD), jnp.bfloat16),
        ),
        grid_spec=pltpu.PrefetchScalarGridSpec(
            num_scalar_prefetch=1,
            grid=(1,),
            in_specs=[whole((2 * TOK, HD)) for _ in lasts]
            + [
                pl.BlockSpec(
                    (2, 1, 128, HD), lambda i, w: (0, BRANCH - 1, w[4], HEADS_HERE - 1)
                )
            ],
            out_specs=(whole((LAST_KEYS, HD)), whole((LAST_KEYS, 2 * HD))),
        ),
        compiler_params=pltpu.CompilerParams(vmem_limit_bytes=16 * MIB),
        cost_estimate=pl.CostEstimate(
            flops=10_000_000_000, bytes_accessed=10_000_000, transcendentals=0
        ),
        name="lay_last",
    )(where, *lasts, text_kv)


def attend_last_kernel(where_ref, q_ref, keys_ref, value_ref, out_ref, score_ref):
    video_keys = QUAD * TOK
    q = q_ref[...].reshape(TILE, HD)
    top = jnp.full((TILE, 128), -jnp.inf, jnp.float32)
    top = score_keys(q, keys_ref[0:video_keys, :], score_ref, 0, top)
    top = score_text(q, keys_ref[video_keys:, :], where_ref[3], score_ref, video_keys, top)
    top = jnp.max(top, axis=1, keepdims=True) * EXP_SCALE
    mixed = mix(score_ref, value_ref, top, LAST_KEYS)
    total = mixed[:, HD : HD + 1]
    result = mixed[:, :HD] / total
    first = pl.program_id(0) * QUAD
    out_ref[pl.ds(first, QUAD), 0:TOK, :] = result.astype(jnp.bfloat16).reshape(QUAD, TOK, HD)
    level = jnp.broadcast_to(top + jnp.log(total) * LOG2E, (TILE, HD))
    for f in range(QUAD):
        row = jnp.transpose(level[f * TOK : (f + 1) * TOK])[0:1]
        stats = limbs_of(row) + [jnp.zeros((STAT_ROWS - 3, HD), jnp.float32)]
        out_ref[first + f, TOK:LAST_ROWS, :] = jnp.concatenate(stats, axis=0).astype(jnp.bfloat16)


def attend_last(where, received, keys, values):
    return pl.pallas_call(
        attend_last_kernel,
        out_shape=pltpu.VMEM((RING, LAST_ROWS, HD), jnp.bfloat16),
        grid_spec=pltpu.PrefetchScalarGridSpec(
            num_scalar_prefetch=1,
            grid=(SET // TILE,),
            in_specs=[
                pl.BlockSpec((QUAD, TOK, HD), lambda i, w: (i, 3, 0)),
                whole((LAST_KEYS, HD)),
                whole((LAST_KEYS, 2 * HD)),
            ],
            out_specs=IN_VMEM,
            scratch_shapes=[pltpu.VMEM((TILE, LAST_KEYS), jnp.float32)],
        ),
        compiler_params=pltpu.CompilerParams(vmem_limit_bytes=16 * MIB),
        cost_estimate=pl.CostEstimate(
            flops=4 * SET * 640 * HD, bytes_accessed=1_000_000, transcendentals=SET * 640
        ),
        name="attend_last",
    )(where, received, keys, values)


def attend_far_kernel(finish, q_ref, set_ref, *refs):
    mixed_in, total_in, top_in, *refs = refs
    here = tile_rows()
    before = top_in[here, 0:1]
    score_ref = refs[-1]
    top, total, mixed = gather_rows(q_ref[here, :], [set_piece(set_ref)], score_ref, before)
    decay = jnp.exp2(before - top)
    total += total_in[here, :] * decay
    mixed += mixed_in[here, :] * decay
    if finish:
        last_ref, out_ref = refs[:2]
        result = (mixed / jnp.sum(total, axis=1, keepdims=True)).astype(jnp.bfloat16)
        frames = pl.ds(pl.program_id(0) * QUAD, QUAD)
        out_ref[frames, 0:TOK, :] = result.reshape(QUAD, TOK, HD)
        out_ref[frames, TOK:RETURN, :] = last_ref[frames]
    else:
        mixed_ref, total_ref, top_ref = refs[:3]
        mixed_ref[here, :] = mixed
        total_ref[here, :] = total
        top_ref[here, :] = jnp.broadcast_to(top, (TILE, 128))


def attend_far(queries, keys, state, last=None):
    finish = last is not None
    operands = [queries, keys, *state] + ([last] if finish else [])
    return pl.pallas_call(
        functools.partial(attend_far_kernel, finish),
        out_shape=pltpu.VMEM((RING, RETURN, HD), jnp.bfloat16) if finish else STATE,
        grid=(SET // TILE,),
        in_specs=[IN_VMEM] * len(operands),
        out_specs=IN_VMEM if finish else (IN_VMEM,) * 3,
        scratch_shapes=[pltpu.VMEM((TILE, SET), jnp.float32)],
        compiler_params=pltpu.CompilerParams(vmem_limit_bytes=16 * MIB),
        cost_estimate=pl.CostEstimate(
            flops=4 * SET * SET * HD, bytes_accessed=3_000_000, transcendentals=SET * SET
        ),
        name="attend_far",
    )(*map(in_vmem, operands))


def output_kernel(place_ref, back_ref, w_ref, *refs):
    out_refs, attn_ref = refs[:-1], refs[-1]
    for p in range(RING):
        b, hd = divmod(p, HEADS_HERE)
        attn_ref[b * TOK : (b + 1) * TOK, hd * HD : (hd + 1) * HD] = back_ref[p, 0:TOK, :]
    levels = []
    for p in range(RING):
        stats = back_ref[p, 2 * TOK : RETURN, :].astype(jnp.float32)
        row = stats[0:1] + stats[1:2] + stats[2:3]
        levels.append(jnp.transpose(jnp.broadcast_to(row, (TOK, HD))))
    top = levels[0]
    for level in levels[1:]:
        top = jnp.maximum(top, level)
    total = jnp.zeros((TOK, HD), jnp.float32)
    mixed = jnp.zeros((TOK, HD), jnp.float32)
    for p, level in enumerate(levels):
        weight = jnp.exp2(level - top)
        total += weight
        mixed += weight * back_ref[p, TOK : 2 * TOK, :].astype(jnp.float32)
    attn_ref[(BRANCH - 1) * TOK :, (HEADS_HERE - 1) * HD :] = (mixed / total).astype(jnp.bfloat16)
    multiply(place_ref, EARLY, attn_ref, w_ref, out_refs)


EARLY = (4, 5)
LATE = (7, 2, 3, 0, 1, 6)


def multiply(place_ref, places, attn_ref, w_ref, out_refs):
    for s, out_ref in zip(places, out_refs):
        start = pl.multiple_of(place_ref[s] * DSH, DSH)
        out_ref[...] = jnp.dot(
            attn_ref[...], w_ref[:, pl.ds(start, DSH)], preferred_element_type=jnp.float32
        ).astype(jnp.bfloat16)


def late_kernel(place_ref, attn_ref, w_ref, *out_refs):
    multiply(place_ref, LATE, attn_ref, w_ref, out_refs)


def output(kernel, places, rows, w_out, count):
    return pl.pallas_call(
        kernel,
        out_shape=(pltpu.VMEM((ROWS, DSH), jnp.bfloat16),) * count,
        grid_spec=pltpu.PrefetchScalarGridSpec(
            num_scalar_prefetch=1,
            grid=(1,),
            in_specs=[IN_VMEM, IN_VMEM],
            out_specs=(IN_VMEM,) * count,
        ),
        compiler_params=pltpu.CompilerParams(vmem_limit_bytes=16 * MIB),
        cost_estimate=pl.CostEstimate(
            flops=2 * ROWS * DSH * DSH * count, bytes_accessed=3_000_000, transcendentals=0
        ),
        name="output",
    )(places, in_vmem(rows), in_vmem(w_out))


def head_move(x, step):
    return lax.ppermute(x, "head", [(i, (i + step) % HEAD_AXIS) for i in range(HEAD_AXIS)])


def head_partner(x):
    return lax.ppermute(x, "head", [(i, i ^ 1) for i in range(HEAD_AXIS)])


def frame_move(x, flip):
    return lax.ppermute(x, "frame", [(i, i ^ flip) for i in range(FRAMES)])


def gather_head(own):
    partner = head_partner(own)
    opposite = head_move(own, 4)
    ahead = head_move(own, -2)
    behind = head_move(own, 2)
    return [
        own,
        partner,
        ahead,
        behind,
        head_move(partner, -2),
        head_move(partner, 2),
        opposite,
        head_partner(opposite),
    ]


def add(*terms):
    total = terms[0].astype(jnp.float32)
    for term in terms[1:]:
        total += term.astype(jnp.float32)
    return total


def scatter_head(places, back, w_out):
    ahead, behind, attention = output(output_kernel, places, back, w_out, 3)
    for_partner = [head_move(ahead, 2), head_move(behind, -2)]
    over, ahead, behind, own, partner, opposite = output(
        late_kernel, places, attention, w_out, len(LATE)
    )
    for_opposite = head_partner(over)
    direct = [head_move(ahead, 2), head_move(behind, -2)]
    over_y = head_partner(add(partner, *for_partner).astype(jnp.bfloat16))
    across = head_move(add(opposite, for_opposite).astype(jnp.bfloat16), 4)
    return add(own, *direct, over_y, across)


def body(
    video, w_qkv, w_out, text_kv, text_lengths, norm_gains, mod_table, timestep_ids, queue_shift
):
    text_kv = in_hbm(text_kv)
    frame = lax.axis_index("frame").astype(jnp.int32)
    head = lax.axis_index("head").astype(jnp.int32)
    own, gate, gains, places, where = prep(
        frame.reshape(1),
        head.reshape(1),
        queue_shift,
        in_hbm(timestep_ids),
        in_hbm(text_lengths),
        in_hbm(video),
        in_hbm(mod_table.transpose(1, 0, 2)),
        in_hbm(norm_gains),
    )
    cosine, sine = rope_tables(frame)
    blocks = gather_head(own)
    weights = in_hbm(w_qkv.transpose(1, 0, 2))
    send, last = project(places, blocks, weights, gains, cosine, sine)
    rings = [[(y * RING + z) * 2 + core for z in range(RING)] for y in range(2) for core in range(2)]

    def over_rings(x):
        return lax.all_to_all(x, "frame", 0, 0, axis_index_groups=rings, tiled=True)

    received = over_rings(send)
    flips = (1, FRAMES // 2, FRAMES // 2 + 1)
    lasts = [last] + [frame_move(last, flip) for flip in flips]
    last_keys, last_values = lay_last(where, lasts, text_kv)
    near = received[:, : 2 * TOK]
    over_y = frame_move(near, FRAMES // 2)
    ninth = attend_last(where, received, last_keys, last_values)
    near_later, _ = lax.optimization_barrier((near, ninth))
    over_core = frame_move(near_later, 1)
    *state, queries, w_held = attend_near(where, received, near, over_core, text_kv, in_hbm(w_out))
    over_y, _, _ = lax.optimization_barrier((over_y, state[0], ninth))
    diagonal = frame_move(over_y, 1)
    state = attend_far(queries, over_y, state)
    returned = attend_far(queries, diagonal, state, ninth)
    back = over_rings(returned)
    proj = scatter_head(places, back, w_held).reshape(video.shape)
    return (video.astype(jnp.float32) + gate * proj).astype(jnp.bfloat16)


def solution(mesh):
    in_specs = (
        P(None, "frame", "head"),
        P(None, None, "head"),
        P("head", None),
        P(None, None, None, "head"),
        P(),
        P(),
        P(None, None, "head"),
        P(),
        P(),
    )
    out_specs = P(None, "frame", "head")
    return jax.shard_map(body, mesh=mesh, in_specs=in_specs, out_specs=out_specs, check_vma=False)
```

```python
import functools

import jax
import jax.numpy as jnp
import numpy as np
from jax import lax
from jax.experimental import pallas as pl
from jax.experimental.pallas import tpu as pltpu
from jax.sharding import PartitionSpec as P

HD = 128
TOK = 128
LAT_W = 16
FRAMES = 32
HEAD_AXIS = 8
BRANCH = 3
HEADS_HERE = 3
PAIRS = BRANCH * HEADS_HERE
DSH = 384
TXT = 256
RING = 8
ROWS = BRANCH * TOK
MOD_ROWS = 16
SENT = ROWS + MOD_ROWS
LAST = PAIRS - 1
STAT_ROWS = 16
LAST_ROWS = TOK + STAT_ROWS
RETURN = TOK + LAST_ROWS
WIDE = 3 * DSH
rope_base = 256.0
norm_eps = 1e-06
LOG2E = float(np.log2(np.e))
EXP_SCALE = float(HD ** (-0.5) * np.log2(np.e))
MIB = 1024 * 1024


def whole(shape):
    return pl.BlockSpec(shape, lambda *_: (0,) * len(shape))


IN_VMEM = pl.BlockSpec(memory_space=pltpu.VMEM)


def in_vmem(x):
    return pltpu.with_memory_space_constraint(x, pltpu.VMEM)


def in_hbm(x):
    return pltpu.with_memory_space_constraint(x, pltpu.HBM)


def limbs_of(value):
    limbs = []
    for _ in range(3):
        limb = value.astype(jnp.bfloat16).astype(jnp.float32)
        limbs.append(limb)
        value = value - limb
    return limbs


def rope_tables(frame):
    time_dims = HD // 8
    space_dims = (HD - time_dims) // 2
    freq = np.concatenate(
        [
            np.repeat(rope_base ** (-np.arange(0, z, 2, dtype=np.float64) / z), 2)
            for z in (time_dims, space_dims, space_dims)
        ]
    ).astype(np.float32)
    section = np.repeat(np.arange(3), (time_dims, space_dims, space_dims))
    token = jnp.arange(TOK, dtype=jnp.int32)[:, None]
    section = jnp.asarray(section)[None, :]
    position = jnp.where(
        section == 0, frame, jnp.where(section == 1, token // LAT_W, token % LAT_W)
    )
    angle = position.astype(jnp.float32) * jnp.asarray(freq)[None, :]
    sign = jnp.asarray(np.tile(np.array([-1.0, 1.0], np.float32), HD // 2))
    return jnp.cos(angle), jnp.sin(angle) * sign[None, :]


def prep_kernel(
    frame_ref, head_ref, shift_ref, ids_ref, lengths_ref, video_ref, table_ref, gain_ref,
    own_ref, gate_ref, gain_out_ref, place_ref, where_ref,
):
    head = head_ref[0]
    for s, step in enumerate((0, 0, 2, -2, 2, -2, 4, 4)):
        near = lax.rem(head + step + HEAD_AXIS, HEAD_AXIS)
        place_ref[s] = near if s in (0, 2, 3, 6) else near + 1 - 2 * lax.rem(near, 2)
    slab = lax.rem(lax.div(frame_ref[0], 2), RING)
    branch = lax.div(slab, HEADS_HERE)
    text_block = jnp.minimum(slab, 1)
    where_ref[0] = branch
    where_ref[1] = lax.rem(slab, HEADS_HERE)
    where_ref[2] = lengths_ref[branch]
    where_ref[3] = jnp.where(slab < 2, lengths_ref[BRANCH - 1] - 128 * text_block, 0)
    where_ref[4] = text_block
    level = ids_ref[lax.rem(frame_ref[0] + shift_ref[0], FRAMES)]
    looked = [table_ref[part, pl.ds(level, 1), :] for part in range(3)]
    gate_ref[...] = looked[2]
    gain_out_ref[...] = gain_ref[...]
    limbs = limbs_of(looked[0]) + limbs_of(looked[1])
    limbs.append(jnp.zeros((MOD_ROWS - 6, DSH), jnp.float32))
    for b in range(BRANCH):
        own_ref[b * TOK : (b + 1) * TOK, :] = video_ref[b]
    own_ref[ROWS:SENT, :] = jnp.concatenate(limbs, axis=0).astype(jnp.bfloat16)


def prep(frame, head, queue_shift, timestep_ids, lengths, video, table, gains):
    return pl.pallas_call(
        prep_kernel,
        out_shape=(
            pltpu.VMEM((SENT, DSH), jnp.bfloat16),
            jax.ShapeDtypeStruct((1, DSH), jnp.float32),
            pltpu.VMEM((2, HD), jnp.float32),
            jax.ShapeDtypeStruct((HEAD_AXIS,), jnp.int32),
            jax.ShapeDtypeStruct((5,), jnp.int32),
        ),
        grid_spec=pltpu.PrefetchScalarGridSpec(
            num_scalar_prefetch=5,
            grid=(1,),
            in_specs=[whole((BRANCH, TOK, DSH)), whole((3, FRAMES, DSH)), whole((2, HD))],
            out_specs=(
                IN_VMEM,
                whole((1, DSH)),
                IN_VMEM,
                pl.BlockSpec(memory_space=pltpu.SMEM),
                pl.BlockSpec(memory_space=pltpu.SMEM),
            ),
        ),
        compiler_params=pltpu.CompilerParams(vmem_limit_bytes=16 * MIB),
        name="prep",
    )(frame, head, queue_shift, timestep_ids, lengths, video, table, gains)


def project_kernel(place_ref, *refs):
    blocks = refs[:HEAD_AXIS]
    (
        w_hbm, gain_ref, cos_ref, sin_ref, out_ref, last_ref, mod_ref, acc_ref, w_ref, sems,
    ) = refs[HEAD_AXIS:]
    copies = [
        pltpu.make_async_copy(w_hbm.at[n], w_ref.at[:, pl.ds(n * DSH, DSH)], sems.at[n])
        for n in range(3)
    ]
    for copy in copies:
        copy.start()
    step = 64

    def chunk(n, carry):
        here = pl.ds(pl.multiple_of(n * step, step), step)
        total = jnp.zeros((step, 128), jnp.float32)
        square = jnp.zeros((step, 128), jnp.float32)
        for block in blocks:
            for lane in range(0, DSH, 128):
                x = block[here, lane : lane + 128].astype(jnp.float32)
                total += x
                square += x * x
        mean = jnp.sum(total, axis=1, keepdims=True) / (HEAD_AXIS * DSH)
        var = jnp.sum(square, axis=1, keepdims=True) / (HEAD_AXIS * DSH) - mean * mean
        inv = lax.rsqrt(var + norm_eps)
        for s, block in enumerate(blocks):
            limbs = block[ROWS:SENT, :].astype(jnp.float32)
            shift = limbs[0:1] + limbs[1:2] + limbs[2:3]
            scale = limbs[3:4] + limbs[4:5] + limbs[5:6]
            x = block[here, :].astype(jnp.float32)
            y = (x - mean) * inv * (1.0 + scale) + shift
            start = pl.multiple_of(place_ref[s] * DSH, DSH)
            mod_ref[here, pl.ds(start, DSH)] = y.astype(jnp.bfloat16)
        return carry

    lax.fori_loop(0, ROWS // step, chunk, 0)

    def piece(part, p):
        b, hd = divmod(p, HEADS_HERE)
        lane = part * DSH + hd * HD
        return acc_ref[b * TOK : (b + 1) * TOK, lane : lane + HD]

    def turned(part, p):
        t = piece(part, p)
        t = t * lax.rsqrt(jnp.mean(t * t, axis=1, keepdims=True) + norm_eps)
        t = t * gain_ref[part : part + 1, :]
        even = lax.broadcasted_iota(jnp.int32, t.shape, 1) % 2 == 0
        other = jnp.where(even, pltpu.roll(t, HD - 1, 1), pltpu.roll(t, 1, 1))
        return (t * cos_ref[...] + other * sin_ref[...]).astype(jnp.bfloat16)

    for copy in copies:
        copy.wait()
    acc_ref[...] = jnp.dot(mod_ref[...], w_ref[...], preferred_element_type=jnp.float32)
    for part in range(3):
        for p in range(PAIRS):
            if part == 2:
                result = piece(part, p).astype(jnp.bfloat16)
            else:
                result = turned(part, p)
            if part == 0 and p == LAST:
                for n in range(RING):
                    out_ref[n, 3 * TOK : 4 * TOK, :] = result
            elif part == 0:
                out_ref[p, 2 * TOK : 3 * TOK, :] = result
            elif p == LAST:
                last_ref[(part - 1) * TOK : part * TOK, :] = result
            else:
                out_ref[p, (part - 1) * TOK : part * TOK, :] = result


def project(places, blocks, w, gains, cosine, sine):
    return pl.pallas_call(
        project_kernel,
        out_shape=(
            pltpu.VMEM((RING, 4 * TOK, HD), jnp.bfloat16),
            pltpu.VMEM((2 * TOK, HD), jnp.bfloat16),
        ),
        grid_spec=pltpu.PrefetchScalarGridSpec(
            num_scalar_prefetch=1,
            grid=(1,),
            in_specs=[IN_VMEM] * HEAD_AXIS
            + [pl.BlockSpec(memory_space=pltpu.HBM), IN_VMEM, IN_VMEM, IN_VMEM],
            out_specs=(IN_VMEM, IN_VMEM),
            scratch_shapes=[
                pltpu.VMEM((ROWS, HEAD_AXIS * DSH), jnp.bfloat16),
                pltpu.VMEM((ROWS, WIDE), jnp.float32),
                pltpu.VMEM((HEAD_AXIS * DSH, WIDE), jnp.bfloat16),
                pltpu.SemaphoreType.DMA((3,)),
            ],
        ),
        compiler_params=pltpu.CompilerParams(vmem_limit_bytes=28 * MIB),
        cost_estimate=pl.CostEstimate(
            flops=2 * ROWS * HEAD_AXIS * DSH * 3 * DSH, bytes_accessed=12_000_000, transcendentals=0
        ),
        name="project",
    )(places, *map(in_vmem, blocks), w, *map(in_vmem, (gains, cosine, sine)))


QUAD = 4
TILE = QUAD * TOK
SET = RING * TOK
DIMS = (((1,), (1,)), ((), ()))


def score_keys(q, keys, score_ref, column, top):
    scores = lax.dot_general(q, keys, DIMS, preferred_element_type=jnp.float32)
    score_ref[:, column : column + scores.shape[1]] = scores
    for lane in range(0, scores.shape[1], 128):
        top = jnp.maximum(top, scores[:, lane : lane + 128])
    return top


def score_text(q, keys, valid, score_ref, column, top):
    scores = lax.dot_general(q, keys, DIMS, preferred_element_type=jnp.float32)
    index = lax.broadcasted_iota(jnp.int32, scores.shape, 1)
    scores = jnp.where(index < valid, scores, -jnp.inf)
    score_ref[:, column : column + scores.shape[1]] = scores
    for lane in range(0, scores.shape[1], 128):
        top = jnp.maximum(top, scores[:, lane : lane + 128])
    return top


def mix(score_ref, value_ref, top, count):
    mixed = jnp.zeros((TILE, 2 * HD), jnp.float32)
    for first in range(0, count, SET):
        stop = min(first + SET, count)
        weights = jnp.exp2(score_ref[:, first:stop] * EXP_SCALE - top).astype(jnp.bfloat16)
        mixed += jnp.dot(weights, value_ref[first:stop, :], preferred_element_type=jnp.float32)
    return mixed


def lay_values(value_ref, pieces):
    lane = lax.broadcasted_iota(jnp.int32, (value_ref.shape[0], HD), 1)
    value_ref[:, HD:] = jnp.where(lane == 0, 1.0, 0.0).astype(jnp.bfloat16)
    row = 0
    for piece in pieces:
        value_ref[row : row + piece.shape[0], :HD] = piece
        row += piece.shape[0]


def set_keys(ref):
    return ref[:, 0:TOK, :].reshape(SET, HD)


def set_values(ref):
    return ref[:, TOK : 2 * TOK, :].reshape(SET, HD)


def first_step():
    return pl.program_id(0) == 0


def tile_rows():
    return pl.ds(pl.multiple_of(pl.program_id(0) * TILE, TILE), TILE)


def gather_rows(flag_ref, q, pieces, before, score_ref, top_ref, total_ref, mixed_ref):
    def add_up(weights, values, total, mixed):
        for lane in range(0, weights.shape[1], 128):
            total += weights[:, lane : lane + 128]
        mixed += jnp.dot(weights.astype(jnp.bfloat16), values, preferred_element_type=jnp.float32)
        return total, mixed

    zeros = jnp.zeros((TILE, 128), jnp.float32)

    @pl.when(flag_ref[0] == 1)
    def _():
        total, mixed = zeros, zeros
        for keys, values, valid in pieces:
            scores = lax.dot_general(q, keys, DIMS, preferred_element_type=jnp.float32)
            if valid is not None:
                index = lax.broadcasted_iota(jnp.int32, scores.shape, 1)
                scores = jnp.where(index < valid, scores, -jnp.inf)
            total, mixed = add_up(jnp.exp2(scores * EXP_SCALE), values, total, mixed)
        top_ref[...] = zeros
        total_ref[...] = total
        mixed_ref[...] = mixed

    @pl.when(flag_ref[0] != 1)
    def _():
        top = jnp.full((TILE, 128), -jnp.inf, jnp.float32)
        column = 0
        for keys, _, valid in pieces:
            if valid is None:
                top = score_keys(q, keys, score_ref, column, top)
            else:
                top = score_text(q, keys, valid, score_ref, column, top)
            column += keys.shape[0]
        top = jnp.max(top, axis=1, keepdims=True) * EXP_SCALE
        if before is not None:
            top = jnp.maximum(top, before)
        total, mixed = zeros, zeros
        column = 0
        for _, values, _ in pieces:
            stop = column + values.shape[0]
            weights = jnp.exp2(score_ref[:, column:stop] * EXP_SCALE - top)
            total, mixed = add_up(weights, values, total, mixed)
            column = stop
        top_ref[...] = jnp.broadcast_to(top, (TILE, 128))
        total_ref[...] = total
        mixed_ref[...] = mixed


def set_piece(ref):
    return set_keys(ref), set_values(ref), None


def attend_near_kernel(
    where_ref, flag_ref, q_ref, own_ref, core_ref, text_ref, w_hbm,
    mixed_ref, total_ref, top_ref, q_out_ref, w_ref, score_ref, sem,
):
    copy = pltpu.make_async_copy(w_hbm, w_ref, sem)

    @pl.when(first_step())
    def _():
        copy.start()

    q = q_ref[...].reshape(TILE, HD)
    text = (text_ref[0, 0], text_ref[1, 0], where_ref[2])
    here = tile_rows()
    gather_rows(
        flag_ref, q, [set_piece(own_ref), set_piece(core_ref), text], None, score_ref,
        top_ref.at[here], total_ref.at[here], mixed_ref.at[here],
    )
    q_out_ref[here, :] = q

    @pl.when(pl.program_id(0) == SET // TILE - 1)
    def _():
        copy.wait()


STATE = (pltpu.VMEM((SET, HD), jnp.float32),) * 3


def attend_near(where, flag, received, own, core, text_kv, w_out):
    return pl.pallas_call(
        attend_near_kernel,
        out_shape=STATE + (pltpu.VMEM((SET, HD), jnp.bfloat16), pltpu.VMEM(w_out.shape, w_out.dtype)),
        grid_spec=pltpu.PrefetchScalarGridSpec(
            num_scalar_prefetch=2,
            grid=(SET // TILE,),
            in_specs=[
                pl.BlockSpec((QUAD, TOK, HD), lambda i, w, f: (i, 2, 0)),
                whole((RING, 2 * TOK, HD)),
                whole((RING, 2 * TOK, HD)),
                pl.BlockSpec((2, 1, TXT, HD), lambda i, w, f: (0, w[0], 0, w[1])),
                pl.BlockSpec(memory_space=pltpu.HBM),
            ],
            out_specs=(IN_VMEM,) * 5,
            scratch_shapes=[
                pltpu.VMEM((TILE, 2 * SET + TXT), jnp.float32),
                pltpu.SemaphoreType.DMA(()),
            ],
        ),
        compiler_params=pltpu.CompilerParams(vmem_limit_bytes=18 * MIB),
        cost_estimate=pl.CostEstimate(
            flops=4 * SET * 2304 * HD, bytes_accessed=3_000_000, transcendentals=SET * 2304
        ),
        name="attend_near",
    )(where, flag, received, own, core, text_kv, w_out)


LAST_KEYS = QUAD * TOK + 128


def lay_last_kernel(where_ref, *refs):
    last_refs = refs[:QUAD]
    text_ref, own_text_ref, gain_ref, keys_ref, value_ref, flag_ref = refs[QUAD:]
    for n, ref in enumerate(last_refs):
        keys_ref[n * TOK : (n + 1) * TOK, :] = ref[0:TOK, :]
    keys_ref[QUAD * TOK :, :] = text_ref[0, 0]
    lay_values(value_ref, [ref[TOK : 2 * TOK, :] for ref in last_refs] + [text_ref[1, 0]])
    room = 1.03 * HD
    gains = gain_ref[...] * gain_ref[...]
    text = own_text_ref[0, 0].astype(jnp.float32)
    key_norm = jnp.maximum(
        room * jnp.max(gains[1:2]), jnp.max(jnp.sum(text * text, axis=1, keepdims=True))
    )
    bound = EXP_SCALE * EXP_SCALE * room * jnp.max(gains[0:1]) * key_norm
    flag_ref[0] = jnp.where(bound < MOST_LOG2 * MOST_LOG2, 1, 0)


MOST_LOG2 = 90.0


def lay_last(where, lasts, text_kv, gains):
    return pl.pallas_call(
        lay_last_kernel,
        out_shape=(
            jax.ShapeDtypeStruct((LAST_KEYS, HD), jnp.bfloat16),
            jax.ShapeDtypeStruct((LAST_KEYS, 2 * HD), jnp.bfloat16),
            jax.ShapeDtypeStruct((1,), jnp.int32),
        ),
        grid_spec=pltpu.PrefetchScalarGridSpec(
            num_scalar_prefetch=1,
            grid=(1,),
            in_specs=[whole((2 * TOK, HD)) for _ in lasts]
            + [
                pl.BlockSpec(
                    (2, 1, 128, HD), lambda i, w: (0, BRANCH - 1, w[4], HEADS_HERE - 1)
                ),
                pl.BlockSpec((1, 1, TXT, HD), lambda i, w: (0, w[0], 0, w[1])),
                whole((2, HD)),
            ],
            out_specs=(
                whole((LAST_KEYS, HD)),
                whole((LAST_KEYS, 2 * HD)),
                pl.BlockSpec(memory_space=pltpu.SMEM),
            ),
        ),
        compiler_params=pltpu.CompilerParams(vmem_limit_bytes=16 * MIB),
        cost_estimate=pl.CostEstimate(
            flops=10_000_000_000, bytes_accessed=10_000_000, transcendentals=0
        ),
        name="lay_last",
    )(where, *lasts, text_kv, text_kv, gains)


def attend_last_kernel(where_ref, q_ref, keys_ref, value_ref, out_ref, score_ref):
    video_keys = QUAD * TOK
    q = q_ref[...].reshape(TILE, HD)
    top = jnp.full((TILE, 128), -jnp.inf, jnp.float32)
    top = score_keys(q, keys_ref[0:video_keys, :], score_ref, 0, top)
    top = score_text(q, keys_ref[video_keys:, :], where_ref[3], score_ref, video_keys, top)
    top = jnp.max(top, axis=1, keepdims=True) * EXP_SCALE
    mixed = mix(score_ref, value_ref, top, LAST_KEYS)
    total = mixed[:, HD : HD + 1]
    result = mixed[:, :HD] / total
    first = pl.program_id(0) * QUAD
    out_ref[pl.ds(first, QUAD), 0:TOK, :] = result.astype(jnp.bfloat16).reshape(QUAD, TOK, HD)
    level = jnp.broadcast_to(top + jnp.log(total) * LOG2E, (TILE, HD))
    for f in range(QUAD):
        row = jnp.transpose(level[f * TOK : (f + 1) * TOK])[0:1]
        stats = limbs_of(row) + [jnp.zeros((STAT_ROWS - 3, HD), jnp.float32)]
        out_ref[first + f, TOK:LAST_ROWS, :] = jnp.concatenate(stats, axis=0).astype(jnp.bfloat16)


def attend_last(where, received, keys, values):
    return pl.pallas_call(
        attend_last_kernel,
        out_shape=pltpu.VMEM((RING, LAST_ROWS, HD), jnp.bfloat16),
        grid_spec=pltpu.PrefetchScalarGridSpec(
            num_scalar_prefetch=1,
            grid=(SET // TILE,),
            in_specs=[
                pl.BlockSpec((QUAD, TOK, HD), lambda i, w: (i, 3, 0)),
                whole((LAST_KEYS, HD)),
                whole((LAST_KEYS, 2 * HD)),
            ],
            out_specs=IN_VMEM,
            scratch_shapes=[pltpu.VMEM((TILE, LAST_KEYS), jnp.float32)],
        ),
        compiler_params=pltpu.CompilerParams(vmem_limit_bytes=16 * MIB),
        cost_estimate=pl.CostEstimate(
            flops=4 * SET * 640 * HD, bytes_accessed=1_000_000, transcendentals=SET * 640
        ),
        name="attend_last",
    )(where, received, keys, values)


def attend_far_kernel(finish, flag_ref, q_ref, set_ref, *refs):
    mixed_in, total_in, top_in, *refs = refs
    score_ref, top_ref, total_ref, mixed_ref = refs[-4:]
    here = tile_rows()
    before = top_in[here, 0:1]
    gather_rows(
        flag_ref, q_ref[here, :], [set_piece(set_ref)], before, score_ref,
        top_ref, total_ref, mixed_ref,
    )
    decay = jnp.exp2(before - top_ref[:, 0:1])
    total = total_ref[...] + total_in[here, :] * decay
    mixed = mixed_ref[...] + mixed_in[here, :] * decay
    if finish:
        last_ref, out_ref = refs[:2]
        result = (mixed / jnp.sum(total, axis=1, keepdims=True)).astype(jnp.bfloat16)
        frames = pl.ds(pl.program_id(0) * QUAD, QUAD)
        out_ref[frames, 0:TOK, :] = result.reshape(QUAD, TOK, HD)
        out_ref[frames, TOK:RETURN, :] = last_ref[frames]
    else:
        mixed_out, total_out, top_out = refs[:3]
        mixed_out[here, :] = mixed
        total_out[here, :] = total
        top_out[here, :] = top_ref[...]


def attend_far(flag, queries, keys, state, last=None):
    finish = last is not None
    operands = [queries, keys, *state] + ([last] if finish else [])
    return pl.pallas_call(
        functools.partial(attend_far_kernel, finish),
        out_shape=pltpu.VMEM((RING, RETURN, HD), jnp.bfloat16) if finish else STATE,
        grid_spec=pltpu.PrefetchScalarGridSpec(
            num_scalar_prefetch=1,
            grid=(SET // TILE,),
            in_specs=[IN_VMEM] * len(operands),
            out_specs=IN_VMEM if finish else (IN_VMEM,) * 3,
            scratch_shapes=[pltpu.VMEM((TILE, SET), jnp.float32)]
            + [pltpu.VMEM((TILE, 128), jnp.float32)] * 3,
        ),
        compiler_params=pltpu.CompilerParams(vmem_limit_bytes=16 * MIB),
        cost_estimate=pl.CostEstimate(
            flops=4 * SET * SET * HD, bytes_accessed=3_000_000, transcendentals=SET * SET
        ),
        name="attend_far",
    )(flag, *map(in_vmem, operands))


def output_kernel(place_ref, back_ref, w_ref, *refs):
    out_refs, attn_ref = refs[:-1], refs[-1]
    for p in range(RING):
        b, hd = divmod(p, HEADS_HERE)
        attn_ref[b * TOK : (b + 1) * TOK, hd * HD : (hd + 1) * HD] = back_ref[p, 0:TOK, :]
    levels = []
    for p in range(RING):
        stats = back_ref[p, 2 * TOK : RETURN, :].astype(jnp.float32)
        row = stats[0:1] + stats[1:2] + stats[2:3]
        levels.append(jnp.transpose(jnp.broadcast_to(row, (TOK, HD))))
    top = levels[0]
    for level in levels[1:]:
        top = jnp.maximum(top, level)
    total = jnp.zeros((TOK, HD), jnp.float32)
    mixed = jnp.zeros((TOK, HD), jnp.float32)
    for p, level in enumerate(levels):
        weight = jnp.exp2(level - top)
        total += weight
        mixed += weight * back_ref[p, TOK : 2 * TOK, :].astype(jnp.float32)
    attn_ref[(BRANCH - 1) * TOK :, (HEADS_HERE - 1) * HD :] = (mixed / total).astype(jnp.bfloat16)
    multiply(place_ref, EARLY, attn_ref, w_ref, out_refs)


EARLY = (4, 5)
LATE = (7, 2, 3, 0, 1, 6)


def multiply(place_ref, places, attn_ref, w_ref, out_refs):
    for s, out_ref in zip(places, out_refs):
        start = pl.multiple_of(place_ref[s] * DSH, DSH)
        out_ref[...] = jnp.dot(
            attn_ref[...], w_ref[:, pl.ds(start, DSH)], preferred_element_type=jnp.float32
        ).astype(jnp.bfloat16)


def late_kernel(place_ref, attn_ref, w_ref, *out_refs):
    multiply(place_ref, LATE, attn_ref, w_ref, out_refs)


def output(kernel, places, rows, w_out, count):
    return pl.pallas_call(
        kernel,
        out_shape=(pltpu.VMEM((ROWS, DSH), jnp.bfloat16),) * count,
        grid_spec=pltpu.PrefetchScalarGridSpec(
            num_scalar_prefetch=1,
            grid=(1,),
            in_specs=[IN_VMEM, IN_VMEM],
            out_specs=(IN_VMEM,) * count,
        ),
        compiler_params=pltpu.CompilerParams(vmem_limit_bytes=16 * MIB),
        cost_estimate=pl.CostEstimate(
            flops=2 * ROWS * DSH * DSH * count, bytes_accessed=3_000_000, transcendentals=0
        ),
        name="output",
    )(places, in_vmem(rows), in_vmem(w_out))


def head_move(x, step):
    return lax.ppermute(x, "head", [(i, (i + step) % HEAD_AXIS) for i in range(HEAD_AXIS)])


def head_partner(x):
    return lax.ppermute(x, "head", [(i, i ^ 1) for i in range(HEAD_AXIS)])


def frame_move(x, flip):
    return lax.ppermute(x, "frame", [(i, i ^ flip) for i in range(FRAMES)])


def gather_head(own):
    partner = head_partner(own)
    opposite = head_move(own, 4)
    ahead = head_move(own, -2)
    behind = head_move(own, 2)
    return [
        own,
        partner,
        ahead,
        behind,
        head_move(partner, -2),
        head_move(partner, 2),
        opposite,
        head_partner(opposite),
    ]


def add(*terms):
    total = terms[0].astype(jnp.float32)
    for term in terms[1:]:
        total += term.astype(jnp.float32)
    return total


def scatter_head(places, back, w_out):
    ahead, behind, attention = output(output_kernel, places, back, w_out, 3)
    for_partner = [head_move(ahead, 2), head_move(behind, -2)]
    over, ahead, behind, own, partner, opposite = output(
        late_kernel, places, attention, w_out, len(LATE)
    )
    for_opposite = head_partner(over)
    direct = [head_move(ahead, 2), head_move(behind, -2)]
    over_y = head_partner(add(partner, *for_partner).astype(jnp.bfloat16))
    across = head_move(add(opposite, for_opposite).astype(jnp.bfloat16), 4)
    return add(own, *direct, over_y, across)


def body(
    video, w_qkv, w_out, text_kv, text_lengths, norm_gains, mod_table, timestep_ids, queue_shift
):
    text_kv = in_hbm(text_kv)
    frame = lax.axis_index("frame").astype(jnp.int32)
    head = lax.axis_index("head").astype(jnp.int32)
    own, gate, gains, places, where = prep(
        frame.reshape(1),
        head.reshape(1),
        queue_shift,
        in_hbm(timestep_ids),
        in_hbm(text_lengths),
        in_hbm(video),
        in_hbm(mod_table.transpose(1, 0, 2)),
        in_hbm(norm_gains),
    )
    cosine, sine = rope_tables(frame)
    blocks = gather_head(own)
    weights = in_hbm(w_qkv.transpose(1, 0, 2))
    send, last = project(places, blocks, weights, gains, cosine, sine)
    rings = [[(y * RING + z) * 2 + core for z in range(RING)] for y in range(2) for core in range(2)]

    def over_rings(x):
        return lax.all_to_all(x, "frame", 0, 0, axis_index_groups=rings, tiled=True)

    received = over_rings(send)
    flips = (1, FRAMES // 2, FRAMES // 2 + 1)
    lasts = [last] + [frame_move(last, flip) for flip in flips]
    last_keys, last_values, flag = lay_last(where, lasts, text_kv, gains)
    near = received[:, : 2 * TOK]
    over_y = frame_move(near, FRAMES // 2)
    near_later, last_keys = lax.optimization_barrier((near, last_keys))
    over_core = frame_move(near_later, 1)
    ninth = attend_last(where, received, last_keys, last_values)
    *state, queries, w_held = attend_near(
        where, flag, received, near, over_core, text_kv, in_hbm(w_out)
    )
    over_y, _, _ = lax.optimization_barrier((over_y, state[0], ninth))
    diagonal = frame_move(over_y, 1)
    state = attend_far(flag, queries, over_y, state)
    returned = attend_far(flag, queries, diagonal, state, ninth)
    back = over_rings(returned)
    proj = scatter_head(places, back, w_held).reshape(video.shape)
    return (video.astype(jnp.float32) + gate * proj).astype(jnp.bfloat16)


def solution(mesh):
    in_specs = (
        P(None, "frame", "head"),
        P(None, None, "head"),
        P("head", None),
        P(None, None, None, "head"),
        P(),
        P(),
        P(None, None, "head"),
        P(),
        P(),
    )
    out_specs = P(None, "frame", "head")
    return jax.shard_map(body, mesh=mesh, in_specs=in_specs, out_specs=out_specs, check_vma=False)
```

```python
import functools

import jax
import jax.numpy as jnp
import numpy as np
from jax import lax
from jax.experimental import pallas as pl
from jax.experimental.pallas import tpu as pltpu
from jax.sharding import PartitionSpec as P

HD = 128
TOK = 128
LAT_W = 16
FRAMES = 32
HEAD_AXIS = 8
BRANCH = 3
HEADS_HERE = 3
PAIRS = BRANCH * HEADS_HERE
DSH = 384
TXT = 256
RING = 8
ROWS = BRANCH * TOK
MOD_ROWS = 16
SENT = ROWS + MOD_ROWS
CUT = ROWS // 2
LAST = PAIRS - 1
STAT_ROWS = 16
LAST_ROWS = TOK + STAT_ROWS
RETURN = TOK + LAST_ROWS
WIDE = 3 * DSH
rope_base = 256.0
norm_eps = 1e-06
LOG2E = float(np.log2(np.e))
EXP_SCALE = float(HD ** (-0.5) * np.log2(np.e))
MIB = 1024 * 1024


def whole(shape):
    return pl.BlockSpec(shape, lambda *_: (0,) * len(shape))


IN_VMEM = pl.BlockSpec(memory_space=pltpu.VMEM)


def in_vmem(x):
    return pltpu.with_memory_space_constraint(x, pltpu.VMEM)


def in_hbm(x):
    return pltpu.with_memory_space_constraint(x, pltpu.HBM)


def limbs_of(value):
    limbs = []
    for _ in range(3):
        limb = value.astype(jnp.bfloat16).astype(jnp.float32)
        limbs.append(limb)
        value = value - limb
    return limbs


def rope_tables(frame):
    time_dims = HD // 8
    space_dims = (HD - time_dims) // 2
    freq = np.concatenate(
        [
            np.repeat(rope_base ** (-np.arange(0, z, 2, dtype=np.float64) / z), 2)
            for z in (time_dims, space_dims, space_dims)
        ]
    ).astype(np.float32)
    section = np.repeat(np.arange(3), (time_dims, space_dims, space_dims))
    token = jnp.arange(TOK, dtype=jnp.int32)[:, None]
    section = jnp.asarray(section)[None, :]
    position = jnp.where(
        section == 0, frame, jnp.where(section == 1, token // LAT_W, token % LAT_W)
    )
    angle = position.astype(jnp.float32) * jnp.asarray(freq)[None, :]
    sign = jnp.asarray(np.tile(np.array([-1.0, 1.0], np.float32), HD // 2))
    return jnp.cos(angle), jnp.sin(angle) * sign[None, :]


def prep_kernel(
    frame_ref, head_ref, shift_ref, ids_ref, lengths_ref, video_ref, table_ref, gain_ref,
    own_ref, gate_ref, gain_out_ref, place_ref, where_ref,
):
    head = head_ref[0]
    for s, step in enumerate((0, 0, 2, -2, 2, -2, 4, 4)):
        near = lax.rem(head + step + HEAD_AXIS, HEAD_AXIS)
        place_ref[s] = near if s in (0, 2, 3, 6) else near + 1 - 2 * lax.rem(near, 2)
    slab = lax.rem(lax.div(frame_ref[0], 2), RING)
    branch = lax.div(slab, HEADS_HERE)
    text_block = jnp.minimum(slab, 1)
    where_ref[0] = branch
    where_ref[1] = lax.rem(slab, HEADS_HERE)
    where_ref[2] = lengths_ref[branch]
    where_ref[3] = jnp.where(slab < 2, lengths_ref[BRANCH - 1] - 128 * text_block, 0)
    where_ref[4] = text_block
    level = ids_ref[lax.rem(frame_ref[0] + shift_ref[0], FRAMES)]
    looked = [table_ref[part, pl.ds(level, 1), :] for part in range(3)]
    gate_ref[...] = looked[2]
    gain_out_ref[...] = gain_ref[...]
    limbs = limbs_of(looked[0]) + limbs_of(looked[1])
    limbs.append(jnp.zeros((MOD_ROWS - 6, DSH), jnp.float32))
    for b in range(BRANCH):
        own_ref[b * TOK : (b + 1) * TOK, :] = video_ref[b]
    own_ref[ROWS:SENT, :] = jnp.concatenate(limbs, axis=0).astype(jnp.bfloat16)


def prep(frame, head, queue_shift, timestep_ids, lengths, video, table, gains):
    return pl.pallas_call(
        prep_kernel,
        out_shape=(
            pltpu.VMEM((SENT, DSH), jnp.bfloat16),
            jax.ShapeDtypeStruct((1, DSH), jnp.float32),
            pltpu.VMEM((2, HD), jnp.float32),
            jax.ShapeDtypeStruct((HEAD_AXIS,), jnp.int32),
            jax.ShapeDtypeStruct((5,), jnp.int32),
        ),
        grid_spec=pltpu.PrefetchScalarGridSpec(
            num_scalar_prefetch=5,
            grid=(1,),
            in_specs=[whole((BRANCH, TOK, DSH)), whole((3, FRAMES, DSH)), whole((2, HD))],
            out_specs=(
                IN_VMEM,
                whole((1, DSH)),
                IN_VMEM,
                pl.BlockSpec(memory_space=pltpu.SMEM),
                pl.BlockSpec(memory_space=pltpu.SMEM),
            ),
        ),
        compiler_params=pltpu.CompilerParams(vmem_limit_bytes=16 * MIB),
        name="prep",
    )(frame, head, queue_shift, timestep_ids, lengths, video, table, gains)


def project_kernel(place_ref, *refs):
    blocks, parts = refs[:6], refs[6:10]
    (
        w_hbm, gain_ref, cos_ref, sin_ref, out_ref, last_ref, mod_ref, acc_ref, w_ref, sems,
    ) = refs[10:]
    copies = [
        pltpu.make_async_copy(w_hbm.at[n], w_ref.at[:, pl.ds(n * DSH, DSH)], sems.at[n])
        for n in range(3)
    ]
    for copy in copies:
        copy.start()
    limbs = [block[ROWS:SENT, :] for block in blocks]
    limbs += [parts[n][ROWS - CUT : SENT - CUT, :] for n in (1, 3)]
    mods = []
    for limb in limbs:
        limb = limb.astype(jnp.float32)
        shift = limb[0:1] + limb[1:2] + limb[2:3]
        mods.append((shift, 1.0 + (limb[3:4] + limb[4:5] + limb[5:6])))
    step = 64
    for first in (0, CUT):
        late = 1 if first else 0

        def chunk(n, carry):
            there = pl.ds(pl.multiple_of(n * step, step), step)
            here = pl.ds(pl.multiple_of(first + n * step, step), step)
            sources = [(block, here) for block in blocks]
            sources += [(parts[late], there), (parts[2 + late], there)]
            total = jnp.zeros((step, 128), jnp.float32)
            square = jnp.zeros((step, 128), jnp.float32)
            for ref, rows in sources:
                for lane in range(0, DSH, 128):
                    x = ref[rows, lane : lane + 128].astype(jnp.float32)
                    total += x
                    square += x * x
            mean = jnp.sum(total, axis=1, keepdims=True) / (HEAD_AXIS * DSH)
            var = jnp.sum(square, axis=1, keepdims=True) / (HEAD_AXIS * DSH) - mean * mean
            inv = lax.rsqrt(var + norm_eps)
            for s, (ref, rows) in enumerate(sources):
                shift, scale = mods[s]
                y = (ref[rows, :].astype(jnp.float32) - mean) * inv * scale + shift
                start = pl.multiple_of(place_ref[s] * DSH, DSH)
                mod_ref[here, pl.ds(start, DSH)] = y.astype(jnp.bfloat16)
            return carry

        lax.fori_loop(0, CUT // step, chunk, 0)

    def piece(part, p):
        b, hd = divmod(p, HEADS_HERE)
        lane = part * DSH + hd * HD
        return acc_ref[b * TOK : (b + 1) * TOK, lane : lane + HD]

    def turned(part, p):
        t = piece(part, p)
        t = t * lax.rsqrt(jnp.mean(t * t, axis=1, keepdims=True) + norm_eps)
        t = t * gain_ref[part : part + 1, :]
        even = lax.broadcasted_iota(jnp.int32, t.shape, 1) % 2 == 0
        other = jnp.where(even, pltpu.roll(t, HD - 1, 1), pltpu.roll(t, 1, 1))
        return (t * cos_ref[...] + other * sin_ref[...]).astype(jnp.bfloat16)

    for copy in copies:
        copy.wait()
    acc_ref[...] = jnp.dot(mod_ref[...], w_ref[...], preferred_element_type=jnp.float32)
    for part in range(3):
        for p in range(PAIRS):
            if part == 2:
                result = piece(part, p).astype(jnp.bfloat16)
            else:
                result = turned(part, p)
            if part == 0 and p == LAST:
                for n in range(RING):
                    out_ref[n, 3 * TOK : 4 * TOK, :] = result
            elif part == 0:
                out_ref[p, 2 * TOK : 3 * TOK, :] = result
            elif p == LAST:
                last_ref[(part - 1) * TOK : part * TOK, :] = result
            else:
                out_ref[p, (part - 1) * TOK : part * TOK, :] = result


def project(places, blocks, w, gains, cosine, sine):
    return pl.pallas_call(
        project_kernel,
        out_shape=(
            pltpu.VMEM((RING, 4 * TOK, HD), jnp.bfloat16),
            pltpu.VMEM((2 * TOK, HD), jnp.bfloat16),
        ),
        grid_spec=pltpu.PrefetchScalarGridSpec(
            num_scalar_prefetch=1,
            grid=(1,),
            in_specs=[IN_VMEM] * len(blocks)
            + [pl.BlockSpec(memory_space=pltpu.HBM), IN_VMEM, IN_VMEM, IN_VMEM],
            out_specs=(IN_VMEM, IN_VMEM),
            scratch_shapes=[
                pltpu.VMEM((ROWS, HEAD_AXIS * DSH), jnp.bfloat16),
                pltpu.VMEM((ROWS, WIDE), jnp.float32),
                pltpu.VMEM((HEAD_AXIS * DSH, WIDE), jnp.bfloat16),
                pltpu.SemaphoreType.DMA((3,)),
            ],
        ),
        compiler_params=pltpu.CompilerParams(vmem_limit_bytes=28 * MIB),
        cost_estimate=pl.CostEstimate(
            flops=2 * ROWS * HEAD_AXIS * DSH * 3 * DSH, bytes_accessed=12_000_000, transcendentals=0
        ),
        name="project",
    )(places, *map(in_vmem, blocks), w, *map(in_vmem, (gains, cosine, sine)))


QUAD = 4
TILE = QUAD * TOK
SET = RING * TOK
DIMS = (((1,), (1,)), ((), ()))


def score_keys(q, keys, score_ref, column, top):
    scores = lax.dot_general(q, keys, DIMS, preferred_element_type=jnp.float32)
    score_ref[:, column : column + scores.shape[1]] = scores
    for lane in range(0, scores.shape[1], 128):
        top = jnp.maximum(top, scores[:, lane : lane + 128])
    return top


def score_text(q, keys, valid, score_ref, column, top):
    scores = lax.dot_general(q, keys, DIMS, preferred_element_type=jnp.float32)
    index = lax.broadcasted_iota(jnp.int32, scores.shape, 1)
    scores = jnp.where(index < valid, scores, -jnp.inf)
    score_ref[:, column : column + scores.shape[1]] = scores
    for lane in range(0, scores.shape[1], 128):
        top = jnp.maximum(top, scores[:, lane : lane + 128])
    return top


def mix(score_ref, value_ref, top, count):
    mixed = jnp.zeros((TILE, 2 * HD), jnp.float32)
    for first in range(0, count, SET):
        stop = min(first + SET, count)
        weights = jnp.exp2(score_ref[:, first:stop] * EXP_SCALE - top).astype(jnp.bfloat16)
        mixed += jnp.dot(weights, value_ref[first:stop, :], preferred_element_type=jnp.float32)
    return mixed


def lay_values(value_ref, pieces):
    lane = lax.broadcasted_iota(jnp.int32, (value_ref.shape[0], HD), 1)
    value_ref[:, HD:] = jnp.where(lane == 0, 1.0, 0.0).astype(jnp.bfloat16)
    row = 0
    for piece in pieces:
        value_ref[row : row + piece.shape[0], :HD] = piece
        row += piece.shape[0]


def set_keys(ref):
    return ref[:, 0:TOK, :].reshape(SET, HD)


def set_values(ref):
    return ref[:, TOK : 2 * TOK, :].reshape(SET, HD)


def first_step():
    return pl.program_id(0) == 0


def tile_rows():
    return pl.ds(pl.multiple_of(pl.program_id(0) * TILE, TILE), TILE)


def gather_rows(flag_ref, q, pieces, before, score_ref, top_ref, total_ref, mixed_ref):
    def add_up(weights, values, total, mixed):
        for lane in range(0, weights.shape[1], 128):
            total += weights[:, lane : lane + 128]
        mixed += jnp.dot(weights.astype(jnp.bfloat16), values, preferred_element_type=jnp.float32)
        return total, mixed

    zeros = jnp.zeros((TILE, 128), jnp.float32)

    @pl.when(flag_ref[0] == 1)
    def _():
        total, mixed = zeros, zeros
        for keys, values, valid in pieces:
            scores = lax.dot_general(q, keys, DIMS, preferred_element_type=jnp.float32)
            if valid is not None:
                index = lax.broadcasted_iota(jnp.int32, scores.shape, 1)
                scores = jnp.where(index < valid, scores, -jnp.inf)
            total, mixed = add_up(jnp.exp2(scores * EXP_SCALE), values, total, mixed)
        top_ref[...] = zeros
        total_ref[...] = total
        mixed_ref[...] = mixed

    @pl.when(flag_ref[0] != 1)
    def _():
        top = jnp.full((TILE, 128), -jnp.inf, jnp.float32)
        column = 0
        for keys, _, valid in pieces:
            if valid is None:
                top = score_keys(q, keys, score_ref, column, top)
            else:
                top = score_text(q, keys, valid, score_ref, column, top)
            column += keys.shape[0]
        top = jnp.max(top, axis=1, keepdims=True) * EXP_SCALE
        if before is not None:
            top = jnp.maximum(top, before)
        total, mixed = zeros, zeros
        column = 0
        for _, values, _ in pieces:
            stop = column + values.shape[0]
            weights = jnp.exp2(score_ref[:, column:stop] * EXP_SCALE - top)
            total, mixed = add_up(weights, values, total, mixed)
            column = stop
        top_ref[...] = jnp.broadcast_to(top, (TILE, 128))
        total_ref[...] = total
        mixed_ref[...] = mixed


def set_piece(ref):
    return set_keys(ref), set_values(ref), None


def attend_near_kernel(
    where_ref, flag_ref, q_ref, own_ref, core_ref, text_ref, w_hbm,
    mixed_ref, total_ref, top_ref, q_out_ref, w_ref, score_ref, sem,
):
    copy = pltpu.make_async_copy(w_hbm, w_ref, sem)

    @pl.when(first_step())
    def _():
        copy.start()

    q = q_ref[...].reshape(TILE, HD)
    text = (text_ref[0, 0], text_ref[1, 0], where_ref[2])
    here = tile_rows()
    gather_rows(
        flag_ref, q, [set_piece(own_ref), set_piece(core_ref), text], None, score_ref,
        top_ref.at[here], total_ref.at[here], mixed_ref.at[here],
    )
    q_out_ref[here, :] = q

    @pl.when(pl.program_id(0) == SET // TILE - 1)
    def _():
        copy.wait()


STATE = (pltpu.VMEM((SET, HD), jnp.float32),) * 3


def attend_near(where, flag, received, own, core, text_kv, w_out):
    return pl.pallas_call(
        attend_near_kernel,
        out_shape=STATE + (pltpu.VMEM((SET, HD), jnp.bfloat16), pltpu.VMEM(w_out.shape, w_out.dtype)),
        grid_spec=pltpu.PrefetchScalarGridSpec(
            num_scalar_prefetch=2,
            grid=(SET // TILE,),
            in_specs=[
                pl.BlockSpec((QUAD, TOK, HD), lambda i, w, f: (i, 2, 0)),
                whole((RING, 2 * TOK, HD)),
                whole((RING, 2 * TOK, HD)),
                pl.BlockSpec((2, 1, TXT, HD), lambda i, w, f: (0, w[0], 0, w[1])),
                pl.BlockSpec(memory_space=pltpu.HBM),
            ],
            out_specs=(IN_VMEM,) * 5,
            scratch_shapes=[
                pltpu.VMEM((TILE, 2 * SET + TXT), jnp.float32),
                pltpu.SemaphoreType.DMA(()),
            ],
        ),
        compiler_params=pltpu.CompilerParams(vmem_limit_bytes=18 * MIB),
        cost_estimate=pl.CostEstimate(
            flops=4 * SET * 2304 * HD, bytes_accessed=3_000_000, transcendentals=SET * 2304
        ),
        name="attend_near",
    )(where, flag, received, own, core, text_kv, w_out)


LAST_KEYS = QUAD * TOK + 128


def lay_last_kernel(where_ref, *refs):
    last_refs = refs[:QUAD]
    text_ref, own_text_ref, gain_ref, keys_ref, value_ref, flag_ref = refs[QUAD:]
    for n, ref in enumerate(last_refs):
        keys_ref[n * TOK : (n + 1) * TOK, :] = ref[0:TOK, :]
    keys_ref[QUAD * TOK :, :] = text_ref[0, 0]
    lay_values(value_ref, [ref[TOK : 2 * TOK, :] for ref in last_refs] + [text_ref[1, 0]])
    room = 1.03 * HD
    gains = gain_ref[...] * gain_ref[...]
    text = own_text_ref[0, 0].astype(jnp.float32)
    key_norm = jnp.maximum(
        room * jnp.max(gains[1:2]), jnp.max(jnp.sum(text * text, axis=1, keepdims=True))
    )
    bound = EXP_SCALE * EXP_SCALE * room * jnp.max(gains[0:1]) * key_norm
    flag_ref[0] = jnp.where(bound < MOST_LOG2 * MOST_LOG2, 1, 0)


MOST_LOG2 = 90.0


def lay_last(where, lasts, text_kv, gains):
    return pl.pallas_call(
        lay_last_kernel,
        out_shape=(
            jax.ShapeDtypeStruct((LAST_KEYS, HD), jnp.bfloat16),
            jax.ShapeDtypeStruct((LAST_KEYS, 2 * HD), jnp.bfloat16),
            jax.ShapeDtypeStruct((1,), jnp.int32),
        ),
        grid_spec=pltpu.PrefetchScalarGridSpec(
            num_scalar_prefetch=1,
            grid=(1,),
            in_specs=[whole((2 * TOK, HD)) for _ in lasts]
            + [
                pl.BlockSpec(
                    (2, 1, 128, HD), lambda i, w: (0, BRANCH - 1, w[4], HEADS_HERE - 1)
                ),
                pl.BlockSpec((1, 1, TXT, HD), lambda i, w: (0, w[0], 0, w[1])),
                whole((2, HD)),
            ],
            out_specs=(
                whole((LAST_KEYS, HD)),
                whole((LAST_KEYS, 2 * HD)),
                pl.BlockSpec(memory_space=pltpu.SMEM),
            ),
        ),
        compiler_params=pltpu.CompilerParams(vmem_limit_bytes=16 * MIB),
        cost_estimate=pl.CostEstimate(
            flops=10_000_000_000, bytes_accessed=10_000_000, transcendentals=0
        ),
        name="lay_last",
    )(where, *lasts, text_kv, text_kv, gains)


def attend_last_kernel(where_ref, q_ref, keys_ref, value_ref, out_ref, score_ref):
    video_keys = QUAD * TOK
    q = q_ref[...].reshape(TILE, HD)
    top = jnp.full((TILE, 128), -jnp.inf, jnp.float32)
    top = score_keys(q, keys_ref[0:video_keys, :], score_ref, 0, top)
    top = score_text(q, keys_ref[video_keys:, :], where_ref[3], score_ref, video_keys, top)
    top = jnp.max(top, axis=1, keepdims=True) * EXP_SCALE
    mixed = mix(score_ref, value_ref, top, LAST_KEYS)
    total = mixed[:, HD : HD + 1]
    result = mixed[:, :HD] / total
    first = pl.program_id(0) * QUAD
    out_ref[pl.ds(first, QUAD), 0:TOK, :] = result.astype(jnp.bfloat16).reshape(QUAD, TOK, HD)
    level = jnp.broadcast_to(top + jnp.log(total) * LOG2E, (TILE, HD))
    for f in range(QUAD):
        row = jnp.transpose(level[f * TOK : (f + 1) * TOK])[0:1]
        stats = limbs_of(row) + [jnp.zeros((STAT_ROWS - 3, HD), jnp.float32)]
        out_ref[first + f, TOK:LAST_ROWS, :] = jnp.concatenate(stats, axis=0).astype(jnp.bfloat16)


def attend_last(where, received, keys, values):
    return pl.pallas_call(
        attend_last_kernel,
        out_shape=pltpu.VMEM((RING, LAST_ROWS, HD), jnp.bfloat16),
        grid_spec=pltpu.PrefetchScalarGridSpec(
            num_scalar_prefetch=1,
            grid=(SET // TILE,),
            in_specs=[
                pl.BlockSpec((QUAD, TOK, HD), lambda i, w: (i, 3, 0)),
                whole((LAST_KEYS, HD)),
                whole((LAST_KEYS, 2 * HD)),
            ],
            out_specs=IN_VMEM,
            scratch_shapes=[pltpu.VMEM((TILE, LAST_KEYS), jnp.float32)],
        ),
        compiler_params=pltpu.CompilerParams(vmem_limit_bytes=16 * MIB),
        cost_estimate=pl.CostEstimate(
            flops=4 * SET * 640 * HD, bytes_accessed=1_000_000, transcendentals=SET * 640
        ),
        name="attend_last",
    )(where, received, keys, values)


def attend_far_kernel(finish, flag_ref, q_ref, set_ref, *refs):
    mixed_in, total_in, top_in, *refs = refs
    score_ref, top_ref, total_ref, mixed_ref = refs[-4:]
    here = tile_rows()
    before = top_in[here, 0:1]
    gather_rows(
        flag_ref, q_ref[here, :], [set_piece(set_ref)], before, score_ref,
        top_ref, total_ref, mixed_ref,
    )
    decay = jnp.exp2(before - top_ref[:, 0:1])
    total = total_ref[...] + total_in[here, :] * decay
    mixed = mixed_ref[...] + mixed_in[here, :] * decay
    if finish:
        last_ref, out_ref = refs[:2]
        result = (mixed / jnp.sum(total, axis=1, keepdims=True)).astype(jnp.bfloat16)
        frames = pl.ds(pl.program_id(0) * QUAD, QUAD)
        out_ref[frames, 0:TOK, :] = result.reshape(QUAD, TOK, HD)
        out_ref[frames, TOK:RETURN, :] = last_ref[frames]
    else:
        mixed_out, total_out, top_out = refs[:3]
        mixed_out[here, :] = mixed
        total_out[here, :] = total
        top_out[here, :] = top_ref[...]


def attend_far(flag, queries, keys, state, last=None):
    finish = last is not None
    operands = [queries, keys, *state] + ([last] if finish else [])
    return pl.pallas_call(
        functools.partial(attend_far_kernel, finish),
        out_shape=pltpu.VMEM((RING, RETURN, HD), jnp.bfloat16) if finish else STATE,
        grid_spec=pltpu.PrefetchScalarGridSpec(
            num_scalar_prefetch=1,
            grid=(SET // TILE,),
            in_specs=[IN_VMEM] * len(operands),
            out_specs=IN_VMEM if finish else (IN_VMEM,) * 3,
            scratch_shapes=[pltpu.VMEM((TILE, SET), jnp.float32)]
            + [pltpu.VMEM((TILE, 128), jnp.float32)] * 3,
        ),
        compiler_params=pltpu.CompilerParams(vmem_limit_bytes=16 * MIB),
        cost_estimate=pl.CostEstimate(
            flops=4 * SET * SET * HD, bytes_accessed=3_000_000, transcendentals=SET * SET
        ),
        name="attend_far",
    )(flag, *map(in_vmem, operands))


def output_kernel(place_ref, back_ref, w_ref, *refs):
    out_refs, attn_ref = refs[:-1], refs[-1]
    for p in range(RING):
        b, hd = divmod(p, HEADS_HERE)
        attn_ref[b * TOK : (b + 1) * TOK, hd * HD : (hd + 1) * HD] = back_ref[p, 0:TOK, :]
    levels = []
    for p in range(RING):
        stats = back_ref[p, 2 * TOK : RETURN, :].astype(jnp.float32)
        row = stats[0:1] + stats[1:2] + stats[2:3]
        levels.append(jnp.transpose(jnp.broadcast_to(row, (TOK, HD))))
    top = levels[0]
    for level in levels[1:]:
        top = jnp.maximum(top, level)
    total = jnp.zeros((TOK, HD), jnp.float32)
    mixed = jnp.zeros((TOK, HD), jnp.float32)
    for p, level in enumerate(levels):
        weight = jnp.exp2(level - top)
        total += weight
        mixed += weight * back_ref[p, TOK : 2 * TOK, :].astype(jnp.float32)
    attn_ref[(BRANCH - 1) * TOK :, (HEADS_HERE - 1) * HD :] = (mixed / total).astype(jnp.bfloat16)
    multiply(place_ref, EARLY, attn_ref, w_ref, out_refs)


EARLY = (4, 5, 7)
LATE = (2, 3, 0, 1, 6)


def multiply(place_ref, places, attn_ref, w_ref, out_refs):
    for s, out_ref in zip(places, out_refs):
        start = pl.multiple_of(place_ref[s] * DSH, DSH)
        out_ref[...] = jnp.dot(
            attn_ref[...], w_ref[:, pl.ds(start, DSH)], preferred_element_type=jnp.float32
        ).astype(jnp.bfloat16)


def late_kernel(place_ref, attn_ref, w_ref, *out_refs):
    multiply(place_ref, LATE, attn_ref, w_ref, out_refs)


def output(kernel, places, rows, w_out, count):
    return pl.pallas_call(
        kernel,
        out_shape=(pltpu.VMEM((ROWS, DSH), jnp.bfloat16),) * count,
        grid_spec=pltpu.PrefetchScalarGridSpec(
            num_scalar_prefetch=1,
            grid=(1,),
            in_specs=[IN_VMEM, IN_VMEM],
            out_specs=(IN_VMEM,) * count,
        ),
        compiler_params=pltpu.CompilerParams(vmem_limit_bytes=16 * MIB),
        cost_estimate=pl.CostEstimate(
            flops=2 * ROWS * DSH * DSH * count, bytes_accessed=3_000_000, transcendentals=0
        ),
        name="output",
    )(places, in_vmem(rows), in_vmem(w_out))


def head_move(x, step):
    return lax.ppermute(x, "head", [(i, (i + step) % HEAD_AXIS) for i in range(HEAD_AXIS)])


def head_partner(x):
    return lax.ppermute(x, "head", [(i, i ^ 1) for i in range(HEAD_AXIS)])


def frame_move(x, flip):
    return lax.ppermute(x, "frame", [(i, i ^ flip) for i in range(FRAMES)])


def gather_head(own):
    partner = head_partner(own)
    ahead = head_move(own, -2)
    behind = head_move(own, 2)
    opposite = [head_move(behind[:CUT], 2), head_move(ahead[CUT:], -2)]
    return [
        own,
        partner,
        ahead,
        behind,
        head_move(partner, -2),
        head_move(partner, 2),
        *opposite,
        *map(head_partner, opposite),
    ]


def add(*terms):
    total = terms[0].astype(jnp.float32)
    for term in terms[1:]:
        total += term.astype(jnp.float32)
    return total


def scatter_head(places, back, w_out):
    ahead, behind, over, attention = output(output_kernel, places, back, w_out, 4)
    for_partner = [head_move(ahead, 2), head_move(behind, -2)]
    for_opposite = head_partner(over)
    ahead, behind, own, partner, opposite = output(
        late_kernel, places, attention, w_out, len(LATE)
    )
    direct = [head_move(ahead, 2), head_move(behind, -2)]
    over_y = head_partner(add(partner, *for_partner).astype(jnp.bfloat16))
    across = head_move(add(opposite, for_opposite).astype(jnp.bfloat16), 4)
    return add(own, *direct, over_y, across)


def body(
    video, w_qkv, w_out, text_kv, text_lengths, norm_gains, mod_table, timestep_ids, queue_shift
):
    text_kv = in_hbm(text_kv)
    frame = lax.axis_index("frame").astype(jnp.int32)
    head = lax.axis_index("head").astype(jnp.int32)
    own, gate, gains, places, where = prep(
        frame.reshape(1),
        head.reshape(1),
        queue_shift,
        in_hbm(timestep_ids),
        in_hbm(text_lengths),
        in_hbm(video),
        in_hbm(mod_table.transpose(1, 0, 2)),
        in_hbm(norm_gains),
    )
    cosine, sine = rope_tables(frame)
    blocks = gather_head(own)
    weights = in_hbm(w_qkv.transpose(1, 0, 2))
    send, last = project(places, blocks, weights, gains, cosine, sine)
    rings = [[(y * RING + z) * 2 + core for z in range(RING)] for y in range(2) for core in range(2)]

    def over_rings(x):
        return lax.all_to_all(x, "frame", 0, 0, axis_index_groups=rings, tiled=True)

    received = over_rings(send)
    flips = (1, FRAMES // 2, FRAMES // 2 + 1)
    lasts = [last] + [frame_move(last, flip) for flip in flips]
    last_keys, last_values, flag = lay_last(where, lasts, text_kv, gains)
    near = received[:, : 2 * TOK]
    over_y = frame_move(near, FRAMES // 2)
    near_later, last_keys = lax.optimization_barrier((near, last_keys))
    over_core = frame_move(near_later, 1)
    ninth = attend_last(where, received, last_keys, last_values)
    *state, queries, w_held = attend_near(
        where, flag, received, near, over_core, text_kv, in_hbm(w_out)
    )
    over_y, _, _ = lax.optimization_barrier((over_y, state[0], ninth))
    diagonal = frame_move(over_y, 1)
    state = attend_far(flag, queries, over_y, state)
    returned = attend_far(flag, queries, diagonal, state, ninth)
    back = over_rings(returned)
    proj = scatter_head(places, back, w_held).reshape(video.shape)
    return (video.astype(jnp.float32) + gate * proj).astype(jnp.bfloat16)


def solution(mesh):
    in_specs = (
        P(None, "frame", "head"),
        P(None, None, "head"),
        P("head", None),
        P(None, None, None, "head"),
        P(),
        P(),
        P(None, None, "head"),
        P(),
        P(),
    )
    out_specs = P(None, "frame", "head")
    return jax.shard_map(body, mesh=mesh, in_specs=in_specs, out_specs=out_specs, check_vma=False)
```

```python
import functools

import jax
import jax.numpy as jnp
import numpy as np
from jax import lax
from jax.experimental import pallas as pl
from jax.experimental.pallas import tpu as pltpu
from jax.sharding import PartitionSpec as P

HD = 128
TOK = 128
LAT_W = 16
FRAMES = 32
HEAD_AXIS = 8
BRANCH = 3
HEADS_HERE = 3
PAIRS = BRANCH * HEADS_HERE
DSH = 384
TXT = 256
RING = 8
ROWS = BRANCH * TOK
MOD_ROWS = 16
SENT = ROWS + MOD_ROWS
CUT = ROWS // 2
LAST = PAIRS - 1
STAT_ROWS = 16
LAST_ROWS = TOK + STAT_ROWS
RETURN = TOK + LAST_ROWS
WIDE = 3 * DSH
W_PARTS = 4
W_ROWS = HEAD_AXIS * DSH // W_PARTS
rope_base = 256.0
norm_eps = 1e-06
LOG2E = float(np.log2(np.e))
EXP_SCALE = float(HD ** (-0.5) * np.log2(np.e))
MIB = 1024 * 1024


def whole(shape):
    return pl.BlockSpec(shape, lambda *_: (0,) * len(shape))


IN_VMEM = pl.BlockSpec(memory_space=pltpu.VMEM)


def in_vmem(x):
    return pltpu.with_memory_space_constraint(x, pltpu.VMEM)


def in_hbm(x):
    return pltpu.with_memory_space_constraint(x, pltpu.HBM)


def limbs_of(value):
    limbs = []
    for _ in range(3):
        limb = value.astype(jnp.bfloat16).astype(jnp.float32)
        limbs.append(limb)
        value = value - limb
    return limbs


def rope_tables(frame):
    time_dims = HD // 8
    space_dims = (HD - time_dims) // 2
    freq = np.concatenate(
        [
            np.repeat(rope_base ** (-np.arange(0, z, 2, dtype=np.float64) / z), 2)
            for z in (time_dims, space_dims, space_dims)
        ]
    ).astype(np.float32)
    section = np.repeat(np.arange(3), (time_dims, space_dims, space_dims))
    token = jnp.arange(TOK, dtype=jnp.int32)[:, None]
    section = jnp.asarray(section)[None, :]
    position = jnp.where(
        section == 0, frame, jnp.where(section == 1, token // LAT_W, token % LAT_W)
    )
    angle = position.astype(jnp.float32) * jnp.asarray(freq)[None, :]
    sign = jnp.asarray(np.tile(np.array([-1.0, 1.0], np.float32), HD // 2))
    return jnp.cos(angle), jnp.sin(angle) * sign[None, :]


def prep_kernel(
    frame_ref, head_ref, shift_ref, ids_ref, lengths_ref, video_ref, table_ref, gain_ref,
    own_ref, gate_ref, gain_out_ref, place_ref, where_ref,
):
    head = head_ref[0]
    for s, step in enumerate((0, 0, 2, -2, 2, -2, 4, 4)):
        near = lax.rem(head + step + HEAD_AXIS, HEAD_AXIS)
        place_ref[s] = near if s in (0, 2, 3, 6) else near + 1 - 2 * lax.rem(near, 2)
    slab = lax.rem(lax.div(frame_ref[0], 2), RING)
    branch = lax.div(slab, HEADS_HERE)
    text_block = jnp.minimum(slab, 1)
    where_ref[0] = branch
    where_ref[1] = lax.rem(slab, HEADS_HERE)
    where_ref[2] = lengths_ref[branch]
    where_ref[3] = jnp.where(slab < 2, lengths_ref[BRANCH - 1] - 128 * text_block, 0)
    where_ref[4] = text_block
    level = ids_ref[lax.rem(frame_ref[0] + shift_ref[0], FRAMES)]
    looked = [table_ref[part, pl.ds(level, 1), :] for part in range(3)]
    gate_ref[...] = looked[2]
    gain_out_ref[...] = gain_ref[...]
    limbs = limbs_of(looked[0]) + limbs_of(looked[1])
    limbs.append(jnp.zeros((MOD_ROWS - 6, DSH), jnp.float32))
    for b in range(BRANCH):
        own_ref[b * TOK : (b + 1) * TOK, :] = video_ref[b]
    own_ref[ROWS:SENT, :] = jnp.concatenate(limbs, axis=0).astype(jnp.bfloat16)


def prep(frame, head, queue_shift, timestep_ids, lengths, video, table, gains):
    return pl.pallas_call(
        prep_kernel,
        out_shape=(
            pltpu.VMEM((SENT, DSH), jnp.bfloat16),
            jax.ShapeDtypeStruct((1, DSH), jnp.float32),
            pltpu.VMEM((2, HD), jnp.float32),
            jax.ShapeDtypeStruct((HEAD_AXIS,), jnp.int32),
            jax.ShapeDtypeStruct((5,), jnp.int32),
        ),
        grid_spec=pltpu.PrefetchScalarGridSpec(
            num_scalar_prefetch=5,
            grid=(1,),
            in_specs=[whole((BRANCH, TOK, DSH)), whole((3, FRAMES, DSH)), whole((2, HD))],
            out_specs=(
                IN_VMEM,
                whole((1, DSH)),
                IN_VMEM,
                pl.BlockSpec(memory_space=pltpu.SMEM),
                pl.BlockSpec(memory_space=pltpu.SMEM),
            ),
        ),
        compiler_params=pltpu.CompilerParams(vmem_limit_bytes=16 * MIB),
        name="prep",
    )(frame, head, queue_shift, timestep_ids, lengths, video, table, gains)


def project_kernel(place_ref, *refs):
    blocks, parts = refs[:6], refs[6:10]
    (
        w_hbm, gain_ref, cos_ref, sin_ref, out_ref, last_ref, mod_ref, acc_ref, w_ref, sems,
    ) = refs[10:]
    copies = []
    for n in range(3):
        for r in range(W_PARTS):
            rows = pl.ds(r * W_ROWS, W_ROWS)
            copies.append(
                pltpu.make_async_copy(
                    w_hbm.at[n, rows], w_ref.at[rows, pl.ds(n * DSH, DSH)], sems.at[n, r]
                )
            )
    for copy in copies:
        copy.start()
    limbs = [block[ROWS:SENT, :] for block in blocks]
    limbs += [parts[n][ROWS - CUT : SENT - CUT, :] for n in (1, 3)]
    mods = []
    for limb in limbs:
        limb = limb.astype(jnp.float32)
        shift = limb[0:1] + limb[1:2] + limb[2:3]
        mods.append((shift, 1.0 + (limb[3:4] + limb[4:5] + limb[5:6])))
    step = 64
    for first in (0, CUT):
        late = 1 if first else 0

        def chunk(n, carry):
            there = pl.ds(pl.multiple_of(n * step, step), step)
            here = pl.ds(pl.multiple_of(first + n * step, step), step)
            sources = [(block, here) for block in blocks]
            sources += [(parts[late], there), (parts[2 + late], there)]
            total = jnp.zeros((step, 128), jnp.float32)
            square = jnp.zeros((step, 128), jnp.float32)
            for ref, rows in sources:
                for lane in range(0, DSH, 128):
                    x = ref[rows, lane : lane + 128].astype(jnp.float32)
                    total += x
                    square += x * x
            mean = jnp.sum(total, axis=1, keepdims=True) / (HEAD_AXIS * DSH)
            var = jnp.sum(square, axis=1, keepdims=True) / (HEAD_AXIS * DSH) - mean * mean
            inv = lax.rsqrt(var + norm_eps)
            for s, (ref, rows) in enumerate(sources):
                shift, scale = mods[s]
                y = (ref[rows, :].astype(jnp.float32) - mean) * inv * scale + shift
                start = pl.multiple_of(place_ref[s] * DSH, DSH)
                mod_ref[here, pl.ds(start, DSH)] = y.astype(jnp.bfloat16)
            return carry

        lax.fori_loop(0, CUT // step, chunk, 0)

    def piece(part, p):
        b, hd = divmod(p, HEADS_HERE)
        lane = part * DSH + hd * HD
        return acc_ref[b * TOK : (b + 1) * TOK, lane : lane + HD]

    def turned(part, p):
        t = piece(part, p)
        t = t * lax.rsqrt(jnp.mean(t * t, axis=1, keepdims=True) + norm_eps)
        t = t * gain_ref[part : part + 1, :]
        even = lax.broadcasted_iota(jnp.int32, t.shape, 1) % 2 == 0
        other = jnp.where(even, pltpu.roll(t, HD - 1, 1), pltpu.roll(t, 1, 1))
        return (t * cos_ref[...] + other * sin_ref[...]).astype(jnp.bfloat16)

    for copy in copies:
        copy.wait()
    acc_ref[...] = jnp.dot(mod_ref[...], w_ref[...], preferred_element_type=jnp.float32)
    for part in range(3):
        for p in range(PAIRS):
            if part == 2:
                result = piece(part, p).astype(jnp.bfloat16)
            else:
                result = turned(part, p)
            if part == 0 and p == LAST:
                for n in range(RING):
                    out_ref[n, 3 * TOK : 4 * TOK, :] = result
            elif part == 0:
                out_ref[p, 2 * TOK : 3 * TOK, :] = result
            elif p == LAST:
                last_ref[(part - 1) * TOK : part * TOK, :] = result
            else:
                out_ref[p, (part - 1) * TOK : part * TOK, :] = result


def project(places, blocks, w, gains, cosine, sine):
    return pl.pallas_call(
        project_kernel,
        out_shape=(
            pltpu.VMEM((RING, 4 * TOK, HD), jnp.bfloat16),
            pltpu.VMEM((2 * TOK, HD), jnp.bfloat16),
        ),
        grid_spec=pltpu.PrefetchScalarGridSpec(
            num_scalar_prefetch=1,
            grid=(1,),
            in_specs=[IN_VMEM] * len(blocks)
            + [pl.BlockSpec(memory_space=pltpu.HBM), IN_VMEM, IN_VMEM, IN_VMEM],
            out_specs=(IN_VMEM, IN_VMEM),
            scratch_shapes=[
                pltpu.VMEM((ROWS, HEAD_AXIS * DSH), jnp.bfloat16),
                pltpu.VMEM((ROWS, WIDE), jnp.float32),
                pltpu.VMEM((HEAD_AXIS * DSH, WIDE), jnp.bfloat16),
                pltpu.SemaphoreType.DMA((3, W_PARTS)),
            ],
        ),
        compiler_params=pltpu.CompilerParams(vmem_limit_bytes=28 * MIB),
        cost_estimate=pl.CostEstimate(
            flops=2 * ROWS * HEAD_AXIS * DSH * 3 * DSH, bytes_accessed=12_000_000, transcendentals=0
        ),
        name="project",
    )(places, *map(in_vmem, blocks), w, *map(in_vmem, (gains, cosine, sine)))


QUAD = 4
TILE = QUAD * TOK
SET = RING * TOK
DIMS = (((1,), (1,)), ((), ()))


def score_keys(q, keys, score_ref, column, top):
    scores = lax.dot_general(q, keys, DIMS, preferred_element_type=jnp.float32)
    score_ref[:, column : column + scores.shape[1]] = scores
    for lane in range(0, scores.shape[1], 128):
        top = jnp.maximum(top, scores[:, lane : lane + 128])
    return top


def score_text(q, keys, valid, score_ref, column, top):
    scores = lax.dot_general(q, keys, DIMS, preferred_element_type=jnp.float32)
    index = lax.broadcasted_iota(jnp.int32, scores.shape, 1)
    scores = jnp.where(index < valid, scores, -jnp.inf)
    score_ref[:, column : column + scores.shape[1]] = scores
    for lane in range(0, scores.shape[1], 128):
        top = jnp.maximum(top, scores[:, lane : lane + 128])
    return top


def mix(score_ref, value_ref, top, count):
    mixed = jnp.zeros((TILE, 2 * HD), jnp.float32)
    for first in range(0, count, SET):
        stop = min(first + SET, count)
        weights = jnp.exp2(score_ref[:, first:stop] * EXP_SCALE - top).astype(jnp.bfloat16)
        mixed += jnp.dot(weights, value_ref[first:stop, :], preferred_element_type=jnp.float32)
    return mixed


def lay_values(value_ref, pieces):
    lane = lax.broadcasted_iota(jnp.int32, (value_ref.shape[0], HD), 1)
    value_ref[:, HD:] = jnp.where(lane == 0, 1.0, 0.0).astype(jnp.bfloat16)
    row = 0
    for piece in pieces:
        value_ref[row : row + piece.shape[0], :HD] = piece
        row += piece.shape[0]


def set_keys(ref):
    return ref[:, 0:TOK, :].reshape(SET, HD)


def set_values(ref):
    return ref[:, TOK : 2 * TOK, :].reshape(SET, HD)


def first_step():
    return pl.program_id(0) == 0


def tile_rows():
    return pl.ds(pl.multiple_of(pl.program_id(0) * TILE, TILE), TILE)


def gather_rows(flag_ref, q, pieces, before, score_ref, top_ref, total_ref, mixed_ref):
    def add_up(weights, values, total, mixed):
        for lane in range(0, weights.shape[1], 128):
            total += weights[:, lane : lane + 128]
        mixed += jnp.dot(weights.astype(jnp.bfloat16), values, preferred_element_type=jnp.float32)
        return total, mixed

    zeros = jnp.zeros((TILE, 128), jnp.float32)

    @pl.when(flag_ref[0] == 1)
    def _():
        total, mixed = zeros, zeros
        for keys, values, valid in pieces:
            scores = lax.dot_general(q, keys, DIMS, preferred_element_type=jnp.float32)
            if valid is not None:
                index = lax.broadcasted_iota(jnp.int32, scores.shape, 1)
                scores = jnp.where(index < valid, scores, -jnp.inf)
            total, mixed = add_up(jnp.exp2(scores * EXP_SCALE), values, total, mixed)
        top_ref[...] = zeros
        total_ref[...] = total
        mixed_ref[...] = mixed

    @pl.when(flag_ref[0] != 1)
    def _():
        top = jnp.full((TILE, 128), -jnp.inf, jnp.float32)
        column = 0
        for keys, _, valid in pieces:
            if valid is None:
                top = score_keys(q, keys, score_ref, column, top)
            else:
                top = score_text(q, keys, valid, score_ref, column, top)
            column += keys.shape[0]
        top = jnp.max(top, axis=1, keepdims=True) * EXP_SCALE
        if before is not None:
            top = jnp.maximum(top, before)
        total, mixed = zeros, zeros
        column = 0
        for _, values, _ in pieces:
            stop = column + values.shape[0]
            weights = jnp.exp2(score_ref[:, column:stop] * EXP_SCALE - top)
            total, mixed = add_up(weights, values, total, mixed)
            column = stop
        top_ref[...] = jnp.broadcast_to(top, (TILE, 128))
        total_ref[...] = total
        mixed_ref[...] = mixed


def set_piece(ref):
    return set_keys(ref), set_values(ref), None


def attend_near_kernel(
    where_ref, flag_ref, q_ref, own_ref, core_ref, text_ref, w_hbm,
    mixed_ref, total_ref, top_ref, q_out_ref, w_ref, score_ref, sem,
):
    copy = pltpu.make_async_copy(w_hbm, w_ref, sem)

    @pl.when(first_step())
    def _():
        copy.start()

    q = q_ref[...].reshape(TILE, HD)
    text = (text_ref[0, 0], text_ref[1, 0], where_ref[2])
    here = tile_rows()
    gather_rows(
        flag_ref, q, [set_piece(own_ref), set_piece(core_ref), text], None, score_ref,
        top_ref.at[here], total_ref.at[here], mixed_ref.at[here],
    )
    q_out_ref[here, :] = q

    @pl.when(pl.program_id(0) == SET // TILE - 1)
    def _():
        copy.wait()


STATE = (pltpu.VMEM((SET, HD), jnp.float32),) * 3


def attend_near(where, flag, received, own, core, text_kv, w_out):
    return pl.pallas_call(
        attend_near_kernel,
        out_shape=STATE + (pltpu.VMEM((SET, HD), jnp.bfloat16), pltpu.VMEM(w_out.shape, w_out.dtype)),
        grid_spec=pltpu.PrefetchScalarGridSpec(
            num_scalar_prefetch=2,
            grid=(SET // TILE,),
            in_specs=[
                pl.BlockSpec((QUAD, TOK, HD), lambda i, w, f: (i, 2, 0)),
                whole((RING, 2 * TOK, HD)),
                whole((RING, 2 * TOK, HD)),
                pl.BlockSpec((2, 1, TXT, HD), lambda i, w, f: (0, w[0], 0, w[1])),
                pl.BlockSpec(memory_space=pltpu.HBM),
            ],
            out_specs=(IN_VMEM,) * 5,
            scratch_shapes=[
                pltpu.VMEM((TILE, 2 * SET + TXT), jnp.float32),
                pltpu.SemaphoreType.DMA(()),
            ],
        ),
        compiler_params=pltpu.CompilerParams(vmem_limit_bytes=18 * MIB),
        cost_estimate=pl.CostEstimate(
            flops=4 * SET * 2304 * HD, bytes_accessed=3_000_000, transcendentals=SET * 2304
        ),
        name="attend_near",
    )(where, flag, received, own, core, text_kv, w_out)


LAST_KEYS = QUAD * TOK + 128


def lay_last_kernel(where_ref, *refs):
    last_refs = refs[:QUAD]
    text_ref, own_text_ref, gain_ref, keys_ref, value_ref, flag_ref = refs[QUAD:]
    for n, ref in enumerate(last_refs):
        keys_ref[n * TOK : (n + 1) * TOK, :] = ref[0:TOK, :]
    keys_ref[QUAD * TOK :, :] = text_ref[0, 0]
    lay_values(value_ref, [ref[TOK : 2 * TOK, :] for ref in last_refs] + [text_ref[1, 0]])
    room = 1.03 * HD
    gains = gain_ref[...] * gain_ref[...]
    text = own_text_ref[0, 0].astype(jnp.float32)
    key_norm = jnp.maximum(
        room * jnp.max(gains[1:2]), jnp.max(jnp.sum(text * text, axis=1, keepdims=True))
    )
    bound = EXP_SCALE * EXP_SCALE * room * jnp.max(gains[0:1]) * key_norm
    flag_ref[0] = jnp.where(bound < MOST_LOG2 * MOST_LOG2, 1, 0)


MOST_LOG2 = 90.0


def lay_last(where, lasts, text_kv, gains):
    return pl.pallas_call(
        lay_last_kernel,
        out_shape=(
            jax.ShapeDtypeStruct((LAST_KEYS, HD), jnp.bfloat16),
            jax.ShapeDtypeStruct((LAST_KEYS, 2 * HD), jnp.bfloat16),
            jax.ShapeDtypeStruct((1,), jnp.int32),
        ),
        grid_spec=pltpu.PrefetchScalarGridSpec(
            num_scalar_prefetch=1,
            grid=(1,),
            in_specs=[whole((2 * TOK, HD)) for _ in lasts]
            + [
                pl.BlockSpec(
                    (2, 1, 128, HD), lambda i, w: (0, BRANCH - 1, w[4], HEADS_HERE - 1)
                ),
                pl.BlockSpec((1, 1, TXT, HD), lambda i, w: (0, w[0], 0, w[1])),
                whole((2, HD)),
            ],
            out_specs=(
                whole((LAST_KEYS, HD)),
                whole((LAST_KEYS, 2 * HD)),
                pl.BlockSpec(memory_space=pltpu.SMEM),
            ),
        ),
        compiler_params=pltpu.CompilerParams(vmem_limit_bytes=16 * MIB),
        cost_estimate=pl.CostEstimate(
            flops=10_000_000_000, bytes_accessed=10_000_000, transcendentals=0
        ),
        name="lay_last",
    )(where, *lasts, text_kv, text_kv, gains)


def attend_last_kernel(where_ref, q_ref, keys_ref, value_ref, out_ref, score_ref):
    video_keys = QUAD * TOK
    q = q_ref[...].reshape(TILE, HD)
    top = jnp.full((TILE, 128), -jnp.inf, jnp.float32)
    top = score_keys(q, keys_ref[0:video_keys, :], score_ref, 0, top)
    top = score_text(q, keys_ref[video_keys:, :], where_ref[3], score_ref, video_keys, top)
    top = jnp.max(top, axis=1, keepdims=True) * EXP_SCALE
    mixed = mix(score_ref, value_ref, top, LAST_KEYS)
    total = mixed[:, HD : HD + 1]
    result = mixed[:, :HD] / total
    first = pl.program_id(0) * QUAD
    out_ref[pl.ds(first, QUAD), 0:TOK, :] = result.astype(jnp.bfloat16).reshape(QUAD, TOK, HD)
    level = jnp.broadcast_to(top + jnp.log(total) * LOG2E, (TILE, HD))
    for f in range(QUAD):
        row = jnp.transpose(level[f * TOK : (f + 1) * TOK])[0:1]
        stats = limbs_of(row) + [jnp.zeros((STAT_ROWS - 3, HD), jnp.float32)]
        out_ref[first + f, TOK:LAST_ROWS, :] = jnp.concatenate(stats, axis=0).astype(jnp.bfloat16)


def attend_last(where, received, keys, values):
    return pl.pallas_call(
        attend_last_kernel,
        out_shape=pltpu.VMEM((RING, LAST_ROWS, HD), jnp.bfloat16),
        grid_spec=pltpu.PrefetchScalarGridSpec(
            num_scalar_prefetch=1,
            grid=(SET // TILE,),
            in_specs=[
                pl.BlockSpec((QUAD, TOK, HD), lambda i, w: (i, 3, 0)),
                whole((LAST_KEYS, HD)),
                whole((LAST_KEYS, 2 * HD)),
            ],
            out_specs=IN_VMEM,
            scratch_shapes=[pltpu.VMEM((TILE, LAST_KEYS), jnp.float32)],
        ),
        compiler_params=pltpu.CompilerParams(vmem_limit_bytes=16 * MIB),
        cost_estimate=pl.CostEstimate(
            flops=4 * SET * 640 * HD, bytes_accessed=1_000_000, transcendentals=SET * 640
        ),
        name="attend_last",
    )(where, received, keys, values)


def attend_far_kernel(finish, flag_ref, q_ref, set_ref, *refs):
    mixed_in, total_in, top_in, *refs = refs
    score_ref, top_ref, total_ref, mixed_ref = refs[-4:]
    here = tile_rows()
    before = top_in[here, 0:1]
    gather_rows(
        flag_ref, q_ref[here, :], [set_piece(set_ref)], before, score_ref,
        top_ref, total_ref, mixed_ref,
    )
    decay = jnp.exp2(before - top_ref[:, 0:1])
    total = total_ref[...] + total_in[here, :] * decay
    mixed = mixed_ref[...] + mixed_in[here, :] * decay
    if finish:
        last_ref, out_ref = refs[:2]
        result = (mixed / jnp.sum(total, axis=1, keepdims=True)).astype(jnp.bfloat16)
        frames = pl.ds(pl.program_id(0) * QUAD, QUAD)
        out_ref[frames, 0:TOK, :] = result.reshape(QUAD, TOK, HD)
        out_ref[frames, TOK:RETURN, :] = last_ref[frames]
    else:
        mixed_out, total_out, top_out = refs[:3]
        mixed_out[here, :] = mixed
        total_out[here, :] = total
        top_out[here, :] = top_ref[...]


def attend_far(flag, queries, keys, state, last=None):
    finish = last is not None
    operands = [queries, keys, *state] + ([last] if finish else [])
    return pl.pallas_call(
        functools.partial(attend_far_kernel, finish),
        out_shape=pltpu.VMEM((RING, RETURN, HD), jnp.bfloat16) if finish else STATE,
        grid_spec=pltpu.PrefetchScalarGridSpec(
            num_scalar_prefetch=1,
            grid=(SET // TILE,),
            in_specs=[IN_VMEM] * len(operands),
            out_specs=IN_VMEM if finish else (IN_VMEM,) * 3,
            scratch_shapes=[pltpu.VMEM((TILE, SET), jnp.float32)]
            + [pltpu.VMEM((TILE, 128), jnp.float32)] * 3,
        ),
        compiler_params=pltpu.CompilerParams(vmem_limit_bytes=16 * MIB),
        cost_estimate=pl.CostEstimate(
            flops=4 * SET * SET * HD, bytes_accessed=3_000_000, transcendentals=SET * SET
        ),
        name="attend_far",
    )(flag, *map(in_vmem, operands))


def output_kernel(place_ref, back_ref, w_ref, *refs):
    out_refs, attn_ref = refs[:-1], refs[-1]
    for p in range(RING):
        b, hd = divmod(p, HEADS_HERE)
        attn_ref[b * TOK : (b + 1) * TOK, hd * HD : (hd + 1) * HD] = back_ref[p, 0:TOK, :]
    levels = []
    for p in range(RING):
        stats = back_ref[p, 2 * TOK : RETURN, :].astype(jnp.float32)
        row = stats[0:1] + stats[1:2] + stats[2:3]
        levels.append(jnp.transpose(jnp.broadcast_to(row, (TOK, HD))))
    top = levels[0]
    for level in levels[1:]:
        top = jnp.maximum(top, level)
    total = jnp.zeros((TOK, HD), jnp.float32)
    mixed = jnp.zeros((TOK, HD), jnp.float32)
    for p, level in enumerate(levels):
        weight = jnp.exp2(level - top)
        total += weight
        mixed += weight * back_ref[p, TOK : 2 * TOK, :].astype(jnp.float32)
    attn_ref[(BRANCH - 1) * TOK :, (HEADS_HERE - 1) * HD :] = (mixed / total).astype(jnp.bfloat16)
    multiply(place_ref, EARLY, attn_ref, w_ref, out_refs)


EARLY = (4, 5)
LATE = (7, 2, 3, 0, 1, 6)


def multiply(place_ref, places, attn_ref, w_ref, out_refs):
    for s, out_ref in zip(places, out_refs):
        start = pl.multiple_of(place_ref[s] * DSH, DSH)
        out_ref[...] = jnp.dot(
            attn_ref[...], w_ref[:, pl.ds(start, DSH)], preferred_element_type=jnp.float32
        ).astype(jnp.bfloat16)


def late_kernel(place_ref, attn_ref, w_ref, *out_refs):
    multiply(place_ref, LATE, attn_ref, w_ref, out_refs)


def output(kernel, places, rows, w_out, count):
    return pl.pallas_call(
        kernel,
        out_shape=(pltpu.VMEM((ROWS, DSH), jnp.bfloat16),) * count,
        grid_spec=pltpu.PrefetchScalarGridSpec(
            num_scalar_prefetch=1,
            grid=(1,),
            in_specs=[IN_VMEM, IN_VMEM],
            out_specs=(IN_VMEM,) * count,
        ),
        compiler_params=pltpu.CompilerParams(vmem_limit_bytes=16 * MIB),
        cost_estimate=pl.CostEstimate(
            flops=2 * ROWS * DSH * DSH * count, bytes_accessed=3_000_000, transcendentals=0
        ),
        name="output",
    )(places, in_vmem(rows), in_vmem(w_out))


def head_move(x, step):
    return lax.ppermute(x, "head", [(i, (i + step) % HEAD_AXIS) for i in range(HEAD_AXIS)])


def head_partner(x):
    return lax.ppermute(x, "head", [(i, i ^ 1) for i in range(HEAD_AXIS)])


def frame_move(x, flip):
    return lax.ppermute(x, "frame", [(i, i ^ flip) for i in range(FRAMES)])


def gather_head(own):
    partner = head_partner(own)
    ahead = head_move(own, -2)
    behind = head_move(own, 2)
    opposite = [head_move(behind[:CUT], 2), head_move(ahead[CUT:], -2)]
    return [
        own,
        partner,
        ahead,
        behind,
        head_move(partner, -2),
        head_move(partner, 2),
        *opposite,
        *map(head_partner, opposite),
    ]


def add(*terms):
    total = terms[0].astype(jnp.float32)
    for term in terms[1:]:
        total += term.astype(jnp.float32)
    return total


def scatter_head(places, back, w_out):
    ahead, behind, attention = output(output_kernel, places, back, w_out, 3)
    for_partner = [head_move(ahead, 2), head_move(behind, -2)]
    over, ahead, behind, own, partner, opposite = output(
        late_kernel, places, attention, w_out, len(LATE)
    )
    for_opposite = head_partner(over)
    direct = [head_move(ahead, 2), head_move(behind, -2)]
    over_y = head_partner(add(partner, *for_partner).astype(jnp.bfloat16))
    across = head_move(add(opposite, for_opposite).astype(jnp.bfloat16), 4)
    return add(own, *direct, over_y, across)


def body(
    video, w_qkv, w_out, text_kv, text_lengths, norm_gains, mod_table, timestep_ids, queue_shift
):
    text_kv = in_hbm(text_kv)
    frame = lax.axis_index("frame").astype(jnp.int32)
    head = lax.axis_index("head").astype(jnp.int32)
    own, gate, gains, places, where = prep(
        frame.reshape(1),
        head.reshape(1),
        queue_shift,
        in_hbm(timestep_ids),
        in_hbm(text_lengths),
        in_hbm(video),
        in_hbm(mod_table.transpose(1, 0, 2)),
        in_hbm(norm_gains),
    )
    cosine, sine = rope_tables(frame)
    blocks = gather_head(own)
    weights = in_hbm(w_qkv.transpose(1, 0, 2))
    send, last = project(places, blocks, weights, gains, cosine, sine)
    rings = [[(y * RING + z) * 2 + core for z in range(RING)] for y in range(2) for core in range(2)]

    def over_rings(x):
        return lax.all_to_all(x, "frame", 0, 0, axis_index_groups=rings, tiled=True)

    received = over_rings(send)
    flips = (1, FRAMES // 2, FRAMES // 2 + 1)
    lasts = [last] + [frame_move(last, flip) for flip in flips]
    last_keys, last_values, flag = lay_last(where, lasts, text_kv, gains)
    near = received[:, : 2 * TOK]
    over_y = frame_move(near, FRAMES // 2)
    near_later, last_keys = lax.optimization_barrier((near, last_keys))
    over_core = frame_move(near_later, 1)
    ninth = attend_last(where, received, last_keys, last_values)
    *state, queries, w_held = attend_near(
        where, flag, received, near, over_core, text_kv, in_hbm(w_out)
    )
    over_y, _, _ = lax.optimization_barrier((over_y, state[0], ninth))
    diagonal = frame_move(over_y, 1)
    state = attend_far(flag, queries, over_y, state)
    returned = attend_far(flag, queries, diagonal, state, ninth)
    back = over_rings(returned)
    proj = scatter_head(places, back, w_held).reshape(video.shape)
    return (video.astype(jnp.float32) + gate * proj).astype(jnp.bfloat16)


def solution(mesh):
    in_specs = (
        P(None, "frame", "head"),
        P(None, None, "head"),
        P("head", None),
        P(None, None, None, "head"),
        P(),
        P(),
        P(None, None, "head"),
        P(),
        P(),
    )
    out_specs = P(None, "frame", "head")
    return jax.shard_map(body, mesh=mesh, in_specs=in_specs, out_specs=out_specs, check_vma=False)
```

```python
import functools

import jax
import jax.numpy as jnp
import numpy as np
from jax import lax
from jax.experimental import pallas as pl
from jax.experimental.pallas import tpu as pltpu
from jax.sharding import PartitionSpec as P

HD = 128
TOK = 128
LAT_W = 16
FRAMES = 32
HEAD_AXIS = 8
BRANCH = 3
HEADS_HERE = 3
PAIRS = BRANCH * HEADS_HERE
DSH = 384
TXT = 256
RING = 8
ROWS = BRANCH * TOK
MOD_ROWS = 16
SENT = ROWS + MOD_ROWS
CUT = ROWS // 2
LAST = PAIRS - 1
STAT_ROWS = 16
LAST_ROWS = TOK + STAT_ROWS
RETURN = TOK + LAST_ROWS
WIDE = 3 * DSH
rope_base = 256.0
norm_eps = 1e-06
LOG2E = float(np.log2(np.e))
EXP_SCALE = float(HD ** (-0.5) * np.log2(np.e))
MIB = 1024 * 1024


def whole(shape):
    return pl.BlockSpec(shape, lambda *_: (0,) * len(shape))


IN_VMEM = pl.BlockSpec(memory_space=pltpu.VMEM)


def in_vmem(x):
    return pltpu.with_memory_space_constraint(x, pltpu.VMEM)


def in_hbm(x):
    return pltpu.with_memory_space_constraint(x, pltpu.HBM)


def limbs_of(value):
    limbs = []
    for _ in range(3):
        limb = value.astype(jnp.bfloat16).astype(jnp.float32)
        limbs.append(limb)
        value = value - limb
    return limbs


def rope_tables(frame):
    time_dims = HD // 8
    space_dims = (HD - time_dims) // 2
    freq = np.concatenate(
        [
            np.repeat(rope_base ** (-np.arange(0, z, 2, dtype=np.float64) / z), 2)
            for z in (time_dims, space_dims, space_dims)
        ]
    ).astype(np.float32)
    section = np.repeat(np.arange(3), (time_dims, space_dims, space_dims))
    token = jnp.arange(TOK, dtype=jnp.int32)[:, None]
    section = jnp.asarray(section)[None, :]
    position = jnp.where(
        section == 0, frame, jnp.where(section == 1, token // LAT_W, token % LAT_W)
    )
    angle = position.astype(jnp.float32) * jnp.asarray(freq)[None, :]
    sign = jnp.asarray(np.tile(np.array([-1.0, 1.0], np.float32), HD // 2))
    return jnp.cos(angle), jnp.sin(angle) * sign[None, :]


def prep_kernel(
    frame_ref, head_ref, shift_ref, ids_ref, lengths_ref, video_ref, table_ref, gain_ref,
    own_ref, gate_ref, gain_out_ref, place_ref, where_ref,
):
    head = head_ref[0]
    for s, step in enumerate((0, 0, 2, -2, 2, -2, 4, 4)):
        near = lax.rem(head + step + HEAD_AXIS, HEAD_AXIS)
        place_ref[s] = near if s in (0, 2, 3, 6) else near + 1 - 2 * lax.rem(near, 2)
    slab = lax.rem(lax.div(frame_ref[0], 2), RING)
    branch = lax.div(slab, HEADS_HERE)
    text_block = jnp.minimum(slab, 1)
    where_ref[0] = branch
    where_ref[1] = lax.rem(slab, HEADS_HERE)
    where_ref[2] = lengths_ref[branch]
    where_ref[3] = jnp.where(slab < 2, lengths_ref[BRANCH - 1] - 128 * text_block, 0)
    where_ref[4] = text_block
    level = ids_ref[lax.rem(frame_ref[0] + shift_ref[0], FRAMES)]
    looked = [table_ref[part, pl.ds(level, 1), :] for part in range(3)]
    gate_ref[...] = looked[2]
    gain_out_ref[...] = gain_ref[...]
    limbs = limbs_of(looked[0]) + limbs_of(looked[1])
    limbs.append(jnp.zeros((MOD_ROWS - 6, DSH), jnp.float32))
    for b in range(BRANCH):
        own_ref[b * TOK : (b + 1) * TOK, :] = video_ref[b]
    own_ref[ROWS:SENT, :] = jnp.concatenate(limbs, axis=0).astype(jnp.bfloat16)


def prep(frame, head, queue_shift, timestep_ids, lengths, video, table, gains):
    return pl.pallas_call(
        prep_kernel,
        out_shape=(
            pltpu.VMEM((SENT, DSH), jnp.bfloat16),
            jax.ShapeDtypeStruct((1, DSH), jnp.float32),
            pltpu.VMEM((2, HD), jnp.float32),
            jax.ShapeDtypeStruct((HEAD_AXIS,), jnp.int32),
            jax.ShapeDtypeStruct((5,), jnp.int32),
        ),
        grid_spec=pltpu.PrefetchScalarGridSpec(
            num_scalar_prefetch=5,
            grid=(1,),
            in_specs=[whole((BRANCH, TOK, DSH)), whole((3, FRAMES, DSH)), whole((2, HD))],
            out_specs=(
                IN_VMEM,
                whole((1, DSH)),
                IN_VMEM,
                pl.BlockSpec(memory_space=pltpu.SMEM),
                pl.BlockSpec(memory_space=pltpu.SMEM),
            ),
        ),
        compiler_params=pltpu.CompilerParams(vmem_limit_bytes=16 * MIB),
        name="prep",
    )(frame, head, queue_shift, timestep_ids, lengths, video, table, gains)


def project_kernel(place_ref, *refs):
    blocks, parts = refs[:6], refs[6:10]
    (
        w_hbm, gain_ref, cos_ref, sin_ref, out_ref, last_ref, early_ref, late_ref, acc_ref, w_ref, sems,
    ) = refs[10:]
    copies = [
        pltpu.make_async_copy(w_hbm.at[n], w_ref.at[:, pl.ds(n * DSH, DSH)], sems.at[n])
        for n in range(3)
    ]
    for copy in copies:
        copy.start()
    limbs = [block[ROWS:SENT, :] for block in blocks]
    limbs += [parts[n][ROWS - CUT : SENT - CUT, :] for n in (1, 3)]
    mods = []
    for limb in limbs:
        limb = limb.astype(jnp.float32)
        shift = limb[0:1] + limb[1:2] + limb[2:3]
        mods.append((shift, 1.0 + (limb[3:4] + limb[4:5] + limb[5:6])))
    step = 64

    def normalize(late, n, mod_ref):
        there = pl.ds(n * step if isinstance(n, int) else pl.multiple_of(n * step, step), step)
        here = there if not late else pl.ds(CUT + n * step, step)
        sources = [(block, here) for block in blocks]
        sources += [(parts[late], there), (parts[2 + late], there)]
        total = jnp.zeros((step, 128), jnp.float32)
        square = jnp.zeros((step, 128), jnp.float32)
        for ref, rows in sources:
            for lane in range(0, DSH, 128):
                x = ref[rows, lane : lane + 128].astype(jnp.float32)
                total += x
                square += x * x
        mean = jnp.sum(total, axis=1, keepdims=True) / (HEAD_AXIS * DSH)
        var = jnp.sum(square, axis=1, keepdims=True) / (HEAD_AXIS * DSH) - mean * mean
        inv = lax.rsqrt(var + norm_eps)
        for s, (ref, rows) in enumerate(sources):
            shift, scale = mods[s]
            y = (ref[rows, :].astype(jnp.float32) - mean) * inv * scale + shift
            start = pl.multiple_of(place_ref[s] * DSH, DSH)
            mod_ref[there, pl.ds(start, DSH)] = y.astype(jnp.bfloat16)

    def early_step(n, carry):
        normalize(0, n, early_ref)
        return carry

    lax.fori_loop(0, CUT // step, early_step, 0)
    for copy in copies:
        copy.wait()
    acc_ref[0:CUT, :] = jnp.dot(early_ref[...], w_ref[...], preferred_element_type=jnp.float32)
    for n in range(CUT // step):
        normalize(1, n, late_ref)
    acc_ref[CUT:, :] = jnp.dot(late_ref[...], w_ref[...], preferred_element_type=jnp.float32)

    def piece(part, p):
        b, hd = divmod(p, HEADS_HERE)
        lane = part * DSH + hd * HD
        return acc_ref[b * TOK : (b + 1) * TOK, lane : lane + HD]

    def turned(part, p):
        t = piece(part, p)
        t = t * lax.rsqrt(jnp.mean(t * t, axis=1, keepdims=True) + norm_eps)
        t = t * gain_ref[part : part + 1, :]
        even = lax.broadcasted_iota(jnp.int32, t.shape, 1) % 2 == 0
        other = jnp.where(even, pltpu.roll(t, HD - 1, 1), pltpu.roll(t, 1, 1))
        return (t * cos_ref[...] + other * sin_ref[...]).astype(jnp.bfloat16)

    for part in range(3):
        for p in range(PAIRS):
            if part == 2:
                result = piece(part, p).astype(jnp.bfloat16)
            else:
                result = turned(part, p)
            if part == 0 and p == LAST:
                for n in range(RING):
                    out_ref[n, 3 * TOK : 4 * TOK, :] = result
            elif part == 0:
                out_ref[p, 2 * TOK : 3 * TOK, :] = result
            elif p == LAST:
                last_ref[(part - 1) * TOK : part * TOK, :] = result
            else:
                out_ref[p, (part - 1) * TOK : part * TOK, :] = result


def project(places, blocks, w, gains, cosine, sine):
    return pl.pallas_call(
        project_kernel,
        out_shape=(
            pltpu.VMEM((RING, 4 * TOK, HD), jnp.bfloat16),
            pltpu.VMEM((2 * TOK, HD), jnp.bfloat16),
        ),
        grid_spec=pltpu.PrefetchScalarGridSpec(
            num_scalar_prefetch=1,
            grid=(1,),
            in_specs=[IN_VMEM] * len(blocks)
            + [pl.BlockSpec(memory_space=pltpu.HBM), IN_VMEM, IN_VMEM, IN_VMEM],
            out_specs=(IN_VMEM, IN_VMEM),
            scratch_shapes=[
                pltpu.VMEM((CUT, HEAD_AXIS * DSH), jnp.bfloat16),
                pltpu.VMEM((CUT, HEAD_AXIS * DSH), jnp.bfloat16),
                pltpu.VMEM((ROWS, WIDE), jnp.float32),
                pltpu.VMEM((HEAD_AXIS * DSH, WIDE), jnp.bfloat16),
                pltpu.SemaphoreType.DMA((3,)),
            ],
        ),
        compiler_params=pltpu.CompilerParams(vmem_limit_bytes=28 * MIB),
        cost_estimate=pl.CostEstimate(
            flops=2 * ROWS * HEAD_AXIS * DSH * 3 * DSH, bytes_accessed=12_000_000, transcendentals=0
        ),
        name="project",
    )(places, *map(in_vmem, blocks), w, *map(in_vmem, (gains, cosine, sine)))


QUAD = 4
TILE = QUAD * TOK
SET = RING * TOK
DIMS = (((1,), (1,)), ((), ()))


def score_keys(q, keys, score_ref, column, top):
    scores = lax.dot_general(q, keys, DIMS, preferred_element_type=jnp.float32)
    score_ref[:, column : column + scores.shape[1]] = scores
    for lane in range(0, scores.shape[1], 128):
        top = jnp.maximum(top, scores[:, lane : lane + 128])
    return top


def score_text(q, keys, valid, score_ref, column, top):
    scores = lax.dot_general(q, keys, DIMS, preferred_element_type=jnp.float32)
    index = lax.broadcasted_iota(jnp.int32, scores.shape, 1)
    scores = jnp.where(index < valid, scores, -jnp.inf)
    score_ref[:, column : column + scores.shape[1]] = scores
    for lane in range(0, scores.shape[1], 128):
        top = jnp.maximum(top, scores[:, lane : lane + 128])
    return top


def mix(score_ref, value_ref, top, count):
    mixed = jnp.zeros((TILE, 2 * HD), jnp.float32)
    for first in range(0, count, SET):
        stop = min(first + SET, count)
        weights = jnp.exp2(score_ref[:, first:stop] * EXP_SCALE - top).astype(jnp.bfloat16)
        mixed += jnp.dot(weights, value_ref[first:stop, :], preferred_element_type=jnp.float32)
    return mixed


def lay_values(value_ref, pieces):
    lane = lax.broadcasted_iota(jnp.int32, (value_ref.shape[0], HD), 1)
    value_ref[:, HD:] = jnp.where(lane == 0, 1.0, 0.0).astype(jnp.bfloat16)
    row = 0
    for piece in pieces:
        value_ref[row : row + piece.shape[0], :HD] = piece
        row += piece.shape[0]


def set_keys(ref):
    return ref[:, 0:TOK, :].reshape(SET, HD)


def set_values(ref):
    return ref[:, TOK : 2 * TOK, :].reshape(SET, HD)


def first_step():
    return pl.program_id(0) == 0


def tile_rows():
    return pl.ds(pl.multiple_of(pl.program_id(0) * TILE, TILE), TILE)


def gather_rows(flag_ref, q, pieces, before, score_ref, top_ref, total_ref, mixed_ref):
    def add_up(weights, values, total, mixed):
        for lane in range(0, weights.shape[1], 128):
            total += weights[:, lane : lane + 128]
        mixed += jnp.dot(weights.astype(jnp.bfloat16), values, preferred_element_type=jnp.float32)
        return total, mixed

    zeros = jnp.zeros((TILE, 128), jnp.float32)

    @pl.when(flag_ref[0] == 1)
    def _():
        total, mixed = zeros, zeros
        for keys, values, valid in pieces:
            scores = lax.dot_general(q, keys, DIMS, preferred_element_type=jnp.float32)
            if valid is not None:
                index = lax.broadcasted_iota(jnp.int32, scores.shape, 1)
                scores = jnp.where(index < valid, scores, -jnp.inf)
            total, mixed = add_up(jnp.exp2(scores * EXP_SCALE), values, total, mixed)
        top_ref[...] = zeros
        total_ref[...] = total
        mixed_ref[...] = mixed

    @pl.when(flag_ref[0] != 1)
    def _():
        top = jnp.full((TILE, 128), -jnp.inf, jnp.float32)
        column = 0
        for keys, _, valid in pieces:
            if valid is None:
                top = score_keys(q, keys, score_ref, column, top)
            else:
                top = score_text(q, keys, valid, score_ref, column, top)
            column += keys.shape[0]
        top = jnp.max(top, axis=1, keepdims=True) * EXP_SCALE
        if before is not None:
            top = jnp.maximum(top, before)
        total, mixed = zeros, zeros
        column = 0
        for _, values, _ in pieces:
            stop = column + values.shape[0]
            weights = jnp.exp2(score_ref[:, column:stop] * EXP_SCALE - top)
            total, mixed = add_up(weights, values, total, mixed)
            column = stop
        top_ref[...] = jnp.broadcast_to(top, (TILE, 128))
        total_ref[...] = total
        mixed_ref[...] = mixed


def set_piece(ref):
    return set_keys(ref), set_values(ref), None


def attend_near_kernel(
    where_ref, flag_ref, q_ref, own_ref, core_ref, text_ref, w_hbm,
    mixed_ref, total_ref, top_ref, q_out_ref, w_ref, score_ref, sem,
):
    copy = pltpu.make_async_copy(w_hbm, w_ref, sem)

    @pl.when(first_step())
    def _():
        copy.start()

    q = q_ref[...].reshape(TILE, HD)
    text = (text_ref[0, 0], text_ref[1, 0], where_ref[2])
    here = tile_rows()
    gather_rows(
        flag_ref, q, [set_piece(own_ref), set_piece(core_ref), text], None, score_ref,
        top_ref.at[here], total_ref.at[here], mixed_ref.at[here],
    )
    q_out_ref[here, :] = q

    @pl.when(pl.program_id(0) == SET // TILE - 1)
    def _():
        copy.wait()


STATE = (pltpu.VMEM((SET, HD), jnp.float32),) * 3


def attend_near(where, flag, received, own, core, text_kv, w_out):
    return pl.pallas_call(
        attend_near_kernel,
        out_shape=STATE + (pltpu.VMEM((SET, HD), jnp.bfloat16), pltpu.VMEM(w_out.shape, w_out.dtype)),
        grid_spec=pltpu.PrefetchScalarGridSpec(
            num_scalar_prefetch=2,
            grid=(SET // TILE,),
            in_specs=[
                pl.BlockSpec((QUAD, TOK, HD), lambda i, w, f: (i, 2, 0)),
                whole((RING, 2 * TOK, HD)),
                whole((RING, 2 * TOK, HD)),
                pl.BlockSpec((2, 1, TXT, HD), lambda i, w, f: (0, w[0], 0, w[1])),
                pl.BlockSpec(memory_space=pltpu.HBM),
            ],
            out_specs=(IN_VMEM,) * 5,
            scratch_shapes=[
                pltpu.VMEM((TILE, 2 * SET + TXT), jnp.float32),
                pltpu.SemaphoreType.DMA(()),
            ],
        ),
        compiler_params=pltpu.CompilerParams(vmem_limit_bytes=18 * MIB),
        cost_estimate=pl.CostEstimate(
            flops=4 * SET * 2304 * HD, bytes_accessed=3_000_000, transcendentals=SET * 2304
        ),
        name="attend_near",
    )(where, flag, received, own, core, text_kv, w_out)


LAST_KEYS = QUAD * TOK + 128


def lay_last_kernel(where_ref, *refs):
    last_refs = refs[:QUAD]
    text_ref, own_text_ref, gain_ref, keys_ref, value_ref, flag_ref = refs[QUAD:]
    for n, ref in enumerate(last_refs):
        keys_ref[n * TOK : (n + 1) * TOK, :] = ref[0:TOK, :]
    keys_ref[QUAD * TOK :, :] = text_ref[0, 0]
    lay_values(value_ref, [ref[TOK : 2 * TOK, :] for ref in last_refs] + [text_ref[1, 0]])
    room = 1.03 * HD
    gains = gain_ref[...] * gain_ref[...]
    text = own_text_ref[0, 0].astype(jnp.float32)
    key_norm = jnp.maximum(
        room * jnp.max(gains[1:2]), jnp.max(jnp.sum(text * text, axis=1, keepdims=True))
    )
    bound = EXP_SCALE * EXP_SCALE * room * jnp.max(gains[0:1]) * key_norm
    flag_ref[0] = jnp.where(bound < MOST_LOG2 * MOST_LOG2, 1, 0)


MOST_LOG2 = 90.0


def lay_last(where, lasts, text_kv, gains):
    return pl.pallas_call(
        lay_last_kernel,
        out_shape=(
            jax.ShapeDtypeStruct((LAST_KEYS, HD), jnp.bfloat16),
            jax.ShapeDtypeStruct((LAST_KEYS, 2 * HD), jnp.bfloat16),
            jax.ShapeDtypeStruct((1,), jnp.int32),
        ),
        grid_spec=pltpu.PrefetchScalarGridSpec(
            num_scalar_prefetch=1,
            grid=(1,),
            in_specs=[whole((2 * TOK, HD)) for _ in lasts]
            + [
                pl.BlockSpec(
                    (2, 1, 128, HD), lambda i, w: (0, BRANCH - 1, w[4], HEADS_HERE - 1)
                ),
                pl.BlockSpec((1, 1, TXT, HD), lambda i, w: (0, w[0], 0, w[1])),
                whole((2, HD)),
            ],
            out_specs=(
                whole((LAST_KEYS, HD)),
                whole((LAST_KEYS, 2 * HD)),
                pl.BlockSpec(memory_space=pltpu.SMEM),
            ),
        ),
        compiler_params=pltpu.CompilerParams(vmem_limit_bytes=16 * MIB),
        cost_estimate=pl.CostEstimate(
            flops=10_000_000_000, bytes_accessed=10_000_000, transcendentals=0
        ),
        name="lay_last",
    )(where, *lasts, text_kv, text_kv, gains)


def attend_last_kernel(where_ref, q_ref, keys_ref, value_ref, out_ref, score_ref):
    video_keys = QUAD * TOK
    q = q_ref[...].reshape(TILE, HD)
    top = jnp.full((TILE, 128), -jnp.inf, jnp.float32)
    top = score_keys(q, keys_ref[0:video_keys, :], score_ref, 0, top)
    top = score_text(q, keys_ref[video_keys:, :], where_ref[3], score_ref, video_keys, top)
    top = jnp.max(top, axis=1, keepdims=True) * EXP_SCALE
    mixed = mix(score_ref, value_ref, top, LAST_KEYS)
    total = mixed[:, HD : HD + 1]
    result = mixed[:, :HD] / total
    first = pl.program_id(0) * QUAD
    out_ref[pl.ds(first, QUAD), 0:TOK, :] = result.astype(jnp.bfloat16).reshape(QUAD, TOK, HD)
    level = jnp.broadcast_to(top + jnp.log(total) * LOG2E, (TILE, HD))
    for f in range(QUAD):
        row = jnp.transpose(level[f * TOK : (f + 1) * TOK])[0:1]
        stats = limbs_of(row) + [jnp.zeros((STAT_ROWS - 3, HD), jnp.float32)]
        out_ref[first + f, TOK:LAST_ROWS, :] = jnp.concatenate(stats, axis=0).astype(jnp.bfloat16)


def attend_last(where, received, keys, values):
    return pl.pallas_call(
        attend_last_kernel,
        out_shape=pltpu.VMEM((RING, LAST_ROWS, HD), jnp.bfloat16),
        grid_spec=pltpu.PrefetchScalarGridSpec(
            num_scalar_prefetch=1,
            grid=(SET // TILE,),
            in_specs=[
                pl.BlockSpec((QUAD, TOK, HD), lambda i, w: (i, 3, 0)),
                whole((LAST_KEYS, HD)),
                whole((LAST_KEYS, 2 * HD)),
            ],
            out_specs=IN_VMEM,
            scratch_shapes=[pltpu.VMEM((TILE, LAST_KEYS), jnp.float32)],
        ),
        compiler_params=pltpu.CompilerParams(vmem_limit_bytes=16 * MIB),
        cost_estimate=pl.CostEstimate(
            flops=4 * SET * 640 * HD, bytes_accessed=1_000_000, transcendentals=SET * 640
        ),
        name="attend_last",
    )(where, received, keys, values)


def attend_far_kernel(finish, flag_ref, q_ref, set_ref, *refs):
    mixed_in, total_in, top_in, *refs = refs
    score_ref, top_ref, total_ref, mixed_ref = refs[-4:]
    here = tile_rows()
    before = top_in[here, 0:1]
    gather_rows(
        flag_ref, q_ref[here, :], [set_piece(set_ref)], before, score_ref,
        top_ref, total_ref, mixed_ref,
    )
    decay = jnp.exp2(before - top_ref[:, 0:1])
    total = total_ref[...] + total_in[here, :] * decay
    mixed = mixed_ref[...] + mixed_in[here, :] * decay
    if finish:
        last_ref, out_ref = refs[:2]
        result = (mixed / jnp.sum(total, axis=1, keepdims=True)).astype(jnp.bfloat16)
        frames = pl.ds(pl.program_id(0) * QUAD, QUAD)
        out_ref[frames, 0:TOK, :] = result.reshape(QUAD, TOK, HD)
        out_ref[frames, TOK:RETURN, :] = last_ref[frames]
    else:
        mixed_out, total_out, top_out = refs[:3]
        mixed_out[here, :] = mixed
        total_out[here, :] = total
        top_out[here, :] = top_ref[...]


def attend_far(flag, queries, keys, state, last=None):
    finish = last is not None
    operands = [queries, keys, *state] + ([last] if finish else [])
    return pl.pallas_call(
        functools.partial(attend_far_kernel, finish),
        out_shape=pltpu.VMEM((RING, RETURN, HD), jnp.bfloat16) if finish else STATE,
        grid_spec=pltpu.PrefetchScalarGridSpec(
            num_scalar_prefetch=1,
            grid=(SET // TILE,),
            in_specs=[IN_VMEM] * len(operands),
            out_specs=IN_VMEM if finish else (IN_VMEM,) * 3,
            scratch_shapes=[pltpu.VMEM((TILE, SET), jnp.float32)]
            + [pltpu.VMEM((TILE, 128), jnp.float32)] * 3,
        ),
        compiler_params=pltpu.CompilerParams(vmem_limit_bytes=16 * MIB),
        cost_estimate=pl.CostEstimate(
            flops=4 * SET * SET * HD, bytes_accessed=3_000_000, transcendentals=SET * SET
        ),
        name="attend_far",
    )(flag, *map(in_vmem, operands))


def output_kernel(place_ref, back_ref, w_ref, *refs):
    out_refs, attn_ref = refs[:-1], refs[-1]
    for p in range(RING):
        b, hd = divmod(p, HEADS_HERE)
        attn_ref[b * TOK : (b + 1) * TOK, hd * HD : (hd + 1) * HD] = back_ref[p, 0:TOK, :]
    levels = []
    for p in range(RING):
        stats = back_ref[p, 2 * TOK : RETURN, :].astype(jnp.float32)
        row = stats[0:1] + stats[1:2] + stats[2:3]
        levels.append(jnp.transpose(jnp.broadcast_to(row, (TOK, HD))))
    top = levels[0]
    for level in levels[1:]:
        top = jnp.maximum(top, level)
    total = jnp.zeros((TOK, HD), jnp.float32)
    mixed = jnp.zeros((TOK, HD), jnp.float32)
    for p, level in enumerate(levels):
        weight = jnp.exp2(level - top)
        total += weight
        mixed += weight * back_ref[p, TOK : 2 * TOK, :].astype(jnp.float32)
    attn_ref[(BRANCH - 1) * TOK :, (HEADS_HERE - 1) * HD :] = (mixed / total).astype(jnp.bfloat16)
    multiply(place_ref, EARLY, attn_ref, w_ref, out_refs)


EARLY = (4, 5, 7)
LATE = (2, 3, 0, 1, 6)


def multiply(place_ref, places, attn_ref, w_ref, out_refs):
    for s, out_ref in zip(places, out_refs):
        start = pl.multiple_of(place_ref[s] * DSH, DSH)
        out_ref[...] = jnp.dot(
            attn_ref[...], w_ref[:, pl.ds(start, DSH)], preferred_element_type=jnp.float32
        ).astype(jnp.bfloat16)


def late_kernel(place_ref, attn_ref, w_ref, *out_refs):
    multiply(place_ref, LATE, attn_ref, w_ref, out_refs)


def output(kernel, places, rows, w_out, count):
    return pl.pallas_call(
        kernel,
        out_shape=(pltpu.VMEM((ROWS, DSH), jnp.bfloat16),) * count,
        grid_spec=pltpu.PrefetchScalarGridSpec(
            num_scalar_prefetch=1,
            grid=(1,),
            in_specs=[IN_VMEM, IN_VMEM],
            out_specs=(IN_VMEM,) * count,
        ),
        compiler_params=pltpu.CompilerParams(vmem_limit_bytes=16 * MIB),
        cost_estimate=pl.CostEstimate(
            flops=2 * ROWS * DSH * DSH * count, bytes_accessed=3_000_000, transcendentals=0
        ),
        name="output",
    )(places, in_vmem(rows), in_vmem(w_out))


def head_move(x, step):
    return lax.ppermute(x, "head", [(i, (i + step) % HEAD_AXIS) for i in range(HEAD_AXIS)])


def head_partner(x):
    return lax.ppermute(x, "head", [(i, i ^ 1) for i in range(HEAD_AXIS)])


def frame_move(x, flip):
    return lax.ppermute(x, "frame", [(i, i ^ flip) for i in range(FRAMES)])


def gather_head(own):
    partner = head_partner(own)
    ahead = head_move(own, -2)
    behind = head_move(own, 2)
    opposite = [head_move(behind[:CUT], 2), head_move(ahead[CUT:], -2)]
    return [
        own,
        partner,
        ahead,
        behind,
        head_move(partner, -2),
        head_move(partner, 2),
        *opposite,
        *map(head_partner, opposite),
    ]


def add(*terms):
    total = terms[0].astype(jnp.float32)
    for term in terms[1:]:
        total += term.astype(jnp.float32)
    return total


def scatter_head(places, back, w_out):
    ahead, behind, over, attention = output(output_kernel, places, back, w_out, 4)
    for_partner = [head_move(ahead, 2), head_move(behind, -2)]
    for_opposite = head_partner(over)
    ahead, behind, own, partner, opposite = output(
        late_kernel, places, attention, w_out, len(LATE)
    )
    direct = [head_move(ahead, 2), head_move(behind, -2)]
    over_y = head_partner(add(partner, *for_partner).astype(jnp.bfloat16))
    across = head_move(add(opposite, for_opposite).astype(jnp.bfloat16), 4)
    return add(own, *direct, over_y, across)


def body(
    video, w_qkv, w_out, text_kv, text_lengths, norm_gains, mod_table, timestep_ids, queue_shift
):
    text_kv = in_hbm(text_kv)
    frame = lax.axis_index("frame").astype(jnp.int32)
    head = lax.axis_index("head").astype(jnp.int32)
    own, gate, gains, places, where = prep(
        frame.reshape(1),
        head.reshape(1),
        queue_shift,
        in_hbm(timestep_ids),
        in_hbm(text_lengths),
        in_hbm(video),
        in_hbm(mod_table.transpose(1, 0, 2)),
        in_hbm(norm_gains),
    )
    cosine, sine = rope_tables(frame)
    blocks = gather_head(own)
    weights = in_hbm(w_qkv.transpose(1, 0, 2))
    send, last = project(places, blocks, weights, gains, cosine, sine)
    rings = [[(y * RING + z) * 2 + core for z in range(RING)] for y in range(2) for core in range(2)]

    def over_rings(x):
        return lax.all_to_all(x, "frame", 0, 0, axis_index_groups=rings, tiled=True)

    received = over_rings(send)
    flips = (1, FRAMES // 2, FRAMES // 2 + 1)
    lasts = [last] + [frame_move(last, flip) for flip in flips]
    last_keys, last_values, flag = lay_last(where, lasts, text_kv, gains)
    near = received[:, : 2 * TOK]
    over_y = frame_move(near, FRAMES // 2)
    near_later, last_keys = lax.optimization_barrier((near, last_keys))
    over_core = frame_move(near_later, 1)
    ninth = attend_last(where, received, last_keys, last_values)
    *state, queries, w_held = attend_near(
        where, flag, received, near, over_core, text_kv, in_hbm(w_out)
    )
    over_y, _, _ = lax.optimization_barrier((over_y, state[0], ninth))
    diagonal = frame_move(over_y, 1)
    state = attend_far(flag, queries, over_y, state)
    returned = attend_far(flag, queries, diagonal, state, ninth)
    back = over_rings(returned)
    proj = scatter_head(places, back, w_held).reshape(video.shape)
    return (video.astype(jnp.float32) + gate * proj).astype(jnp.bfloat16)


def solution(mesh):
    in_specs = (
        P(None, "frame", "head"),
        P(None, None, "head"),
        P("head", None),
        P(None, None, None, "head"),
        P(),
        P(),
        P(None, None, "head"),
        P(),
        P(),
    )
    out_specs = P(None, "frame", "head")
    return jax.shard_map(body, mesh=mesh, in_specs=in_specs, out_specs=out_specs, check_vma=False)
```

```python
import functools

import jax
import jax.numpy as jnp
import numpy as np
from jax import lax
from jax.experimental import pallas as pl
from jax.experimental.pallas import tpu as pltpu
from jax.sharding import PartitionSpec as P

HD = 128
TOK = 128
LAT_W = 16
FRAMES = 32
HEAD_AXIS = 8
BRANCH = 3
HEADS_HERE = 3
PAIRS = BRANCH * HEADS_HERE
DSH = 384
TXT = 256
RING = 8
ROWS = BRANCH * TOK
MOD_ROWS = 16
SENT = ROWS + MOD_ROWS
CUT = ROWS // 2
LAST = PAIRS - 1
STAT_ROWS = 16
LAST_ROWS = TOK + STAT_ROWS
RETURN = TOK + LAST_ROWS
WIDE = 3 * DSH
rope_base = 256.0
norm_eps = 1e-06
LOG2E = float(np.log2(np.e))
EXP_SCALE = float(HD ** (-0.5) * np.log2(np.e))
MIB = 1024 * 1024


def whole(shape):
    return pl.BlockSpec(shape, lambda *_: (0,) * len(shape))


IN_VMEM = pl.BlockSpec(memory_space=pltpu.VMEM)


def in_vmem(x):
    return pltpu.with_memory_space_constraint(x, pltpu.VMEM)


def in_hbm(x):
    return pltpu.with_memory_space_constraint(x, pltpu.HBM)


def limbs_of(value):
    limbs = []
    for _ in range(3):
        limb = value.astype(jnp.bfloat16).astype(jnp.float32)
        limbs.append(limb)
        value = value - limb
    return limbs


def rope_tables(frame):
    time_dims = HD // 8
    space_dims = (HD - time_dims) // 2
    freq = np.concatenate(
        [
            np.repeat(rope_base ** (-np.arange(0, z, 2, dtype=np.float64) / z), 2)
            for z in (time_dims, space_dims, space_dims)
        ]
    ).astype(np.float32)
    section = np.repeat(np.arange(3), (time_dims, space_dims, space_dims))
    token = jnp.arange(TOK, dtype=jnp.int32)[:, None]
    section = jnp.asarray(section)[None, :]
    position = jnp.where(
        section == 0, frame, jnp.where(section == 1, token // LAT_W, token % LAT_W)
    )
    angle = position.astype(jnp.float32) * jnp.asarray(freq)[None, :]
    sign = jnp.asarray(np.tile(np.array([-1.0, 1.0], np.float32), HD // 2))
    return jnp.cos(angle), jnp.sin(angle) * sign[None, :]


def prep_kernel(
    frame_ref, head_ref, shift_ref, ids_ref, lengths_ref, video_ref, table_ref, gain_ref,
    own_ref, gate_ref, gain_out_ref, place_ref, where_ref,
):
    head = head_ref[0]
    for s, step in enumerate((0, 0, 2, -2, 2, -2, 4, 4)):
        near = lax.rem(head + step + HEAD_AXIS, HEAD_AXIS)
        place_ref[s] = near if s in (0, 2, 3, 6) else near + 1 - 2 * lax.rem(near, 2)
    slab = lax.rem(lax.div(frame_ref[0], 2), RING)
    branch = lax.div(slab, HEADS_HERE)
    text_block = jnp.minimum(slab, 1)
    where_ref[0] = branch
    where_ref[1] = lax.rem(slab, HEADS_HERE)
    where_ref[2] = lengths_ref[branch]
    where_ref[3] = jnp.where(slab < 2, lengths_ref[BRANCH - 1] - 128 * text_block, 0)
    where_ref[4] = text_block
    level = ids_ref[lax.rem(frame_ref[0] + shift_ref[0], FRAMES)]
    looked = [table_ref[part, pl.ds(level, 1), :] for part in range(3)]
    gate_ref[...] = looked[2]
    gain_out_ref[...] = gain_ref[...]
    limbs = limbs_of(looked[0]) + limbs_of(looked[1])
    limbs.append(jnp.zeros((MOD_ROWS - 6, DSH), jnp.float32))
    for b in range(BRANCH):
        own_ref[b * TOK : (b + 1) * TOK, :] = video_ref[b]
    own_ref[ROWS:SENT, :] = jnp.concatenate(limbs, axis=0).astype(jnp.bfloat16)


def prep(frame, head, queue_shift, timestep_ids, lengths, video, table, gains):
    return pl.pallas_call(
        prep_kernel,
        out_shape=(
            pltpu.VMEM((SENT, DSH), jnp.bfloat16),
            jax.ShapeDtypeStruct((1, DSH), jnp.float32),
            pltpu.VMEM((2, HD), jnp.float32),
            jax.ShapeDtypeStruct((HEAD_AXIS,), jnp.int32),
            jax.ShapeDtypeStruct((5,), jnp.int32),
        ),
        grid_spec=pltpu.PrefetchScalarGridSpec(
            num_scalar_prefetch=5,
            grid=(1,),
            in_specs=[whole((BRANCH, TOK, DSH)), whole((3, FRAMES, DSH)), whole((2, HD))],
            out_specs=(
                IN_VMEM,
                whole((1, DSH)),
                IN_VMEM,
                pl.BlockSpec(memory_space=pltpu.SMEM),
                pl.BlockSpec(memory_space=pltpu.SMEM),
            ),
        ),
        compiler_params=pltpu.CompilerParams(vmem_limit_bytes=16 * MIB),
        name="prep",
    )(frame, head, queue_shift, timestep_ids, lengths, video, table, gains)


def project_kernel(place_ref, *refs):
    blocks, parts = refs[:6], refs[6:10]
    (
        w_hbm, gain_ref, cos_ref, sin_ref, out_ref, last_ref, mod_ref, acc_ref, w_ref, sems,
    ) = refs[10:]
    copies = [
        pltpu.make_async_copy(w_hbm.at[n], w_ref.at[:, pl.ds(n * DSH, DSH)], sems.at[n])
        for n in range(3)
    ]
    for copy in copies:
        copy.start()
    limbs = [block[ROWS:SENT, :] for block in blocks]
    limbs += [parts[n][ROWS - CUT : SENT - CUT, :] for n in (1, 3)]
    mods = []
    for limb in limbs:
        limb = limb.astype(jnp.float32)
        shift = limb[0:1] + limb[1:2] + limb[2:3]
        mods.append((shift, 1.0 + (limb[3:4] + limb[4:5] + limb[5:6])))
    step = 64
    for first in (0, CUT):
        late = 1 if first else 0

        def chunk(n, carry):
            there = pl.ds(pl.multiple_of(n * step, step), step)
            here = pl.ds(pl.multiple_of(first + n * step, step), step)
            sources = [(block, here) for block in blocks]
            sources += [(parts[late], there), (parts[2 + late], there)]
            total = jnp.zeros((step, 128), jnp.float32)
            square = jnp.zeros((step, 128), jnp.float32)
            for ref, rows in sources:
                for lane in range(0, DSH, 128):
                    x = ref[rows, lane : lane + 128].astype(jnp.float32)
                    total += x
                    square += x * x
            mean = jnp.sum(total, axis=1, keepdims=True) / (HEAD_AXIS * DSH)
            var = jnp.sum(square, axis=1, keepdims=True) / (HEAD_AXIS * DSH) - mean * mean
            inv = lax.rsqrt(var + norm_eps)
            for s, (ref, rows) in enumerate(sources):
                shift, scale = mods[s]
                y = (ref[rows, :].astype(jnp.float32) - mean) * inv * scale + shift
                start = pl.multiple_of(place_ref[s] * DSH, DSH)
                mod_ref[here, pl.ds(start, DSH)] = y.astype(jnp.bfloat16)
            return carry

        lax.fori_loop(0, CUT // step, chunk, 0)

    def piece(part, p):
        b, hd = divmod(p, HEADS_HERE)
        lane = part * DSH + hd * HD
        return acc_ref[b * TOK : (b + 1) * TOK, lane : lane + HD]

    def turned(part, p):
        t = piece(part, p)
        t = t * lax.rsqrt(jnp.mean(t * t, axis=1, keepdims=True) + norm_eps)
        t = t * gain_ref[part : part + 1, :]
        even = lax.broadcasted_iota(jnp.int32, t.shape, 1) % 2 == 0
        other = jnp.where(even, pltpu.roll(t, HD - 1, 1), pltpu.roll(t, 1, 1))
        return (t * cos_ref[...] + other * sin_ref[...]).astype(jnp.bfloat16)

    for copy in copies:
        copy.wait()
    acc_ref[...] = jnp.dot(mod_ref[...], w_ref[...], preferred_element_type=jnp.float32)
    for part in range(3):
        for p in range(PAIRS):
            if part == 2:
                result = piece(part, p).astype(jnp.bfloat16)
            else:
                result = turned(part, p)
            if part == 0 and p == LAST:
                for n in range(RING):
                    out_ref[n, 3 * TOK : 4 * TOK, :] = result
            elif part == 0:
                out_ref[p, 2 * TOK : 3 * TOK, :] = result
            elif p == LAST:
                last_ref[(part - 1) * TOK : part * TOK, :] = result
            else:
                out_ref[p, (part - 1) * TOK : part * TOK, :] = result


def project(places, blocks, w, gains, cosine, sine):
    return pl.pallas_call(
        project_kernel,
        out_shape=(
            pltpu.VMEM((RING, 4 * TOK, HD), jnp.bfloat16),
            pltpu.VMEM((2 * TOK, HD), jnp.bfloat16),
        ),
        grid_spec=pltpu.PrefetchScalarGridSpec(
            num_scalar_prefetch=1,
            grid=(1,),
            in_specs=[IN_VMEM] * len(blocks)
            + [pl.BlockSpec(memory_space=pltpu.HBM), IN_VMEM, IN_VMEM, IN_VMEM],
            out_specs=(IN_VMEM, IN_VMEM),
            scratch_shapes=[
                pltpu.VMEM((ROWS, HEAD_AXIS * DSH), jnp.bfloat16),
                pltpu.VMEM((ROWS, WIDE), jnp.float32),
                pltpu.VMEM((HEAD_AXIS * DSH, WIDE), jnp.bfloat16),
                pltpu.SemaphoreType.DMA((3,)),
            ],
        ),
        compiler_params=pltpu.CompilerParams(vmem_limit_bytes=28 * MIB),
        cost_estimate=pl.CostEstimate(
            flops=2 * ROWS * HEAD_AXIS * DSH * 3 * DSH, bytes_accessed=12_000_000, transcendentals=0
        ),
        name="project",
    )(places, *map(in_vmem, blocks), w, *map(in_vmem, (gains, cosine, sine)))


QUAD = 4
TILE = QUAD * TOK
SET = RING * TOK
DIMS = (((1,), (1,)), ((), ()))


def score_keys(q, keys, score_ref, column, top):
    scores = lax.dot_general(q, keys, DIMS, preferred_element_type=jnp.float32)
    score_ref[:, column : column + scores.shape[1]] = scores
    for lane in range(0, scores.shape[1], 128):
        top = jnp.maximum(top, scores[:, lane : lane + 128])
    return top


def score_text(q, keys, valid, score_ref, column, top):
    scores = lax.dot_general(q, keys, DIMS, preferred_element_type=jnp.float32)
    index = lax.broadcasted_iota(jnp.int32, scores.shape, 1)
    scores = jnp.where(index < valid, scores, -jnp.inf)
    score_ref[:, column : column + scores.shape[1]] = scores
    for lane in range(0, scores.shape[1], 128):
        top = jnp.maximum(top, scores[:, lane : lane + 128])
    return top


def mix(score_ref, value_ref, top, count):
    mixed = jnp.zeros((TILE, 2 * HD), jnp.float32)
    for first in range(0, count, SET):
        stop = min(first + SET, count)
        weights = jnp.exp2(score_ref[:, first:stop] * EXP_SCALE - top).astype(jnp.bfloat16)
        mixed += jnp.dot(weights, value_ref[first:stop, :], preferred_element_type=jnp.float32)
    return mixed


def lay_values(value_ref, pieces):
    lane = lax.broadcasted_iota(jnp.int32, (value_ref.shape[0], HD), 1)
    value_ref[:, HD:] = jnp.where(lane == 0, 1.0, 0.0).astype(jnp.bfloat16)
    row = 0
    for piece in pieces:
        value_ref[row : row + piece.shape[0], :HD] = piece
        row += piece.shape[0]


def set_keys(ref):
    return ref[:, 0:TOK, :].reshape(-1, HD)


def set_values(ref):
    return ref[:, TOK : 2 * TOK, :].reshape(-1, HD)


def first_step():
    return pl.program_id(0) == 0


def tile_rows():
    return pl.ds(pl.multiple_of(pl.program_id(0) * TILE, TILE), TILE)


def gather_rows(flag_ref, q, pieces, before, score_ref, top_ref, total_ref, mixed_ref):
    def add_up(weights, values, total, mixed):
        for lane in range(0, weights.shape[1], 128):
            total += weights[:, lane : lane + 128]
        mixed += jnp.dot(weights.astype(jnp.bfloat16), values, preferred_element_type=jnp.float32)
        return total, mixed

    zeros = jnp.zeros((TILE, 128), jnp.float32)

    @pl.when(flag_ref[0] == 1)
    def _():
        total, mixed = zeros, zeros
        for keys, values, valid in pieces:
            scores = lax.dot_general(q, keys, DIMS, preferred_element_type=jnp.float32)
            if valid is not None:
                index = lax.broadcasted_iota(jnp.int32, scores.shape, 1)
                scores = jnp.where(index < valid, scores, -jnp.inf)
            total, mixed = add_up(jnp.exp2(scores * EXP_SCALE), values, total, mixed)
        top_ref[...] = zeros
        total_ref[...] = total
        mixed_ref[...] = mixed

    @pl.when(flag_ref[0] != 1)
    def _():
        top = jnp.full((TILE, 128), -jnp.inf, jnp.float32)
        column = 0
        for keys, _, valid in pieces:
            if valid is None:
                top = score_keys(q, keys, score_ref, column, top)
            else:
                top = score_text(q, keys, valid, score_ref, column, top)
            column += keys.shape[0]
        top = jnp.max(top, axis=1, keepdims=True) * EXP_SCALE
        if before is not None:
            top = jnp.maximum(top, before)
        total, mixed = zeros, zeros
        column = 0
        for _, values, _ in pieces:
            stop = column + values.shape[0]
            weights = jnp.exp2(score_ref[:, column:stop] * EXP_SCALE - top)
            total, mixed = add_up(weights, values, total, mixed)
            column = stop
        top_ref[...] = jnp.broadcast_to(top, (TILE, 128))
        total_ref[...] = total
        mixed_ref[...] = mixed


def set_piece(ref):
    return set_keys(ref), set_values(ref), None


def attend_near_kernel(
    where_ref, flag_ref, q_ref, own_ref, core_ref, text_ref, w_hbm,
    mixed_ref, total_ref, top_ref, q_out_ref, w_ref, score_ref, sem,
):
    copy = pltpu.make_async_copy(w_hbm, w_ref, sem)

    @pl.when(first_step())
    def _():
        copy.start()

    q = q_ref[...].reshape(TILE, HD)
    text = (text_ref[0, 0], text_ref[1, 0], where_ref[2])
    here = tile_rows()
    gather_rows(
        flag_ref, q, [set_piece(own_ref), set_piece(core_ref), text], None, score_ref,
        top_ref.at[here], total_ref.at[here], mixed_ref.at[here],
    )
    q_out_ref[here, :] = q

    @pl.when(pl.program_id(0) == SET // TILE - 1)
    def _():
        copy.wait()


STATE = (pltpu.VMEM((SET, HD), jnp.float32),) * 3


def attend_near(where, flag, received, own, core, text_kv, w_out):
    return pl.pallas_call(
        attend_near_kernel,
        out_shape=STATE + (pltpu.VMEM((SET, HD), jnp.bfloat16), pltpu.VMEM(w_out.shape, w_out.dtype)),
        grid_spec=pltpu.PrefetchScalarGridSpec(
            num_scalar_prefetch=2,
            grid=(SET // TILE,),
            in_specs=[
                pl.BlockSpec((QUAD, TOK, HD), lambda i, w, f: (i, 2, 0)),
                whole((RING, 2 * TOK, HD)),
                whole((RING, 2 * TOK, HD)),
                pl.BlockSpec((2, 1, TXT, HD), lambda i, w, f: (0, w[0], 0, w[1])),
                pl.BlockSpec(memory_space=pltpu.HBM),
            ],
            out_specs=(IN_VMEM,) * 5,
            scratch_shapes=[
                pltpu.VMEM((TILE, 2 * SET + TXT), jnp.float32),
                pltpu.SemaphoreType.DMA(()),
            ],
        ),
        compiler_params=pltpu.CompilerParams(vmem_limit_bytes=18 * MIB),
        cost_estimate=pl.CostEstimate(
            flops=4 * SET * 2304 * HD, bytes_accessed=3_000_000, transcendentals=SET * 2304
        ),
        name="attend_near",
    )(where, flag, received, own, core, text_kv, w_out)


LAST_KEYS = QUAD * TOK + 128


def lay_last_kernel(where_ref, *refs):
    last_refs = refs[:QUAD]
    text_ref, own_text_ref, gain_ref, keys_ref, value_ref, flag_ref = refs[QUAD:]
    for n, ref in enumerate(last_refs):
        keys_ref[n * TOK : (n + 1) * TOK, :] = ref[0:TOK, :]
    keys_ref[QUAD * TOK :, :] = text_ref[0, 0]
    lay_values(value_ref, [ref[TOK : 2 * TOK, :] for ref in last_refs] + [text_ref[1, 0]])
    room = 1.03 * HD
    gains = gain_ref[...] * gain_ref[...]
    text = own_text_ref[0, 0].astype(jnp.float32)
    key_norm = jnp.maximum(
        room * jnp.max(gains[1:2]), jnp.max(jnp.sum(text * text, axis=1, keepdims=True))
    )
    bound = EXP_SCALE * EXP_SCALE * room * jnp.max(gains[0:1]) * key_norm
    flag_ref[0] = jnp.where(bound < MOST_LOG2 * MOST_LOG2, 1, 0)


MOST_LOG2 = 90.0


def lay_last(where, lasts, text_kv, gains):
    return pl.pallas_call(
        lay_last_kernel,
        out_shape=(
            jax.ShapeDtypeStruct((LAST_KEYS, HD), jnp.bfloat16),
            jax.ShapeDtypeStruct((LAST_KEYS, 2 * HD), jnp.bfloat16),
            jax.ShapeDtypeStruct((1,), jnp.int32),
        ),
        grid_spec=pltpu.PrefetchScalarGridSpec(
            num_scalar_prefetch=1,
            grid=(1,),
            in_specs=[whole((2 * TOK, HD)) for _ in lasts]
            + [
                pl.BlockSpec(
                    (2, 1, 128, HD), lambda i, w: (0, BRANCH - 1, w[4], HEADS_HERE - 1)
                ),
                pl.BlockSpec((1, 1, TXT, HD), lambda i, w: (0, w[0], 0, w[1])),
                whole((2, HD)),
            ],
            out_specs=(
                whole((LAST_KEYS, HD)),
                whole((LAST_KEYS, 2 * HD)),
                pl.BlockSpec(memory_space=pltpu.SMEM),
            ),
        ),
        compiler_params=pltpu.CompilerParams(vmem_limit_bytes=16 * MIB),
        cost_estimate=pl.CostEstimate(
            flops=10_000_000_000, bytes_accessed=10_000_000, transcendentals=0
        ),
        name="lay_last",
    )(where, *lasts, text_kv, text_kv, gains)


def attend_last_kernel(where_ref, q_ref, keys_ref, value_ref, out_ref, score_ref):
    video_keys = QUAD * TOK
    q = q_ref[...].reshape(TILE, HD)
    top = jnp.full((TILE, 128), -jnp.inf, jnp.float32)
    top = score_keys(q, keys_ref[0:video_keys, :], score_ref, 0, top)
    top = score_text(q, keys_ref[video_keys:, :], where_ref[3], score_ref, video_keys, top)
    top = jnp.max(top, axis=1, keepdims=True) * EXP_SCALE
    mixed = mix(score_ref, value_ref, top, LAST_KEYS)
    total = mixed[:, HD : HD + 1]
    result = mixed[:, :HD] / total
    first = pl.program_id(0) * QUAD
    out_ref[pl.ds(first, QUAD), 0:TOK, :] = result.astype(jnp.bfloat16).reshape(QUAD, TOK, HD)
    level = jnp.broadcast_to(top + jnp.log(total) * LOG2E, (TILE, HD))
    for f in range(QUAD):
        row = jnp.transpose(level[f * TOK : (f + 1) * TOK])[0:1]
        stats = limbs_of(row) + [jnp.zeros((STAT_ROWS - 3, HD), jnp.float32)]
        out_ref[first + f, TOK:LAST_ROWS, :] = jnp.concatenate(stats, axis=0).astype(jnp.bfloat16)


def attend_last(where, received, keys, values):
    return pl.pallas_call(
        attend_last_kernel,
        out_shape=pltpu.VMEM((RING, LAST_ROWS, HD), jnp.bfloat16),
        grid_spec=pltpu.PrefetchScalarGridSpec(
            num_scalar_prefetch=1,
            grid=(SET // TILE,),
            in_specs=[
                pl.BlockSpec((QUAD, TOK, HD), lambda i, w: (i, 3, 0)),
                whole((LAST_KEYS, HD)),
                whole((LAST_KEYS, 2 * HD)),
            ],
            out_specs=IN_VMEM,
            scratch_shapes=[pltpu.VMEM((TILE, LAST_KEYS), jnp.float32)],
        ),
        compiler_params=pltpu.CompilerParams(vmem_limit_bytes=16 * MIB),
        cost_estimate=pl.CostEstimate(
            flops=4 * SET * 640 * HD, bytes_accessed=1_000_000, transcendentals=SET * 640
        ),
        name="attend_last",
    )(where, received, keys, values)


def attend_far_kernel(finish, flag_ref, q_ref, set_ref, *refs):
    mixed_in, total_in, top_in, *refs = refs
    score_ref, top_ref, total_ref, mixed_ref = refs[-4:]
    here = tile_rows()
    before = top_in[here, 0:1]
    gather_rows(
        flag_ref, q_ref[here, :], [set_piece(set_ref)], before, score_ref,
        top_ref, total_ref, mixed_ref,
    )
    decay = jnp.exp2(before - top_ref[:, 0:1])
    total = total_ref[...] + total_in[here, :] * decay
    mixed = mixed_ref[...] + mixed_in[here, :] * decay
    if finish:
        last_ref, out_ref = refs[:2]
        result = (mixed / jnp.sum(total, axis=1, keepdims=True)).astype(jnp.bfloat16)
        frames = pl.ds(pl.program_id(0) * QUAD, QUAD)
        out_ref[frames, 0:TOK, :] = result.reshape(QUAD, TOK, HD)
        out_ref[frames, TOK:RETURN, :] = last_ref[frames]
    else:
        mixed_out, total_out, top_out = refs[:3]
        mixed_out[here, :] = mixed
        total_out[here, :] = total
        top_out[here, :] = top_ref[...]


def attend_far(flag, queries, keys, state, last=None):
    finish = last is not None
    operands = [queries, keys, *state] + ([last] if finish else [])
    return pl.pallas_call(
        functools.partial(attend_far_kernel, finish),
        out_shape=pltpu.VMEM((RING, RETURN, HD), jnp.bfloat16) if finish else STATE,
        grid_spec=pltpu.PrefetchScalarGridSpec(
            num_scalar_prefetch=1,
            grid=(SET // TILE,),
            in_specs=[IN_VMEM] * len(operands),
            out_specs=IN_VMEM if finish else (IN_VMEM,) * 3,
            scratch_shapes=[pltpu.VMEM((TILE, keys.shape[0] * TOK), jnp.float32)]
            + [pltpu.VMEM((TILE, 128), jnp.float32)] * 3,
        ),
        compiler_params=pltpu.CompilerParams(vmem_limit_bytes=16 * MIB),
        cost_estimate=pl.CostEstimate(
            flops=2 * SET * SET * HD, bytes_accessed=3_000_000, transcendentals=SET * SET // 2
        ),
        name="attend_far",
    )(flag, *map(in_vmem, operands))


def output_kernel(place_ref, back_ref, w_ref, *refs):
    out_refs, attn_ref = refs[:-1], refs[-1]
    for p in range(RING):
        b, hd = divmod(p, HEADS_HERE)
        attn_ref[b * TOK : (b + 1) * TOK, hd * HD : (hd + 1) * HD] = back_ref[p, 0:TOK, :]
    levels = []
    for p in range(RING):
        stats = back_ref[p, 2 * TOK : RETURN, :].astype(jnp.float32)
        row = stats[0:1] + stats[1:2] + stats[2:3]
        levels.append(jnp.transpose(jnp.broadcast_to(row, (TOK, HD))))
    top = levels[0]
    for level in levels[1:]:
        top = jnp.maximum(top, level)
    total = jnp.zeros((TOK, HD), jnp.float32)
    mixed = jnp.zeros((TOK, HD), jnp.float32)
    for p, level in enumerate(levels):
        weight = jnp.exp2(level - top)
        total += weight
        mixed += weight * back_ref[p, TOK : 2 * TOK, :].astype(jnp.float32)
    attn_ref[(BRANCH - 1) * TOK :, (HEADS_HERE - 1) * HD :] = (mixed / total).astype(jnp.bfloat16)
    multiply(place_ref, EARLY, attn_ref, w_ref, out_refs)


EARLY = (4, 5, 7)
LATE = (2, 3, 0, 1, 6)


def multiply(place_ref, places, attn_ref, w_ref, out_refs):
    for s, out_ref in zip(places, out_refs):
        start = pl.multiple_of(place_ref[s] * DSH, DSH)
        out_ref[...] = jnp.dot(
            attn_ref[...], w_ref[:, pl.ds(start, DSH)], preferred_element_type=jnp.float32
        ).astype(jnp.bfloat16)


def late_kernel(place_ref, attn_ref, w_ref, *out_refs):
    multiply(place_ref, LATE, attn_ref, w_ref, out_refs)


def output(kernel, places, rows, w_out, count):
    return pl.pallas_call(
        kernel,
        out_shape=(pltpu.VMEM((ROWS, DSH), jnp.bfloat16),) * count,
        grid_spec=pltpu.PrefetchScalarGridSpec(
            num_scalar_prefetch=1,
            grid=(1,),
            in_specs=[IN_VMEM, IN_VMEM],
            out_specs=(IN_VMEM,) * count,
        ),
        compiler_params=pltpu.CompilerParams(vmem_limit_bytes=16 * MIB),
        cost_estimate=pl.CostEstimate(
            flops=2 * ROWS * DSH * DSH * count, bytes_accessed=3_000_000, transcendentals=0
        ),
        name="output",
    )(places, in_vmem(rows), in_vmem(w_out))


def head_move(x, step):
    return lax.ppermute(x, "head", [(i, (i + step) % HEAD_AXIS) for i in range(HEAD_AXIS)])


def head_partner(x):
    return lax.ppermute(x, "head", [(i, i ^ 1) for i in range(HEAD_AXIS)])


def frame_move(x, flip):
    return lax.ppermute(x, "frame", [(i, i ^ flip) for i in range(FRAMES)])


def gather_head(own):
    partner = head_partner(own)
    ahead = head_move(own, -2)
    behind = head_move(own, 2)
    opposite = [head_move(behind[:CUT], 2), head_move(ahead[CUT:], -2)]
    return [
        own,
        partner,
        ahead,
        behind,
        head_move(partner, -2),
        head_move(partner, 2),
        *opposite,
        *map(head_partner, opposite),
    ]


def add(*terms):
    total = terms[0].astype(jnp.float32)
    for term in terms[1:]:
        total += term.astype(jnp.float32)
    return total


def scatter_head(places, back, w_out):
    ahead, behind, over, attention = output(output_kernel, places, back, w_out, 4)
    for_partner = [head_move(ahead, 2), head_move(behind, -2)]
    for_opposite = head_partner(over)
    ahead, behind, own, partner, opposite = output(
        late_kernel, places, attention, w_out, len(LATE)
    )
    direct = [head_move(ahead, 2), head_move(behind, -2)]
    over_y = head_partner(add(partner, *for_partner).astype(jnp.bfloat16))
    across = head_move(add(opposite, for_opposite).astype(jnp.bfloat16), 4)
    return add(own, *direct, over_y, across)


def body(
    video, w_qkv, w_out, text_kv, text_lengths, norm_gains, mod_table, timestep_ids, queue_shift
):
    text_kv = in_hbm(text_kv)
    frame = lax.axis_index("frame").astype(jnp.int32)
    head = lax.axis_index("head").astype(jnp.int32)
    own, gate, gains, places, where = prep(
        frame.reshape(1),
        head.reshape(1),
        queue_shift,
        in_hbm(timestep_ids),
        in_hbm(text_lengths),
        in_hbm(video),
        in_hbm(mod_table.transpose(1, 0, 2)),
        in_hbm(norm_gains),
    )
    cosine, sine = rope_tables(frame)
    blocks = gather_head(own)
    weights = in_hbm(w_qkv.transpose(1, 0, 2))
    send, last = project(places, blocks, weights, gains, cosine, sine)
    rings = [[(y * RING + z) * 2 + core for z in range(RING)] for y in range(2) for core in range(2)]

    def over_rings(x):
        return lax.all_to_all(x, "frame", 0, 0, axis_index_groups=rings, tiled=True)

    received = over_rings(send)
    flips = (1, FRAMES // 2, FRAMES // 2 + 1)
    lasts = [last] + [frame_move(last, flip) for flip in flips]
    last_keys, last_values, flag = lay_last(where, lasts, text_kv, gains)
    near = received[:, : 2 * TOK]
    halves = [near[: RING // 2], near[RING // 2 :]]
    over_y = [frame_move(half, FRAMES // 2) for half in halves]
    near_later, last_keys = lax.optimization_barrier((near, last_keys))
    over_core = frame_move(near_later, 1)
    ninth = attend_last(where, received, last_keys, last_values)
    *state, queries, w_held = attend_near(
        where, flag, received, near, over_core, text_kv, in_hbm(w_out)
    )
    first, _, _ = lax.optimization_barrier((over_y[0], state[0], ninth))
    diagonal = frame_move(first, 1)
    state = attend_far(flag, queries, first, state)
    state = attend_far(flag, queries, diagonal, state)
    second, _ = lax.optimization_barrier((over_y[1], state[0]))
    diagonal = frame_move(second, 1)
    state = attend_far(flag, queries, second, state)
    returned = attend_far(flag, queries, diagonal, state, ninth)
    back = over_rings(returned)
    proj = scatter_head(places, back, w_held).reshape(video.shape)
    return (video.astype(jnp.float32) + gate * proj).astype(jnp.bfloat16)


def solution(mesh):
    in_specs = (
        P(None, "frame", "head"),
        P(None, None, "head"),
        P("head", None),
        P(None, None, None, "head"),
        P(),
        P(),
        P(None, None, "head"),
        P(),
        P(),
    )
    out_specs = P(None, "frame", "head")
    return jax.shard_map(body, mesh=mesh, in_specs=in_specs, out_specs=out_specs, check_vma=False)
```

```python
import functools

import jax
import jax.numpy as jnp
import numpy as np
from jax import lax
from jax.experimental import pallas as pl
from jax.experimental.pallas import tpu as pltpu
from jax.sharding import PartitionSpec as P

HD = 128
TOK = 128
LAT_W = 16
FRAMES = 32
HEAD_AXIS = 8
BRANCH = 3
HEADS_HERE = 3
PAIRS = BRANCH * HEADS_HERE
DSH = 384
TXT = 256
RING = 8
ROWS = BRANCH * TOK
MOD_ROWS = 16
SENT = ROWS + MOD_ROWS
CUT = ROWS // 2
LAST = PAIRS - 1
STAT_ROWS = 16
LAST_ROWS = TOK + STAT_ROWS
RETURN = TOK + LAST_ROWS
WIDE = 3 * DSH
rope_base = 256.0
norm_eps = 1e-06
LOG2E = float(np.log2(np.e))
EXP_SCALE = float(HD ** (-0.5) * np.log2(np.e))
MIB = 1024 * 1024


def whole(shape):
    return pl.BlockSpec(shape, lambda *_: (0,) * len(shape))


IN_VMEM = pl.BlockSpec(memory_space=pltpu.VMEM)


def in_vmem(x):
    return pltpu.with_memory_space_constraint(x, pltpu.VMEM)


def in_hbm(x):
    return pltpu.with_memory_space_constraint(x, pltpu.HBM)


def limbs_of(value):
    limbs = []
    for _ in range(3):
        limb = value.astype(jnp.bfloat16).astype(jnp.float32)
        limbs.append(limb)
        value = value - limb
    return limbs


def rope_tables(frame):
    time_dims = HD // 8
    space_dims = (HD - time_dims) // 2
    freq = np.concatenate(
        [
            np.repeat(rope_base ** (-np.arange(0, z, 2, dtype=np.float64) / z), 2)
            for z in (time_dims, space_dims, space_dims)
        ]
    ).astype(np.float32)
    section = np.repeat(np.arange(3), (time_dims, space_dims, space_dims))
    token = jnp.arange(TOK, dtype=jnp.int32)[:, None]
    section = jnp.asarray(section)[None, :]
    position = jnp.where(
        section == 0, frame, jnp.where(section == 1, token // LAT_W, token % LAT_W)
    )
    angle = position.astype(jnp.float32) * jnp.asarray(freq)[None, :]
    sign = jnp.asarray(np.tile(np.array([-1.0, 1.0], np.float32), HD // 2))
    return jnp.cos(angle), jnp.sin(angle) * sign[None, :]


def prep_kernel(
    frame_ref, head_ref, shift_ref, ids_ref, lengths_ref, video_ref, table_ref, gain_ref,
    own_ref, gate_ref, gain_out_ref, place_ref, where_ref,
):
    head = head_ref[0]
    for s, step in enumerate((0, 0, 2, -2, 2, -2, 4, 4)):
        near = lax.rem(head + step + HEAD_AXIS, HEAD_AXIS)
        place_ref[s] = near if s in (0, 2, 3, 6) else near + 1 - 2 * lax.rem(near, 2)
    slab = lax.rem(lax.div(frame_ref[0], 2), RING)
    branch = lax.div(slab, HEADS_HERE)
    text_block = jnp.minimum(slab, 1)
    where_ref[0] = branch
    where_ref[1] = lax.rem(slab, HEADS_HERE)
    where_ref[2] = lengths_ref[branch]
    where_ref[3] = jnp.where(slab < 2, lengths_ref[BRANCH - 1] - 128 * text_block, 0)
    where_ref[4] = text_block
    level = ids_ref[lax.rem(frame_ref[0] + shift_ref[0], FRAMES)]
    looked = [table_ref[part, pl.ds(level, 1), :] for part in range(3)]
    gate_ref[...] = looked[2]
    gain_out_ref[...] = gain_ref[...]
    limbs = limbs_of(looked[0]) + limbs_of(looked[1])
    limbs.append(jnp.zeros((MOD_ROWS - 6, DSH), jnp.float32))
    for b in range(BRANCH):
        own_ref[b * TOK : (b + 1) * TOK, :] = video_ref[b]
    own_ref[ROWS:SENT, :] = jnp.concatenate(limbs, axis=0).astype(jnp.bfloat16)


def prep(frame, head, queue_shift, timestep_ids, lengths, video, table, gains):
    return pl.pallas_call(
        prep_kernel,
        out_shape=(
            pltpu.VMEM((SENT, DSH), jnp.bfloat16),
            jax.ShapeDtypeStruct((1, DSH), jnp.float32),
            pltpu.VMEM((2, HD), jnp.float32),
            jax.ShapeDtypeStruct((HEAD_AXIS,), jnp.int32),
            jax.ShapeDtypeStruct((5,), jnp.int32),
        ),
        grid_spec=pltpu.PrefetchScalarGridSpec(
            num_scalar_prefetch=5,
            grid=(1,),
            in_specs=[whole((BRANCH, TOK, DSH)), whole((3, FRAMES, DSH)), whole((2, HD))],
            out_specs=(
                IN_VMEM,
                whole((1, DSH)),
                IN_VMEM,
                pl.BlockSpec(memory_space=pltpu.SMEM),
                pl.BlockSpec(memory_space=pltpu.SMEM),
            ),
        ),
        compiler_params=pltpu.CompilerParams(vmem_limit_bytes=16 * MIB),
        name="prep",
    )(frame, head, queue_shift, timestep_ids, lengths, video, table, gains)


def project_kernel(place_ref, *refs):
    blocks, parts = refs[:6], refs[6:10]
    (
        w_hbm, gain_ref, cos_ref, sin_ref, out_ref, last_ref, mod_ref, acc_ref, w_ref, sems,
    ) = refs[10:]
    copies = [
        pltpu.make_async_copy(w_hbm.at[n], w_ref.at[:, pl.ds(n * DSH, DSH)], sems.at[n])
        for n in range(3)
    ]
    for copy in copies:
        copy.start()
    limbs = [block[ROWS:SENT, :] for block in blocks]
    limbs += [parts[n][ROWS - CUT : SENT - CUT, :] for n in (1, 3)]
    mods = []
    for limb in limbs:
        limb = limb.astype(jnp.float32)
        shift = limb[0:1] + limb[1:2] + limb[2:3]
        mods.append((shift, 1.0 + (limb[3:4] + limb[4:5] + limb[5:6])))
    step = 64
    for first in (0, CUT):
        late = 1 if first else 0

        def chunk(n, carry):
            there = pl.ds(pl.multiple_of(n * step, step), step)
            here = pl.ds(pl.multiple_of(first + n * step, step), step)
            sources = [(block, here) for block in blocks]
            sources += [(parts[late], there), (parts[2 + late], there)]
            total = jnp.zeros((step, 128), jnp.float32)
            square = jnp.zeros((step, 128), jnp.float32)
            for ref, rows in sources:
                for lane in range(0, DSH, 128):
                    x = ref[rows, lane : lane + 128].astype(jnp.float32)
                    total += x
                    square += x * x
            mean = jnp.sum(total, axis=1, keepdims=True) / (HEAD_AXIS * DSH)
            var = jnp.sum(square, axis=1, keepdims=True) / (HEAD_AXIS * DSH) - mean * mean
            inv = lax.rsqrt(var + norm_eps)
            for s, (ref, rows) in enumerate(sources):
                shift, scale = mods[s]
                y = (ref[rows, :].astype(jnp.float32) - mean) * inv * scale + shift
                start = pl.multiple_of(place_ref[s] * DSH, DSH)
                mod_ref[here, pl.ds(start, DSH)] = y.astype(jnp.bfloat16)
            return carry

        lax.fori_loop(0, CUT // step, chunk, 0)

    def piece(part, p):
        b, hd = divmod(p, HEADS_HERE)
        lane = part * DSH + hd * HD
        return acc_ref[b * TOK : (b + 1) * TOK, lane : lane + HD]

    def turned(part, p):
        t = piece(part, p)
        t = t * lax.rsqrt(jnp.mean(t * t, axis=1, keepdims=True) + norm_eps)
        t = t * gain_ref[part : part + 1, :]
        even = lax.broadcasted_iota(jnp.int32, t.shape, 1) % 2 == 0
        other = jnp.where(even, pltpu.roll(t, HD - 1, 1), pltpu.roll(t, 1, 1))
        return (t * cos_ref[...] + other * sin_ref[...]).astype(jnp.bfloat16)

    for copy in copies:
        copy.wait()
    acc_ref[...] = jnp.dot(mod_ref[...], w_ref[...], preferred_element_type=jnp.float32)
    for part in range(3):
        for p in range(PAIRS):
            if part == 2:
                result = piece(part, p).astype(jnp.bfloat16)
            else:
                result = turned(part, p)
            if part == 0 and p == LAST:
                for n in range(RING):
                    out_ref[n, 3 * TOK : 4 * TOK, :] = result
            elif part == 0:
                out_ref[p, 2 * TOK : 3 * TOK, :] = result
            elif p == LAST:
                last_ref[(part - 1) * TOK : part * TOK, :] = result
            else:
                out_ref[p, (part - 1) * TOK : part * TOK, :] = result


def project(places, blocks, w, gains, cosine, sine):
    return pl.pallas_call(
        project_kernel,
        out_shape=(
            pltpu.VMEM((RING, 4 * TOK, HD), jnp.bfloat16),
            pltpu.VMEM((2 * TOK, HD), jnp.bfloat16),
        ),
        grid_spec=pltpu.PrefetchScalarGridSpec(
            num_scalar_prefetch=1,
            grid=(1,),
            in_specs=[IN_VMEM] * len(blocks)
            + [pl.BlockSpec(memory_space=pltpu.HBM), IN_VMEM, IN_VMEM, IN_VMEM],
            out_specs=(IN_VMEM, IN_VMEM),
            scratch_shapes=[
                pltpu.VMEM((ROWS, HEAD_AXIS * DSH), jnp.bfloat16),
                pltpu.VMEM((ROWS, WIDE), jnp.float32),
                pltpu.VMEM((HEAD_AXIS * DSH, WIDE), jnp.bfloat16),
                pltpu.SemaphoreType.DMA((3,)),
            ],
        ),
        compiler_params=pltpu.CompilerParams(vmem_limit_bytes=28 * MIB),
        cost_estimate=pl.CostEstimate(
            flops=2 * ROWS * HEAD_AXIS * DSH * 3 * DSH, bytes_accessed=12_000_000, transcendentals=0
        ),
        name="project",
    )(places, *map(in_vmem, blocks), w, *map(in_vmem, (gains, cosine, sine)))


QUAD = 4
TILE = QUAD * TOK
SET = RING * TOK
DIMS = (((1,), (1,)), ((), ()))


def score_keys(q, keys, score_ref, column, top):
    scores = lax.dot_general(q, keys, DIMS, preferred_element_type=jnp.float32)
    score_ref[:, column : column + scores.shape[1]] = scores
    for lane in range(0, scores.shape[1], 128):
        top = jnp.maximum(top, scores[:, lane : lane + 128])
    return top


def score_text(q, keys, valid, score_ref, column, top):
    scores = lax.dot_general(q, keys, DIMS, preferred_element_type=jnp.float32)
    index = lax.broadcasted_iota(jnp.int32, scores.shape, 1)
    scores = jnp.where(index < valid, scores, -jnp.inf)
    score_ref[:, column : column + scores.shape[1]] = scores
    for lane in range(0, scores.shape[1], 128):
        top = jnp.maximum(top, scores[:, lane : lane + 128])
    return top


def mix(score_ref, value_ref, top, count):
    mixed = jnp.zeros((TILE, 2 * HD), jnp.float32)
    for first in range(0, count, SET):
        stop = min(first + SET, count)
        weights = jnp.exp2(score_ref[:, first:stop] * EXP_SCALE - top).astype(jnp.bfloat16)
        mixed += jnp.dot(weights, value_ref[first:stop, :], preferred_element_type=jnp.float32)
    return mixed


def lay_values(value_ref, pieces):
    lane = lax.broadcasted_iota(jnp.int32, (value_ref.shape[0], HD), 1)
    value_ref[:, HD:] = jnp.where(lane == 0, 1.0, 0.0).astype(jnp.bfloat16)
    row = 0
    for piece in pieces:
        value_ref[row : row + piece.shape[0], :HD] = piece
        row += piece.shape[0]


def set_keys(ref):
    return ref[:, 0:TOK, :].reshape(SET, HD)


def set_values(ref):
    return ref[:, TOK : 2 * TOK, :].reshape(SET, HD)


def first_step():
    return pl.program_id(0) == 0


def tile_rows():
    return pl.ds(pl.multiple_of(pl.program_id(0) * TILE, TILE), TILE)


def gather_rows(flag_ref, q, pieces, before, score_ref, top_ref, total_ref, mixed_ref):
    def add_up(weights, values, total, mixed):
        for lane in range(0, weights.shape[1], 128):
            total += weights[:, lane : lane + 128]
        mixed += jnp.dot(weights.astype(jnp.bfloat16), values, preferred_element_type=jnp.float32)
        return total, mixed

    zeros = jnp.zeros((q.shape[0], 128), jnp.float32)

    @pl.when(flag_ref[0] == 1)
    def _():
        total, mixed = zeros, zeros
        for keys, values, valid in pieces:
            scores = lax.dot_general(q, keys, DIMS, preferred_element_type=jnp.float32)
            if valid is not None:
                index = lax.broadcasted_iota(jnp.int32, scores.shape, 1)
                scores = jnp.where(index < valid, scores, -jnp.inf)
            total, mixed = add_up(jnp.exp2(scores * EXP_SCALE), values, total, mixed)
        top_ref[...] = zeros
        total_ref[...] = total
        mixed_ref[...] = mixed

    @pl.when(flag_ref[0] != 1)
    def _():
        top = jnp.full((q.shape[0], 128), -jnp.inf, jnp.float32)
        column = 0
        for keys, _, valid in pieces:
            if valid is None:
                top = score_keys(q, keys, score_ref, column, top)
            else:
                top = score_text(q, keys, valid, score_ref, column, top)
            column += keys.shape[0]
        top = jnp.max(top, axis=1, keepdims=True) * EXP_SCALE
        if before is not None:
            top = jnp.maximum(top, before)
        total, mixed = zeros, zeros
        column = 0
        for _, values, _ in pieces:
            stop = column + values.shape[0]
            weights = jnp.exp2(score_ref[:, column:stop] * EXP_SCALE - top)
            total, mixed = add_up(weights, values, total, mixed)
            column = stop
        top_ref[...] = jnp.broadcast_to(top, (q.shape[0], 128))
        total_ref[...] = total
        mixed_ref[...] = mixed


def set_piece(ref):
    return set_keys(ref), set_values(ref), None


def attend_near_kernel(
    where_ref, flag_ref, q_ref, own_ref, core_ref, text_ref, w_hbm,
    mixed_ref, total_ref, top_ref, q_out_ref, w_ref, score_ref, sem,
):
    copy = pltpu.make_async_copy(w_hbm, w_ref, sem)

    @pl.when(first_step())
    def _():
        copy.start()

    q = q_ref[...].reshape(TILE, HD)
    text = (text_ref[0, 0], text_ref[1, 0], where_ref[2])
    here = tile_rows()
    gather_rows(
        flag_ref, q, [set_piece(own_ref), set_piece(core_ref), text], None, score_ref,
        top_ref.at[here], total_ref.at[here], mixed_ref.at[here],
    )
    q_out_ref[here, :] = q

    @pl.when(pl.program_id(0) == SET // TILE - 1)
    def _():
        copy.wait()


STATE = (pltpu.VMEM((SET, HD), jnp.float32),) * 3


def attend_near(where, flag, received, own, core, text_kv, w_out):
    return pl.pallas_call(
        attend_near_kernel,
        out_shape=STATE + (pltpu.VMEM((SET, HD), jnp.bfloat16), pltpu.VMEM(w_out.shape, w_out.dtype)),
        grid_spec=pltpu.PrefetchScalarGridSpec(
            num_scalar_prefetch=2,
            grid=(SET // TILE,),
            in_specs=[
                pl.BlockSpec((QUAD, TOK, HD), lambda i, w, f: (i, 2, 0)),
                whole((RING, 2 * TOK, HD)),
                whole((RING, 2 * TOK, HD)),
                pl.BlockSpec((2, 1, TXT, HD), lambda i, w, f: (0, w[0], 0, w[1])),
                pl.BlockSpec(memory_space=pltpu.HBM),
            ],
            out_specs=(IN_VMEM,) * 5,
            scratch_shapes=[
                pltpu.VMEM((TILE, 2 * SET + TXT), jnp.float32),
                pltpu.SemaphoreType.DMA(()),
            ],
        ),
        compiler_params=pltpu.CompilerParams(vmem_limit_bytes=18 * MIB),
        cost_estimate=pl.CostEstimate(
            flops=4 * SET * 2304 * HD, bytes_accessed=3_000_000, transcendentals=SET * 2304
        ),
        name="attend_near",
    )(where, flag, received, own, core, text_kv, w_out)


LAST_KEYS = QUAD * TOK + 128


def lay_last_kernel(where_ref, *refs):
    last_refs = refs[:QUAD]
    text_ref, own_text_ref, gain_ref, keys_ref, value_ref, flag_ref = refs[QUAD:]
    for n, ref in enumerate(last_refs):
        keys_ref[n * TOK : (n + 1) * TOK, :] = ref[0:TOK, :]
    keys_ref[QUAD * TOK :, :] = text_ref[0, 0]
    lay_values(value_ref, [ref[TOK : 2 * TOK, :] for ref in last_refs] + [text_ref[1, 0]])
    room = 1.03 * HD
    gains = gain_ref[...] * gain_ref[...]
    text = own_text_ref[0, 0].astype(jnp.float32)
    key_norm = jnp.maximum(
        room * jnp.max(gains[1:2]), jnp.max(jnp.sum(text * text, axis=1, keepdims=True))
    )
    bound = EXP_SCALE * EXP_SCALE * room * jnp.max(gains[0:1]) * key_norm
    flag_ref[0] = jnp.where(bound < MOST_LOG2 * MOST_LOG2, 1, 0)


MOST_LOG2 = 90.0


def lay_last(where, lasts, text_kv, gains):
    return pl.pallas_call(
        lay_last_kernel,
        out_shape=(
            jax.ShapeDtypeStruct((LAST_KEYS, HD), jnp.bfloat16),
            jax.ShapeDtypeStruct((LAST_KEYS, 2 * HD), jnp.bfloat16),
            jax.ShapeDtypeStruct((1,), jnp.int32),
        ),
        grid_spec=pltpu.PrefetchScalarGridSpec(
            num_scalar_prefetch=1,
            grid=(1,),
            in_specs=[whole((2 * TOK, HD)) for _ in lasts]
            + [
                pl.BlockSpec(
                    (2, 1, 128, HD), lambda i, w: (0, BRANCH - 1, w[4], HEADS_HERE - 1)
                ),
                pl.BlockSpec((1, 1, TXT, HD), lambda i, w: (0, w[0], 0, w[1])),
                whole((2, HD)),
            ],
            out_specs=(
                whole((LAST_KEYS, HD)),
                whole((LAST_KEYS, 2 * HD)),
                pl.BlockSpec(memory_space=pltpu.SMEM),
            ),
        ),
        compiler_params=pltpu.CompilerParams(vmem_limit_bytes=16 * MIB),
        cost_estimate=pl.CostEstimate(
            flops=10_000_000_000, bytes_accessed=10_000_000, transcendentals=0
        ),
        name="lay_last",
    )(where, *lasts, text_kv, text_kv, gains)


def attend_last_kernel(where_ref, q_ref, keys_ref, value_ref, out_ref, score_ref):
    video_keys = QUAD * TOK
    q = q_ref[...].reshape(TILE, HD)
    top = jnp.full((TILE, 128), -jnp.inf, jnp.float32)
    top = score_keys(q, keys_ref[0:video_keys, :], score_ref, 0, top)
    top = score_text(q, keys_ref[video_keys:, :], where_ref[3], score_ref, video_keys, top)
    top = jnp.max(top, axis=1, keepdims=True) * EXP_SCALE
    mixed = mix(score_ref, value_ref, top, LAST_KEYS)
    total = mixed[:, HD : HD + 1]
    result = mixed[:, :HD] / total
    first = pl.program_id(0) * QUAD
    out_ref[pl.ds(first, QUAD), 0:TOK, :] = result.astype(jnp.bfloat16).reshape(QUAD, TOK, HD)
    level = jnp.broadcast_to(top + jnp.log(total) * LOG2E, (TILE, HD))
    for f in range(QUAD):
        row = jnp.transpose(level[f * TOK : (f + 1) * TOK])[0:1]
        stats = limbs_of(row) + [jnp.zeros((STAT_ROWS - 3, HD), jnp.float32)]
        out_ref[first + f, TOK:LAST_ROWS, :] = jnp.concatenate(stats, axis=0).astype(jnp.bfloat16)


def attend_last(where, received, keys, values):
    return pl.pallas_call(
        attend_last_kernel,
        out_shape=pltpu.VMEM((RING, LAST_ROWS, HD), jnp.bfloat16),
        grid_spec=pltpu.PrefetchScalarGridSpec(
            num_scalar_prefetch=1,
            grid=(SET // TILE,),
            in_specs=[
                pl.BlockSpec((QUAD, TOK, HD), lambda i, w: (i, 3, 0)),
                whole((LAST_KEYS, HD)),
                whole((LAST_KEYS, 2 * HD)),
            ],
            out_specs=IN_VMEM,
            scratch_shapes=[pltpu.VMEM((TILE, LAST_KEYS), jnp.float32)],
        ),
        compiler_params=pltpu.CompilerParams(vmem_limit_bytes=16 * MIB),
        cost_estimate=pl.CostEstimate(
            flops=4 * SET * 640 * HD, bytes_accessed=1_000_000, transcendentals=SET * 640
        ),
        name="attend_last",
    )(where, received, keys, values)


def attend_far_kernel(finish, flag_ref, q_ref, set_ref, *refs):
    mixed_in, total_in, top_in, *refs = refs
    score_ref, top_ref, total_ref, mixed_ref = refs[-4:]
    here = slice(None)
    before = top_in[here, 0:1]
    gather_rows(
        flag_ref, q_ref[here, :], [set_piece(set_ref)], before, score_ref,
        top_ref, total_ref, mixed_ref,
    )
    decay = jnp.exp2(before - top_ref[:, 0:1])
    total = total_ref[...] + total_in[here, :] * decay
    mixed = mixed_ref[...] + mixed_in[here, :] * decay
    if finish:
        last_ref, out_ref = refs[:2]
        result = (mixed / jnp.sum(total, axis=1, keepdims=True)).astype(jnp.bfloat16)
        out_ref[:, 0:TOK, :] = result.reshape(RING, TOK, HD)
        out_ref[:, TOK:RETURN, :] = last_ref[...]
    else:
        mixed_out, total_out, top_out = refs[:3]
        mixed_out[here, :] = mixed
        total_out[here, :] = total
        top_out[here, :] = top_ref[...]


def attend_far(flag, queries, keys, state, last=None):
    finish = last is not None
    operands = [queries, keys, *state] + ([last] if finish else [])
    return pl.pallas_call(
        functools.partial(attend_far_kernel, finish),
        out_shape=pltpu.VMEM((RING, RETURN, HD), jnp.bfloat16) if finish else STATE,
        grid_spec=pltpu.PrefetchScalarGridSpec(
            num_scalar_prefetch=1,
            grid=(1,),
            in_specs=[IN_VMEM] * len(operands),
            out_specs=IN_VMEM if finish else (IN_VMEM,) * 3,
            scratch_shapes=[pltpu.VMEM((SET, SET), jnp.float32)]
            + [pltpu.VMEM((SET, 128), jnp.float32)] * 3,
        ),
        compiler_params=pltpu.CompilerParams(vmem_limit_bytes=16 * MIB),
        cost_estimate=pl.CostEstimate(
            flops=4 * SET * SET * HD, bytes_accessed=3_000_000, transcendentals=SET * SET
        ),
        name="attend_far",
    )(flag, *map(in_vmem, operands))


def output_kernel(place_ref, back_ref, w_ref, *refs):
    out_refs, attn_ref = refs[:-1], refs[-1]
    for p in range(RING):
        b, hd = divmod(p, HEADS_HERE)
        attn_ref[b * TOK : (b + 1) * TOK, hd * HD : (hd + 1) * HD] = back_ref[p, 0:TOK, :]
    levels = []
    for p in range(RING):
        stats = back_ref[p, 2 * TOK : RETURN, :].astype(jnp.float32)
        row = stats[0:1] + stats[1:2] + stats[2:3]
        levels.append(jnp.transpose(jnp.broadcast_to(row, (TOK, HD))))
    top = levels[0]
    for level in levels[1:]:
        top = jnp.maximum(top, level)
    total = jnp.zeros((TOK, HD), jnp.float32)
    mixed = jnp.zeros((TOK, HD), jnp.float32)
    for p, level in enumerate(levels):
        weight = jnp.exp2(level - top)
        total += weight
        mixed += weight * back_ref[p, TOK : 2 * TOK, :].astype(jnp.float32)
    attn_ref[(BRANCH - 1) * TOK :, (HEADS_HERE - 1) * HD :] = (mixed / total).astype(jnp.bfloat16)
    multiply(place_ref, EARLY, attn_ref, w_ref, out_refs)


EARLY = (4, 5, 7)
LATE = (2, 3, 0, 1, 6)


def multiply(place_ref, places, attn_ref, w_ref, out_refs):
    for s, out_ref in zip(places, out_refs):
        start = pl.multiple_of(place_ref[s] * DSH, DSH)
        out_ref[...] = jnp.dot(
            attn_ref[...], w_ref[:, pl.ds(start, DSH)], preferred_element_type=jnp.float32
        ).astype(jnp.bfloat16)


def late_kernel(place_ref, attn_ref, w_ref, *out_refs):
    multiply(place_ref, LATE, attn_ref, w_ref, out_refs)


def output(kernel, places, rows, w_out, count):
    return pl.pallas_call(
        kernel,
        out_shape=(pltpu.VMEM((ROWS, DSH), jnp.bfloat16),) * count,
        grid_spec=pltpu.PrefetchScalarGridSpec(
            num_scalar_prefetch=1,
            grid=(1,),
            in_specs=[IN_VMEM, IN_VMEM],
            out_specs=(IN_VMEM,) * count,
        ),
        compiler_params=pltpu.CompilerParams(vmem_limit_bytes=16 * MIB),
        cost_estimate=pl.CostEstimate(
            flops=2 * ROWS * DSH * DSH * count, bytes_accessed=3_000_000, transcendentals=0
        ),
        name="output",
    )(places, in_vmem(rows), in_vmem(w_out))


def head_move(x, step):
    return lax.ppermute(x, "head", [(i, (i + step) % HEAD_AXIS) for i in range(HEAD_AXIS)])


def head_partner(x):
    return lax.ppermute(x, "head", [(i, i ^ 1) for i in range(HEAD_AXIS)])


def frame_move(x, flip):
    return lax.ppermute(x, "frame", [(i, i ^ flip) for i in range(FRAMES)])


def gather_head(own):
    partner = head_partner(own)
    ahead = head_move(own, -2)
    behind = head_move(own, 2)
    opposite = [head_move(behind[:CUT], 2), head_move(ahead[CUT:], -2)]
    return [
        own,
        partner,
        ahead,
        behind,
        head_move(partner, -2),
        head_move(partner, 2),
        *opposite,
        *map(head_partner, opposite),
    ]


def add(*terms):
    total = terms[0].astype(jnp.float32)
    for term in terms[1:]:
        total += term.astype(jnp.float32)
    return total


def scatter_head(places, back, w_out):
    ahead, behind, over, attention = output(output_kernel, places, back, w_out, 4)
    for_partner = [head_move(ahead, 2), head_move(behind, -2)]
    for_opposite = head_partner(over)
    ahead, behind, own, partner, opposite = output(
        late_kernel, places, attention, w_out, len(LATE)
    )
    direct = [head_move(ahead, 2), head_move(behind, -2)]
    over_y = head_partner(add(partner, *for_partner).astype(jnp.bfloat16))
    across = head_move(add(opposite, for_opposite).astype(jnp.bfloat16), 4)
    return add(own, *direct, over_y, across)


def body(
    video, w_qkv, w_out, text_kv, text_lengths, norm_gains, mod_table, timestep_ids, queue_shift
):
    text_kv = in_hbm(text_kv)
    frame = lax.axis_index("frame").astype(jnp.int32)
    head = lax.axis_index("head").astype(jnp.int32)
    own, gate, gains, places, where = prep(
        frame.reshape(1),
        head.reshape(1),
        queue_shift,
        in_hbm(timestep_ids),
        in_hbm(text_lengths),
        in_hbm(video),
        in_hbm(mod_table.transpose(1, 0, 2)),
        in_hbm(norm_gains),
    )
    cosine, sine = rope_tables(frame)
    blocks = gather_head(own)
    weights = in_hbm(w_qkv.transpose(1, 0, 2))
    send, last = project(places, blocks, weights, gains, cosine, sine)
    rings = [[(y * RING + z) * 2 + core for z in range(RING)] for y in range(2) for core in range(2)]

    def over_rings(x):
        return lax.all_to_all(x, "frame", 0, 0, axis_index_groups=rings, tiled=True)

    received = over_rings(send)
    flips = (1, FRAMES // 2, FRAMES // 2 + 1)
    lasts = [last] + [frame_move(last, flip) for flip in flips]
    last_keys, last_values, flag = lay_last(where, lasts, text_kv, gains)
    near = received[:, : 2 * TOK]
    over_y = frame_move(near, FRAMES // 2)
    near_later, last_keys = lax.optimization_barrier((near, last_keys))
    over_core = frame_move(near_later, 1)
    ninth = attend_last(where, received, last_keys, last_values)
    *state, queries, w_held = attend_near(
        where, flag, received, near, over_core, text_kv, in_hbm(w_out)
    )
    over_y, _, _ = lax.optimization_barrier((over_y, state[0], ninth))
    diagonal = frame_move(over_y, 1)
    state = attend_far(flag, queries, over_y, state)
    returned = attend_far(flag, queries, diagonal, state, ninth)
    back = over_rings(returned)
    proj = scatter_head(places, back, w_held).reshape(video.shape)
    return (video.astype(jnp.float32) + gate * proj).astype(jnp.bfloat16)


def solution(mesh):
    in_specs = (
        P(None, "frame", "head"),
        P(None, None, "head"),
        P("head", None),
        P(None, None, None, "head"),
        P(),
        P(),
        P(None, None, "head"),
        P(),
        P(),
    )
    out_specs = P(None, "frame", "head")
    return jax.shard_map(body, mesh=mesh, in_specs=in_specs, out_specs=out_specs, check_vma=False)
```
